128 devices in a mesh: gx: 16 (over z_lo, x, core), gy: 8 (over z_hi, y).
Axes of the slice: x: 4, y: 4, z: 4 (z_hi: 2, z_lo: 2; z = z_hi * 2 + z_lo), core: 2. Of those that a mesh axis runs over, the one named last changes fastest.
Arguments:
- u_now: float32 [3, 12, 128, 1024], P(None, None, 'gx', 'gy'), may hold values from -6 to 6
- u_prev: float32 [3, 12, 128, 1024], P(None, None, 'gx', 'gy'), may hold values from -6 to 6
- adjoint_next: float32 [3, 12, 128, 1024], P(None, None, 'gx', 'gy'), may hold values from -6 to 6
- adjoint_later: float32 [3, 12, 128, 1024], P(None, None, 'gx', 'gy'), may hold values from -6 to 6
- density: float32 [11, 128, 1024], P(None, 'gx', 'gy'), may hold values from 0.05 to 1
- step_factor: float32 [12, 128, 1024], P(None, 'gx', 'gy'), may hold values from 0.003 to 0.01
- fixed_nodes: int32 [12, 128, 1024], P(None, 'gx', 'gy'), may hold values 0 or 1
- load_top: float32 [128, 1024], P('gx', 'gy'), may hold values from -6 to 6
- load_depth: int32 [128, 1024], P('gx', 'gy'), may hold values from 0 to 11
- brick_stiffness: float32 [24, 24], replicated, as said below
Outputs:
- adjoint_first: float32 [3, 12, 128, 1024], P(None, None, 'gx', 'gy')
- adjoint_second: float32 [3, 12, 128, 1024], P(None, None, 'gx', 'gy')
- sensitivity: float32 [11, 128, 1024], P(None, 'gx', 'gy')
The draws below stay inside these ranges and needn't reach their ends.
Inputs may be any that keep to these rules, and one draw needn't show every extreme that they name: `fixed_nodes`: 1 marks a fixed node. `load_depth`: a node layer index. brick_stiffness is symmetric.
All inputs are finite; a program needn't handle non-finite values. No bound on the sum of `fixed_nodes` on one device may be relied on, other than what follows from the above.
Results may differ from the reference program's by a relative error of at most 0.00015.
Values sent between devices are 32-bit elements; how exact they have to be, the bound alone decides.
A program may use at most 64 MiB of HBM per device.

```python
import math
import jax
import jax.numpy as jnp
from jax import lax

NZ = 12
NX = 128
NY = 1024


def draw_brick_stiffness(key, part):
    key = jax.random.fold_in(key, 7)
    raw = 0.2 * jax.random.normal(key, (24, 24), jnp.float32)
    symmetric = 0.5 * (raw + raw.T)
    return symmetric + 6.0 * jnp.eye(24, dtype=jnp.float32)


def touch_ends(values, stream_key, smallest, high):
    longest = values.shape.index(max(values.shape))
    spots = []
    for shift in (0, 1):
        where = [jax.random.randint(jax.random.fold_in(stream_key, axis), (), 0, length) for axis, length in enumerate(values.shape)]
        where[longest] = (where[longest] + shift) % values.shape[longest]
        spots.append(tuple(where))
    return values.at[spots[0]].set(smallest).at[spots[1]].set(high)


def level_of(stream_key, shape, cuts, low, high):
    def one(position, blocks):
        steps = jax.random.uniform(jax.random.fold_in(jax.random.fold_in(stream_key, 6), position), (blocks,), jnp.float32, low / len(cuts), high / len(cuts))
        return jnp.repeat(jnp.exp(steps), shape[position] // blocks).reshape((-1,) + (1,) * (len(shape) - position - 1))

    loudness = one(*cuts[0])
    for cut in cuts[1:]:
        loudness = loudness * one(*cut)
    return loudness


def centred(key, extent, width, bound, cuts=(), kind=jnp.bfloat16):
    gain = level_of(key, extent, cuts, -0.22, 0.18) if cuts else 1.0
    array = jax.random.normal(key, extent, jnp.float32) * width * gain
    return jnp.minimum(jnp.maximum(array, -bound), bound).astype(kind)


def setup_inputs(seed: int = 0) -> dict:
    key_list = jax.random.split(jax.random.key(seed), 11)
    u_now = centred(key_list[0], (3, NZ, NX, NY), 1.0, 6.0, ((2, 16), (3, 8)), jnp.float32)
    u_prev = centred(key_list[1], (3, NZ, NX, NY), 1.0, 6.0, ((2, 16), (3, 8)), jnp.float32)
    adjoint_next = centred(key_list[2], (3, NZ, NX, NY), 1.0, 6.0, ((2, 16), (3, 8)), jnp.float32)
    adjoint_later = centred(key_list[3], (3, NZ, NX, NY), 1.0, 6.0, ((2, 16), (3, 8)), jnp.float32)
    density = jnp.clip(0.05 + 0.95 * jax.random.uniform(key_list[4], (NZ - 1, NX, NY), jnp.float32) ** level_of(key_list[4], (NZ - 1, NX, NY), ((1, 16), (2, 8)), -0.2, 0.2), 0.05, 1.0)
    step_factor = jnp.clip(jnp.exp(math.log(0.01) - 1.2039728 * jax.random.uniform(key_list[5], (NZ, NX, NY), jnp.float32) ** level_of(key_list[5], (NZ, NX, NY), ((1, 16), (2, 8)), -0.2, 0.2)), 0.003, 0.01)
    fixed_nodes = touch_ends((jax.random.randint(key_list[6], (NZ, NX, NY), 0, 16) < 1).astype(jnp.int32), jax.random.fold_in(key_list[6], 1), 0, 1)
    load_top = centred(key_list[7], (NX, NY), 1.0, 6.0, ((0, 16), (1, 8)), jnp.float32)
    load_depth = touch_ends(jax.random.randint(key_list[8], (NX, NY), 0, NZ), jax.random.fold_in(key_list[8], 1), 0, NZ - 1).astype(jnp.int32)
    brick_stiffness = draw_brick_stiffness(jax.random.fold_in(key_list[10], 71), 0)
    return {"u_now": u_now, "u_prev": u_prev, "adjoint_next": adjoint_next, "adjoint_later": adjoint_later, "density": density, "step_factor": step_factor, "fixed_nodes": fixed_nodes, "load_top": load_top, "load_depth": load_depth, "brick_stiffness": brick_stiffness}


EMIN = 1e-3
precise = lax.Precision.HIGHEST
OFFSETS = tuple((lift_z, lift_x, lift_y) for lift_z in (0, 1) for lift_x in (0, 1) for lift_y in (0, 1))


def nodal_load(load_top, load_depth, layer_count):
    layers = lax.broadcasted_iota(jnp.int32, (layer_count,) + load_top.shape, 0)
    vertical = jnp.where(layers == load_depth[None], load_top[None], jnp.zeros_like(load_top)[None])
    zeros = jnp.zeros_like(vertical)
    return jnp.stack([zeros, zeros, vertical])


def layer_corners(extended, layer):
    slab = lax.dynamic_slice_in_dim(extended, layer, 2, 1)
    rows = extended.shape[2] - 1
    cols = extended.shape[3] - 1
    parts = [slab[:, offset[0], offset[1]:offset[1] + rows, offset[2]:offset[2] + cols] for offset in OFFSETS]
    return jnp.stack(parts, axis=1).reshape(24, rows * cols)


def widen(field):
    return jnp.pad(field, ((0, 0), (0, 0), (0, 1), (0, 1)))


def stiffness_apply(stiffness, factor, field):
    extended = widen(field)
    rows = field.shape[2]
    cols = field.shape[3]

    def one_layer(layer):
        corners = layer_corners(extended, layer)
        forces = jnp.dot(stiffness, corners, precision=precise).reshape(3, 8, rows, cols)
        forces = forces * factor[layer][None, None]
        lower = jnp.zeros((3, rows + 1, cols + 1), jnp.float32)
        upper = jnp.zeros((3, rows + 1, cols + 1), jnp.float32)
        for place, offset in enumerate(OFFSETS):
            padded = jnp.pad(forces[:, place], ((0, 0), (offset[1], 1 - offset[1]), (offset[2], 1 - offset[2])))
            if offset[0] == 0:
                lower = lower + padded
            else:
                upper = upper + padded
        return lower, upper

    lowers, uppers = lax.map(one_layer, jnp.arange(field.shape[1] - 1, dtype=jnp.int32))
    zero_layer = jnp.zeros_like(lowers[:1])
    total = jnp.concatenate([lowers, zero_layer], 0) + jnp.concatenate([zero_layer, uppers], 0)
    return jnp.transpose(total, (1, 0, 2, 3))[:, :, :rows, :cols]


def sensitivity_term(stiffness, weighted, state):
    wide_weighted = widen(weighted)
    wide_state = widen(state)
    rows = state.shape[2]
    cols = state.shape[3]

    def one_layer(layer):
        pushed = jnp.dot(stiffness, layer_corners(wide_weighted, layer), precision=precise)
        return jnp.sum((pushed * layer_corners(wide_state, layer)).reshape(24, rows, cols), axis=0)

    return lax.map(one_layer, jnp.arange(state.shape[1] - 1, dtype=jnp.int32))


def reference(u_now, u_prev, adjoint_next, adjoint_later, density, step_factor, fixed_nodes, load_top, load_depth, brick_stiffness):
    free = 1.0 - fixed_nodes.astype(jnp.float32)
    load = nodal_load(load_top, load_depth, u_now.shape[1])
    factor = EMIN + (1.0 - EMIN) * density ** 3
    fields = [u_prev, u_now]
    for step in range(2):
        pushed = stiffness_apply(brick_stiffness, factor, fields[-1])
        fields.append(free * (2.0 * fields[-1] - fields[-2] + step_factor * (load - pushed)))
    later = adjoint_later
    current = adjoint_next
    total = jnp.zeros(density.shape, jnp.float32)
    results = []
    for level in (2, 1, 0):
        weighted = free * step_factor * current
        total = total + sensitivity_term(brick_stiffness, weighted, fields[level + 1])
        newest = 2.0 * current - later + load - stiffness_apply(brick_stiffness, factor, weighted)
        later = current
        current = newest
        results.append(newest)
    sensitivity = -3.0 * (1.0 - EMIN) * density ** 2 * total
    return results[2], results[1], sensitivity
```

```python
import jax
import jax.numpy as jnp
import numpy as np
from jax import lax
from jax.experimental import pallas as pl
from jax.experimental.pallas import tpu as pltpu
from jax.sharding import PartitionSpec as P

EMIN = 0.001
MESH = pl.DeviceIdType.MESH
F32 = jnp.float32
BF16 = jnp.bfloat16

ROWS = 8
TILES = 16
LEFT, RIGHT = 14, 15
U, S, A, D, B, LOAD, Q, PLANES = 0, 36, 48, 84, 96, 132, 136, 176
DEEP = 96
GROUP = 40
SLOT = 48
OUT = 8 * GROUP
DEPTH = 4 * SLOT


def band_tables():
    m = np.arange(OUT)
    group, r = m // GROUP, m % GROUP
    place, dz = group // 2, group % 2
    comp, layer = r // 12, r % 12
    element = layer - dz
    real = (r < 36) & (element >= 0) & (element <= 10)
    pick = np.zeros((OUT, 24), np.float32)
    pick[m[real], (comp * 8 + 4 * dz + place)[real]] = 1
    q = np.arange(DEPTH)
    place_in, s = q // SLOT, q % SLOT
    comp_in, layer_in = s // 12, s % 12
    spread = np.zeros((2, 24, DEPTH), np.float32)
    band = np.zeros((2, OUT, DEPTH), np.float32)
    for up in (0, 1):
        ok = s < 36
        spread[up, (comp_in * 8 + 4 * up + place_in)[ok], q[ok]] = 1
        band[up] = layer_in[None, :] == (element + up)[:, None]
    return pick, spread, band


def exchange_kernel(u, b, a, q, den, step, fix, top, depth, stiff, pick, spread, band, e, w, packed, from_left, from_right, send_sem, recv_sem):
    gx, gy = lax.axis_index("gx"), lax.axis_index("gy")
    nx, ny = lax.axis_size("gx"), lax.axis_size("gy")
    has = {"down": gx > 0, "up": gx < nx - 1, "left": gy > 0, "right": gy < ny - 1}
    where = {"down": (gx - 1, gy), "up": (gx + 1, gy), "left": (gx, gy - 1), "right": (gx, gy + 1)}
    barrier = pltpu.get_barrier_semaphore()
    for side in where:
        @pl.when(has[side])
        def _(side=side):
            pl.semaphore_signal(barrier, inc=1, device_id=where[side], device_id_type=MESH)

    e[LEFT] = jnp.zeros((PLANES, 128), F32)
    e[RIGHT] = jnp.zeros((PLANES, 128), F32)
    for r in range(ROWS):
        t = r + 3
        free = 1.0 - fix[pl.ds(r, 12, stride=8), :].astype(F32)
        e[t, U:U + 36] = u[pl.ds(r, 36, stride=8), :]
        e[t, S:S + 12] = free * step[pl.ds(r, 12, stride=8), :]
        e[t, A:A + 36] = a[pl.ds(r, 36, stride=8), :]
        e[t, D:D + 11] = den[pl.ds(r, 11, stride=8), :]
        e[t, D + 11:D + 12] = jnp.zeros((1, 128), F32)
        e[t, B:B + 36] = b[pl.ds(r, 36, stride=8), :]
        e[t, LOAD:LOAD + 1] = top[r:r + 1, :]
        e[t, LOAD + 1:LOAD + 2] = depth[r:r + 1, :].astype(F32)
        e[t, LOAD + 2:LOAD + 4] = jnp.zeros((2, 128), F32)
        e[t, Q:Q + 36] = q[pl.ds(r, 36, stride=8), :]
        e[t, Q + 36:Q + 40] = jnp.zeros((4, 128), F32)
    for t in (0, 13):
        e[t, DEEP:PLANES] = jnp.zeros((PLANES - DEEP, 128), F32)

    @pl.when(gx == 0)
    def _():
        for t in (0, 1, 2):
            e[t] = jnp.zeros((PLANES, 128), F32)

    @pl.when(gx == nx - 1)
    def _():
        for t in (11, 12, 13):
            e[t] = jnp.zeros((PLANES, 128), F32)

    count = sum(has[side].astype(jnp.int32) for side in where)
    pl.semaphore_wait(barrier, count)

    def remote(src, dst, k, side):
        return pltpu.make_async_remote_copy(
            src_ref=src, dst_ref=dst, send_sem=send_sem.at[k], recv_sem=recv_sem.at[k],
            device_id=where[side], device_id_type=MESH,
        )

    down = [
        remote(e.at[3:6, 0:DEEP], e.at[11:14, 0:DEEP], 0, "down"),
        remote(e.at[3:5, DEEP:PLANES], e.at[11:13, DEEP:PLANES], 1, "down"),
    ]
    up = [
        remote(e.at[8:11, 0:DEEP], e.at[0:3, 0:DEEP], 2, "up"),
        remote(e.at[9:11, DEEP:PLANES], e.at[1:3, DEEP:PLANES], 3, "up"),
    ]

    @pl.when(has["down"])
    def _():
        for c in down:
            c.start()

    @pl.when(has["up"])
    def _():
        for c in up:
            c.start()

    lane = lax.broadcasted_iota(jnp.int32, (PLANES, 128), 1)
    row_of = ((lane + 1) & 127) >> 3
    column = ((lane + 1) & 7) - 1

    def pack(tiles):
        total = packed[...]
        for t in tiles:
            total = jnp.where(row_of == t, pltpu.roll(e[t], 8 * t + 3, 1), total)
        packed[...] = total

    packed[...] = jnp.zeros((PLANES, 128), F32)
    pack(range(3, 11))

    low = stiff[...] - stiff[...].astype(BF16).astype(F32)
    for part, value in enumerate((stiff[...].astype(BF16), low.astype(BF16))):
        rows = jnp.dot(pick[...], value, preferred_element_type=F32).astype(BF16)
        full = jnp.zeros((OUT, DEPTH), F32)
        for dz in (0, 1):
            full = full + band[dz].astype(F32) * jnp.dot(rows, spread[dz], preferred_element_type=F32)
        w[part] = full.astype(BF16)

    @pl.when(has["down"])
    def _():
        for c in up:
            c.wait_recv()

    @pl.when(has["up"])
    def _():
        for c in down:
            c.wait_recv()

    pack((0, 1, 2, 11, 12, 13))
    to_left = remote(packed, from_right, 4, "left")
    to_right = remote(packed, from_left, 5, "right")

    @pl.when(has["left"])
    def _():
        to_left.start()

    @pl.when(has["right"])
    def _():
        to_right.start()

    e[LEFT] = jnp.where(column >= 3, packed[...], 0.0)
    e[RIGHT] = jnp.where(column <= 2, packed[...], 0.0)

    @pl.when(has["left"])
    def _():
        to_right.wait_recv()
        e[LEFT] = jnp.where(column <= 2, from_left[...], e[LEFT])

    @pl.when(has["right"])
    def _():
        to_left.wait_recv()
        e[RIGHT] = jnp.where(column >= 3, from_right[...], e[RIGHT])

    @pl.when(has["down"])
    def _():
        for c in down:
            c.wait_send()

    @pl.when(has["up"])
    def _():
        for c in up:
            c.wait_send()

    @pl.when(has["left"])
    def _():
        to_left.wait_send()

    @pl.when(has["right"])
    def _():
        to_right.wait_send()


def plate_kernel(e, w, first, second, sens, fac, fup, srep, load, u1, u2, a2, a1, z, xh, xl, xsh, xsl, acc0, acc1):
    lane = lax.broadcasted_iota(jnp.int32, (GROUP, 128), 1)
    layer = lax.broadcasted_iota(jnp.int32, (12, 128), 0).astype(F32)
    edge = (lane == 0) | (lane == 127)
    from_left = ((lane + 1) & 7) >= 4
    wl = jnp.zeros((8, 128), F32)

    def halves(v):
        v = jnp.concatenate([v, wl], 0)
        high = v.astype(BF16)
        return high, (v - high.astype(F32)).astype(BF16)

    def put(t, v):
        high, low = halves(v)
        xh[t, 0:SLOT] = high
        xl[t, 0:SLOT] = low
        high, low = halves(pltpu.roll(v, 127, 1))
        xh[t, SLOT:2 * SLOT] = high
        xl[t, SLOT:2 * SLOT] = low

    def put_seam(side, v):
        cols = slice(128 * side, 128 * side + 128)
        for k, by in enumerate((0, 127, 120, 119)):
            high, low = halves(pltpu.roll(v, by, 1) if by else v)
            xsh[SLOT * k:SLOT * (k + 1), cols] = high
            xsl[SLOT * k:SLOT * (k + 1), cols] = low

    def field(t, at):
        rows = lax.broadcasted_iota(jnp.int32, (GROUP, 128), 0)
        return jnp.where(rows < 36, e[t, at:at + GROUP], 0.0)

    zeros = jnp.zeros((GROUP, 128), F32)

    def prepare(t, _):
        d = e[t, D:D + 12]
        f = jnp.where(d > 0.0, EMIN + (1.0 - EMIN) * (d * d * d), 0.0)
        s = e[t, S:S + 12]
        fac[t] = zeros
        fup[t] = zeros
        srep[t] = zeros
        load[t] = zeros
        for c in (0, 12, 24):
            fac[t, c:c + 12] = f
            fup[t, c + 1:c + 12] = f[0:11]
            srep[t, c:c + 12] = s
        load[t, 24:36] = jnp.where(e[t, LOAD + 1:LOAD + 2] == layer, e[t, LOAD:LOAD + 1], 0.0)
        acc0[t] = zeros
        acc1[t] = zeros
        put(t, field(t, U))
        return 0

    lax.fori_loop(0, TILES, prepare, 0)
    for side in (0, 1):
        put_seam(side, field(LEFT + side, U))

    def forces(high, low):
        return (
            jnp.dot(w[0], high, preferred_element_type=F32)
            + jnp.dot(w[1], high, preferred_element_type=F32)
            + jnp.dot(w[0], low, preferred_element_type=F32)
        )

    def weigh(t, f):
        return [
            fac[t] * f[(2 * k) * GROUP:(2 * k + 1) * GROUP] + fup[t] * f[(2 * k + 1) * GROUP:(2 * k + 2) * GROUP]
            for k in range(4)
        ]

    def collect(t, f, corners):
        for dz, acc in ((0, acc0), (1, acc1)):
            total = acc[t]
            for k in range(4):
                total = total + f[(2 * k + dz) * GROUP:(2 * k + dz + 1) * GROUP] * corners[k]
            acc[t] = total

    def stiffness_map(start, pairs, finish, seam_finish, state=None):
        f = forces(xsh[...], xsl[...])
        seams = []
        for side in (0, 1):
            t = LEFT + side
            part = f[:, 128 * side:128 * side + 128]
            if state is not None and side == 1:
                v = state(t)
                collect(t, part, [pltpu.roll(v, by, 1) if by else v for by in (0, 127, 120, 119)])
            g = weigh(t, part)
            seams.append(g[0] + pltpu.roll(g[1], 1, 1) + pltpu.roll(g[2], 8, 1) + pltpu.roll(g[3], 9, 1))
        both = jnp.where(from_left, seams[0], seams[1])

        def step(i, carry):
            t0 = start + 2 * i
            tiles = [xh[t0 + k] for k in range(3)]
            lows = [xl[t0 + k] for k in range(3)]
            high = jnp.concatenate([jnp.concatenate(tiles[0:2], 0), jnp.concatenate(tiles[1:3], 0)], 1)
            low = jnp.concatenate([jnp.concatenate(lows[0:2], 0), jnp.concatenate(lows[1:3], 0)], 1)
            f = forces(high, low)
            if state is not None:
                @pl.when((t0 >= 2) & (t0 <= 10))
                def _():
                    for k in (0, 1):
                        here, there = state(t0 + k), state(t0 + k + 1)
                        collect(t0 + k, f[:, 128 * k:128 * k + 128], [here, pltpu.roll(here, 127, 1), there, pltpu.roll(there, 127, 1)])
            below, below_rolled = carry
            for k in (0, 1):
                t = t0 + k
                g = weigh(t, f[:, 128 * k:128 * k + 128])
                out = g[0] + below + pltpu.roll(g[1] + below_rolled, 1, 1)
                out = jnp.where(edge, pltpu.roll(both, 125 - 8 * t, 1), out)
                finish(t, out)
                below, below_rolled = g[2], g[3]
            return below, below_rolled

        lax.fori_loop(0, pairs, step, (zeros, zeros))
        for side in (0, 1):
            seam_finish(side, seams[side])

    def displacement(now, before, target, follow):
        def value(t, out):
            s = srep[t]
            return jnp.where(s > 0.0, 2.0 * now(t) - before(t) + s * (load[t] - out), 0.0)

        def finish(t, out):
            v = value(t, out)
            target[t] = v
            if follow:
                put(t, v)

        def seam_finish(side, out):
            v = value(LEFT + side, out)
            target[LEFT + side] = v
            if follow:
                put_seam(side, v)

        return finish, seam_finish

    def adjoint(now, before, target, result):
        def value(t, out):
            return 2.0 * now(t) - before(t) + load[t] - out

        def finish(t, out):
            v = value(t, out)
            if target is not None:
                target[t] = v
                put(t, srep[t] * v)
            if result is not None:
                @pl.when((t >= 3) & (t <= 10))
                def _():
                    result[pl.ds(t - 3, 36, stride=8), :] = v[0:36]

        def seam_finish(side, out):
            if target is not None:
                v = value(LEFT + side, out)
                target[LEFT + side] = v
                put_seam(side, srep[LEFT + side] * v)

        return finish, seam_finish

    u_now = lambda t: field(t, U)
    u_before = lambda t: field(t, B)
    adj_next = lambda t: field(t, A)
    adj_later = lambda t: field(t, Q)
    of = lambda ref: (lambda t: ref[t])

    stiffness_map(1, 6, *displacement(u_now, u_before, u1, True))
    stiffness_map(2, 5, *displacement(of(u1), u_now, u2, False))

    def weighted(t, _):
        put(t, srep[t] * adj_next(t))
        return 0

    lax.fori_loop(0, TILES, weighted, 0)
    for side in (0, 1):
        put_seam(side, srep[LEFT + side] * adj_next(LEFT + side))

    stiffness_map(0, 7, *adjoint(adj_next, adj_later, a2, None), of(u2))
    stiffness_map(1, 6, *adjoint(of(a2), adj_next, a1, second), of(u1))
    stiffness_map(2, 5, *adjoint(of(a1), of(a2), None, first), u_now)

    def total(t):
        p, r = acc0[t], acc1[t]
        return p[0:11] + p[12:23] + p[24:35] + r[1:12] + r[13:24] + r[25:36]

    seam = total(RIGHT)
    last = lax.broadcasted_iota(jnp.int32, (11, 128), 1) == 127
    for r in range(ROWS):
        t = r + 3
        d = e[t, D:D + 11]
        both = jnp.where(last, pltpu.roll(seam, 125 - 8 * t, 1), total(t))
        sens[pl.ds(r, 11, stride=8), :] = (-3.0 * (1.0 - EMIN)) * (d * d) * both


def local(u_now, u_prev, adjoint_next, adjoint_later, density, step_factor, fixed_nodes, load_top, load_depth, brick_stiffness):
    pick, spread, band = (jnp.asarray(x, BF16) for x in band_tables())
    vmem = pl.BlockSpec(memory_space=pltpu.VMEM)
    flat = lambda x: x.reshape(-1, 128)
    e, w = pl.pallas_call(
        exchange_kernel,
        out_shape=(
            jax.ShapeDtypeStruct((TILES, PLANES, 128), F32),
            jax.ShapeDtypeStruct((2, OUT, DEPTH), BF16),
        ),
        in_specs=[vmem] * 13,
        out_specs=(vmem, vmem),
        scratch_shapes=[
            pltpu.VMEM((PLANES, 128), F32),
            pltpu.VMEM((PLANES, 128), F32),
            pltpu.VMEM((PLANES, 128), F32),
            pltpu.SemaphoreType.DMA((6,)),
            pltpu.SemaphoreType.DMA((6,)),
        ],
        compiler_params=pltpu.CompilerParams(collective_id=0, has_side_effects=True, vmem_limit_bytes=24 * 2**20),
        name="exchange",
    )(
        flat(u_now), flat(u_prev), flat(adjoint_next), flat(adjoint_later), flat(density), flat(step_factor),
        flat(fixed_nodes), load_top, load_depth, brick_stiffness, pick, spread, band,
    )
    tile = pltpu.VMEM((TILES, GROUP, 128), F32)
    first, second, sens = pl.pallas_call(
        plate_kernel,
        out_shape=(
            jax.ShapeDtypeStruct((36 * ROWS, 128), F32),
            jax.ShapeDtypeStruct((36 * ROWS, 128), F32),
            jax.ShapeDtypeStruct((11 * ROWS, 128), F32),
        ),
        in_specs=[vmem] * 2,
        out_specs=(vmem,) * 3,
        scratch_shapes=[tile] * 9 + [
            pltpu.VMEM((TILES, 2 * SLOT, 128), BF16),
            pltpu.VMEM((TILES, 2 * SLOT, 128), BF16),
            pltpu.VMEM((DEPTH, 256), BF16),
            pltpu.VMEM((DEPTH, 256), BF16),
            tile, tile,
        ],
        compiler_params=pltpu.CompilerParams(vmem_limit_bytes=40 * 2**20),
        name="plate",
    )(e, w)
    return (
        first.reshape(u_now.shape),
        second.reshape(u_now.shape),
        sens.reshape(density.shape),
    )


def solution(mesh):
    in_specs = (
        P(None, None, "gx", "gy"),
        P(None, None, "gx", "gy"),
        P(None, None, "gx", "gy"),
        P(None, None, "gx", "gy"),
        P(None, "gx", "gy"),
        P(None, "gx", "gy"),
        P(None, "gx", "gy"),
        P("gx", "gy"),
        P("gx", "gy"),
        P(),
    )
    out_specs = (P(None, None, "gx", "gy"), P(None, None, "gx", "gy"), P(None, "gx", "gy"))
    return jax.shard_map(local, mesh=mesh, in_specs=in_specs, out_specs=out_specs, check_vma=False)
```

```python
import jax
import jax.numpy as jnp
from jax import lax
from jax.experimental import pallas as pl
from jax.experimental.pallas import tpu as pltpu
from jax.sharding import PartitionSpec as P

EMIN = 0.001
MESH = pl.DeviceIdType.MESH
F32 = jnp.float32
BF16 = jnp.bfloat16

ROWS = 8
TILES = 16
LEFT, RIGHT = 14, 15
U, S, A, D, B, LOAD, Q, PLANES = 0, 36, 48, 84, 96, 132, 136, 176
DEEP = 96
GROUP = 40
SLOT = 48
OUT = 8 * GROUP
DEPTH = 4 * SLOT


def banded_weights(stiff, w):
    def split(place):
        comp = (place >= 12).astype(jnp.int32) + (place >= 24).astype(jnp.int32)
        return comp, place - 12 * comp

    iota = lambda shape, d: lax.broadcasted_iota(jnp.int32, shape, d)
    group, r = iota((8, GROUP, 24), 0), iota((8, GROUP, 24), 1)
    dz = group & 1
    comp, layer = split(r)
    element = layer - dz
    real = (r < 36) & (element >= 0) & (element <= 10)
    pick = jnp.where(real & (iota((8, GROUP, 24), 2) == comp * 8 + 4 * dz + (group >> 1)), 1.0, 0.0)
    pick = pick.reshape(OUT, 24).astype(BF16)

    def columns(shape):
        q = iota(shape, len(shape) - 1)
        place = sum((q >= SLOT * k).astype(jnp.int32) for k in (1, 2, 3))
        s = q - SLOT * place
        return (place, s) + split(s)

    place, s, comp, _ = columns((24, DEPTH))
    spread = [
        jnp.where((s < 36) & (iota((24, DEPTH), 0) == comp * 8 + 4 * up + place), 1.0, 0.0).astype(BF16)
        for up in (0, 1)
    ]
    group, r = iota((8, GROUP, DEPTH), 0), iota((8, GROUP, DEPTH), 1)
    offset = columns((8, GROUP, DEPTH))[3] - split(r)[1] + (group & 1)
    offset = offset.reshape(OUT, DEPTH)
    low = stiff - stiff.astype(BF16).astype(F32)
    for part, value in enumerate((stiff.astype(BF16), low.astype(BF16))):
        rows = jnp.dot(pick, value, preferred_element_type=F32).astype(BF16)
        full = jnp.zeros((OUT, DEPTH), F32)
        for up in (0, 1):
            full = jnp.where(offset == up, jnp.dot(rows, spread[up], preferred_element_type=F32), full)
        w[part] = full.astype(BF16)


def exchange_kernel(*refs):
    sources, (e, w), held, rest = refs[:10], refs[10:12], refs[12:22], refs[22:]
    u, b, a, q, den, step, fix, top, depth, stiff = held
    packed, from_left, from_right, load_sem, send_sem, recv_sem = rest
    gx, gy = lax.axis_index("gx"), lax.axis_index("gy")
    nx, ny = lax.axis_size("gx"), lax.axis_size("gy")
    has = {"down": gx > 0, "up": gx < nx - 1, "left": gy > 0, "right": gy < ny - 1}
    where = {"down": (gx - 1, gy), "up": (gx + 1, gy), "left": (gx, gy - 1), "right": (gx, gy + 1)}
    barrier = pltpu.get_barrier_semaphore()
    for side in where:
        @pl.when(has[side])
        def _(side=side):
            pl.semaphore_signal(barrier, inc=1, device_id=where[side], device_id_type=MESH)

    loads = [pltpu.make_async_copy(src, dst, load_sem.at[k]) for k, (src, dst) in enumerate(zip(sources, held))]
    for c in loads:
        c.start()
    for c in loads:
        c.wait()
    for r in range(ROWS):
        t = r + 3
        free = 1.0 - fix[pl.ds(r, 12, stride=8), :].astype(F32)
        e[t, U:U + 36] = u[pl.ds(r, 36, stride=8), :]
        e[t, S:S + 12] = free * step[pl.ds(r, 12, stride=8), :]
        e[t, A:A + 36] = a[pl.ds(r, 36, stride=8), :]
        e[t, D:D + 11] = den[pl.ds(r, 11, stride=8), :]
        e[t, D + 11:D + 12] = jnp.zeros((1, 128), F32)
        e[t, B:B + 36] = b[pl.ds(r, 36, stride=8), :]
        e[t, LOAD:LOAD + 1] = top[r:r + 1, :]
        e[t, LOAD + 1:LOAD + 2] = depth[r:r + 1, :].astype(F32)
        e[t, LOAD + 2:LOAD + 4] = jnp.zeros((2, 128), F32)
        e[t, Q:Q + 36] = q[pl.ds(r, 36, stride=8), :]
        e[t, Q + 36:Q + 40] = jnp.zeros((4, 128), F32)
    for t in (0, 13):
        e[t, DEEP:PLANES] = jnp.zeros((PLANES - DEEP, 128), F32)

    @pl.when(gx == 0)
    def _():
        for t in (0, 1, 2):
            e[t] = jnp.zeros((PLANES, 128), F32)

    @pl.when(gx == nx - 1)
    def _():
        for t in (11, 12, 13):
            e[t] = jnp.zeros((PLANES, 128), F32)

    count = sum(has[side].astype(jnp.int32) for side in where)
    pl.semaphore_wait(barrier, count)

    def remote(src, dst, k, side):
        return pltpu.make_async_remote_copy(
            src_ref=src, dst_ref=dst, send_sem=send_sem.at[k], recv_sem=recv_sem.at[k],
            device_id=where[side], device_id_type=MESH,
        )

    down = [
        remote(e.at[3:6, 0:DEEP], e.at[11:14, 0:DEEP], 0, "down"),
        remote(e.at[3:5, DEEP:PLANES], e.at[11:13, DEEP:PLANES], 1, "down"),
    ]
    up = [
        remote(e.at[8:11, 0:DEEP], e.at[0:3, 0:DEEP], 2, "up"),
        remote(e.at[9:11, DEEP:PLANES], e.at[1:3, DEEP:PLANES], 3, "up"),
    ]

    @pl.when(has["down"])
    def _():
        for c in down:
            c.start()

    @pl.when(has["up"])
    def _():
        for c in up:
            c.start()

    lane = lax.broadcasted_iota(jnp.int32, (PLANES, 128), 1)
    row_of = ((lane + 1) & 127) >> 3
    column = ((lane + 1) & 7) - 1

    def pack(tiles):
        total = packed[...]
        for t in tiles:
            total = jnp.where(row_of == t, pltpu.roll(e[t], 8 * t + 3, 1), total)
        packed[...] = total

    packed[...] = jnp.zeros((PLANES, 128), F32)
    pack(range(3, 11))

    banded_weights(stiff[...], w)

    @pl.when(has["down"])
    def _():
        for c in up:
            c.wait_recv()

    @pl.when(has["up"])
    def _():
        for c in down:
            c.wait_recv()

    pack((0, 1, 2, 11, 12, 13))
    to_left = remote(packed, from_right, 4, "left")
    to_right = remote(packed, from_left, 5, "right")

    @pl.when(has["left"])
    def _():
        to_left.start()

    @pl.when(has["right"])
    def _():
        to_right.start()

    e[LEFT] = jnp.where(column >= 3, packed[...], 0.0)
    e[RIGHT] = jnp.where(column <= 2, packed[...], 0.0)

    @pl.when(has["left"])
    def _():
        to_right.wait_recv()
        e[LEFT] = jnp.where(column <= 2, from_left[...], e[LEFT])

    @pl.when(has["right"])
    def _():
        to_left.wait_recv()
        e[RIGHT] = jnp.where(column >= 3, from_right[...], e[RIGHT])

    @pl.when(has["down"])
    def _():
        for c in down:
            c.wait_send()

    @pl.when(has["up"])
    def _():
        for c in up:
            c.wait_send()

    @pl.when(has["left"])
    def _():
        to_left.wait_send()

    @pl.when(has["right"])
    def _():
        to_right.wait_send()


def plate_kernel(e, w, first, second, sens, fac, fup, srep, load, u1, u2, a2, a1, z, xh, xl, xsh, xsl, acc0, acc1):
    lane = lax.broadcasted_iota(jnp.int32, (GROUP, 128), 1)
    layer = lax.broadcasted_iota(jnp.int32, (12, 128), 0).astype(F32)
    edge = (lane == 0) | (lane == 127)
    from_left = ((lane + 1) & 7) >= 4
    wl = jnp.zeros((8, 128), F32)

    def halves(v):
        v = jnp.concatenate([v, wl], 0)
        high = v.astype(BF16)
        return high, (v - high.astype(F32)).astype(BF16)

    def put(t, v):
        high, low = halves(v)
        xh[t, 0:SLOT] = high
        xl[t, 0:SLOT] = low
        high, low = halves(pltpu.roll(v, 127, 1))
        xh[t, SLOT:2 * SLOT] = high
        xl[t, SLOT:2 * SLOT] = low

    def put_seam(side, v):
        cols = slice(128 * side, 128 * side + 128)
        for k, by in enumerate((0, 127, 120, 119)):
            high, low = halves(pltpu.roll(v, by, 1) if by else v)
            xsh[SLOT * k:SLOT * (k + 1), cols] = high
            xsl[SLOT * k:SLOT * (k + 1), cols] = low

    def field(t, at):
        rows = lax.broadcasted_iota(jnp.int32, (GROUP, 128), 0)
        return jnp.where(rows < 36, e[t, at:at + GROUP], 0.0)

    zeros = jnp.zeros((GROUP, 128), F32)

    def prepare(t, _):
        d = e[t, D:D + 12]
        f = jnp.where(d > 0.0, EMIN + (1.0 - EMIN) * (d * d * d), 0.0)
        s = e[t, S:S + 12]
        fac[t] = zeros
        fup[t] = zeros
        srep[t] = zeros
        load[t] = zeros
        for c in (0, 12, 24):
            fac[t, c:c + 12] = f
            fup[t, c + 1:c + 12] = f[0:11]
            srep[t, c:c + 12] = s
        load[t, 24:36] = jnp.where(e[t, LOAD + 1:LOAD + 2] == layer, e[t, LOAD:LOAD + 1], 0.0)
        acc0[t] = zeros
        acc1[t] = zeros
        put(t, field(t, U))
        return 0

    lax.fori_loop(0, TILES, prepare, 0)
    for side in (0, 1):
        put_seam(side, field(LEFT + side, U))

    def forces(high, low):
        return (
            jnp.dot(w[0], high, preferred_element_type=F32)
            + jnp.dot(w[1], high, preferred_element_type=F32)
            + jnp.dot(w[0], low, preferred_element_type=F32)
        )

    def weigh(t, f):
        return [
            fac[t] * f[(2 * k) * GROUP:(2 * k + 1) * GROUP] + fup[t] * f[(2 * k + 1) * GROUP:(2 * k + 2) * GROUP]
            for k in range(4)
        ]

    def collect(t, f, corners):
        for dz, acc in ((0, acc0), (1, acc1)):
            total = acc[t]
            for k in range(4):
                total = total + f[(2 * k + dz) * GROUP:(2 * k + dz + 1) * GROUP] * corners[k]
            acc[t] = total

    def stiffness_map(start, pairs, finish, seam_finish, state=None):
        f = forces(xsh[...], xsl[...])
        seams = []
        for side in (0, 1):
            t = LEFT + side
            part = f[:, 128 * side:128 * side + 128]
            if state is not None and side == 1:
                v = state(t)
                collect(t, part, [pltpu.roll(v, by, 1) if by else v for by in (0, 127, 120, 119)])
            g = weigh(t, part)
            seams.append(g[0] + pltpu.roll(g[1], 1, 1) + pltpu.roll(g[2], 8, 1) + pltpu.roll(g[3], 9, 1))
        both = jnp.where(from_left, seams[0], seams[1])

        def step(i, carry):
            t0 = start + 2 * i
            tiles = [xh[t0 + k] for k in range(3)]
            lows = [xl[t0 + k] for k in range(3)]
            high = jnp.concatenate([jnp.concatenate(tiles[0:2], 0), jnp.concatenate(tiles[1:3], 0)], 1)
            low = jnp.concatenate([jnp.concatenate(lows[0:2], 0), jnp.concatenate(lows[1:3], 0)], 1)
            f = forces(high, low)
            if state is not None:
                @pl.when((t0 >= 2) & (t0 <= 10))
                def _():
                    for k in (0, 1):
                        here, there = state(t0 + k), state(t0 + k + 1)
                        collect(t0 + k, f[:, 128 * k:128 * k + 128], [here, pltpu.roll(here, 127, 1), there, pltpu.roll(there, 127, 1)])
            below, below_rolled = carry
            for k in (0, 1):
                t = t0 + k
                g = weigh(t, f[:, 128 * k:128 * k + 128])
                out = g[0] + below + pltpu.roll(g[1] + below_rolled, 1, 1)
                out = jnp.where(edge, pltpu.roll(both, 125 - 8 * t, 1), out)
                finish(t, out)
                below, below_rolled = g[2], g[3]
            return below, below_rolled

        lax.fori_loop(0, pairs, step, (zeros, zeros))
        for side in (0, 1):
            seam_finish(side, seams[side])

    def displacement(now, before, target, follow):
        def value(t, out):
            s = srep[t]
            return jnp.where(s > 0.0, 2.0 * now(t) - before(t) + s * (load[t] - out), 0.0)

        def finish(t, out):
            v = value(t, out)
            target[t] = v
            if follow:
                put(t, v)

        def seam_finish(side, out):
            v = value(LEFT + side, out)
            target[LEFT + side] = v
            if follow:
                put_seam(side, v)

        return finish, seam_finish

    def adjoint(now, before, target, result):
        def value(t, out):
            return 2.0 * now(t) - before(t) + load[t] - out

        def finish(t, out):
            v = value(t, out)
            if target is not None:
                target[t] = v
                put(t, srep[t] * v)
            if result is not None:
                @pl.when((t >= 3) & (t <= 10))
                def _():
                    result[pl.ds(t - 3, 36, stride=8), :] = v[0:36]

        def seam_finish(side, out):
            if target is not None:
                v = value(LEFT + side, out)
                target[LEFT + side] = v
                put_seam(side, srep[LEFT + side] * v)

        return finish, seam_finish

    u_now = lambda t: field(t, U)
    u_before = lambda t: field(t, B)
    adj_next = lambda t: field(t, A)
    adj_later = lambda t: field(t, Q)
    of = lambda ref: (lambda t: ref[t])

    stiffness_map(1, 6, *displacement(u_now, u_before, u1, True))
    stiffness_map(2, 5, *displacement(of(u1), u_now, u2, False))

    def weighted(t, _):
        put(t, srep[t] * adj_next(t))
        return 0

    lax.fori_loop(0, TILES, weighted, 0)
    for side in (0, 1):
        put_seam(side, srep[LEFT + side] * adj_next(LEFT + side))

    stiffness_map(0, 7, *adjoint(adj_next, adj_later, a2, None), of(u2))
    stiffness_map(1, 6, *adjoint(of(a2), adj_next, a1, second), of(u1))
    stiffness_map(2, 5, *adjoint(of(a1), of(a2), None, first), u_now)

    def total(t):
        p, r = acc0[t], acc1[t]
        return p[0:11] + p[12:23] + p[24:35] + r[1:12] + r[13:24] + r[25:36]

    seam = total(RIGHT)
    last = lax.broadcasted_iota(jnp.int32, (11, 128), 1) == 127
    for r in range(ROWS):
        t = r + 3
        d = e[t, D:D + 11]
        both = jnp.where(last, pltpu.roll(seam, 125 - 8 * t, 1), total(t))
        sens[pl.ds(r, 11, stride=8), :] = (-3.0 * (1.0 - EMIN)) * (d * d) * both


def local(u_now, u_prev, adjoint_next, adjoint_later, density, step_factor, fixed_nodes, load_top, load_depth, brick_stiffness):
    vmem = pl.BlockSpec(memory_space=pltpu.VMEM)
    flat = lambda x: x.reshape(-1, 128)
    sources = (
        flat(u_now), flat(u_prev), flat(adjoint_next), flat(adjoint_later), flat(density), flat(step_factor),
        flat(fixed_nodes), load_top, load_depth, brick_stiffness,
    )
    e, w = pl.pallas_call(
        exchange_kernel,
        out_shape=(
            jax.ShapeDtypeStruct((TILES, PLANES, 128), F32),
            jax.ShapeDtypeStruct((2, OUT, DEPTH), BF16),
        ),
        in_specs=[pl.BlockSpec(memory_space=pltpu.HBM)] * 10,
        out_specs=(vmem, vmem),
        scratch_shapes=[pltpu.VMEM(x.shape, x.dtype) for x in sources] + [
            pltpu.VMEM((PLANES, 128), F32),
            pltpu.VMEM((PLANES, 128), F32),
            pltpu.VMEM((PLANES, 128), F32),
            pltpu.SemaphoreType.DMA((10,)),
            pltpu.SemaphoreType.DMA((6,)),
            pltpu.SemaphoreType.DMA((6,)),
        ],
        compiler_params=pltpu.CompilerParams(collective_id=0, has_side_effects=True, vmem_limit_bytes=48 * 2**20),
        name="exchange",
    )(*(pltpu.with_memory_space_constraint(x, pltpu.HBM) for x in sources))
    tile = pltpu.VMEM((TILES, GROUP, 128), F32)
    first, second, sens = pl.pallas_call(
        plate_kernel,
        out_shape=(
            jax.ShapeDtypeStruct((36 * ROWS, 128), F32),
            jax.ShapeDtypeStruct((36 * ROWS, 128), F32),
            jax.ShapeDtypeStruct((11 * ROWS, 128), F32),
        ),
        in_specs=[vmem] * 2,
        out_specs=(vmem,) * 3,
        scratch_shapes=[tile] * 9 + [
            pltpu.VMEM((TILES, 2 * SLOT, 128), BF16),
            pltpu.VMEM((TILES, 2 * SLOT, 128), BF16),
            pltpu.VMEM((DEPTH, 256), BF16),
            pltpu.VMEM((DEPTH, 256), BF16),
            tile, tile,
        ],
        compiler_params=pltpu.CompilerParams(vmem_limit_bytes=40 * 2**20),
        name="plate",
    )(e, w)
    return (
        first.reshape(u_now.shape),
        second.reshape(u_now.shape),
        sens.reshape(density.shape),
    )


def solution(mesh):
    in_specs = (
        P(None, None, "gx", "gy"),
        P(None, None, "gx", "gy"),
        P(None, None, "gx", "gy"),
        P(None, None, "gx", "gy"),
        P(None, "gx", "gy"),
        P(None, "gx", "gy"),
        P(None, "gx", "gy"),
        P("gx", "gy"),
        P("gx", "gy"),
        P(),
    )
    out_specs = (P(None, None, "gx", "gy"), P(None, None, "gx", "gy"), P(None, "gx", "gy"))
    return jax.shard_map(local, mesh=mesh, in_specs=in_specs, out_specs=out_specs, check_vma=False)
```

```python
import jax
import jax.numpy as jnp
from jax import lax
from jax.experimental import pallas as pl
from jax.experimental.pallas import tpu as pltpu
from jax.sharding import PartitionSpec as P

EMIN = 0.001
MESH = pl.DeviceIdType.MESH
F32 = jnp.float32
BF16 = jnp.bfloat16

ROWS = 8
TILES = 16
LEFT, RIGHT = 14, 15
U, S, A, D, B, LOAD, Q, PLANES = 0, 36, 48, 84, 96, 132, 136, 176
DEEP = 96
GROUP = 40
OUT = 8 * GROUP
WIDE = 6 * GROUP
DEPTH = 2 * WIDE


def banded_weights(stiff, w):
    def split(place):
        comp = (place >= 12).astype(jnp.int32) + (place >= 24).astype(jnp.int32)
        return comp, place - 12 * comp

    iota = lambda shape, d: lax.broadcasted_iota(jnp.int32, shape, d)
    group, r = iota((8, GROUP, 24), 0), iota((8, GROUP, 24), 1)
    dz = group & 1
    comp, layer = split(r)
    element = layer - dz
    real = (r < 36) & (element >= 0) & (element <= 10)
    pick = jnp.where(real & (iota((8, GROUP, 24), 2) == comp * 8 + 4 * dz + (group >> 1)), 1.0, 0.0)
    pick = pick.reshape(OUT, 24).astype(BF16)

    def columns(shape):
        q = iota(shape, len(shape) - 1)
        block = sum((q >= GROUP * k).astype(jnp.int32) for k in range(1, 12))
        s = q - GROUP * block
        dx = (block >= 6).astype(jnp.int32)
        block = block - 6 * dx
        dy = ((block == 2) | (block == 3) | (block == 5)).astype(jnp.int32)
        return (2 * dx + dy, block >= 4, s) + split(s)

    place, fine, s, comp, _ = columns((24, DEPTH))
    offset = columns((8, GROUP, DEPTH))[4] - split(iota((8, GROUP, DEPTH), 1))[1] + (iota((8, GROUP, DEPTH), 0) & 1)
    offset = offset.reshape(OUT, DEPTH)
    low = stiff - stiff.astype(BF16).astype(F32)
    full = jnp.zeros((OUT, DEPTH), F32)
    for part, value in enumerate((stiff.astype(BF16), low.astype(BF16))):
        rows = jnp.dot(pick, value, preferred_element_type=F32).astype(BF16)
        for up in (0, 1):
            here = (s < 36) & (iota((24, DEPTH), 0) == comp * 8 + 4 * up + place) & (fine == bool(part))
            spread = jnp.where(here, 1.0, 0.0).astype(BF16)
            full = full + jnp.where(offset == up, jnp.dot(rows, spread, preferred_element_type=F32), 0.0)
    w[...] = full.astype(BF16)


def exchange_kernel(*refs):
    sources, (e, w), held, rest = refs[:10], refs[10:12], refs[12:22], refs[22:]
    u, b, a, q, den, step, fix, top, depth, stiff = held
    packed, from_left, from_right, load_sem, send_sem, recv_sem = rest
    gx, gy = lax.axis_index("gx"), lax.axis_index("gy")
    nx, ny = lax.axis_size("gx"), lax.axis_size("gy")
    has = {"down": gx > 0, "up": gx < nx - 1, "left": gy > 0, "right": gy < ny - 1}
    where = {"down": (gx - 1, gy), "up": (gx + 1, gy), "left": (gx, gy - 1), "right": (gx, gy + 1)}
    barrier = pltpu.get_barrier_semaphore()
    for side in where:
        @pl.when(has[side])
        def _(side=side):
            pl.semaphore_signal(barrier, inc=1, device_id=where[side], device_id_type=MESH)

    loads = [pltpu.make_async_copy(src, dst, load_sem.at[k]) for k, (src, dst) in enumerate(zip(sources, held))]
    for c in loads:
        c.start()
    for c in loads:
        c.wait()
    for r in range(ROWS):
        t = r + 3
        free = 1.0 - fix[pl.ds(r, 12, stride=8), :].astype(F32)
        e[t, U:U + 36] = u[pl.ds(r, 36, stride=8), :]
        e[t, S:S + 12] = free * step[pl.ds(r, 12, stride=8), :]
        e[t, A:A + 36] = a[pl.ds(r, 36, stride=8), :]
        e[t, D:D + 11] = den[pl.ds(r, 11, stride=8), :]
        e[t, D + 11:D + 12] = jnp.zeros((1, 128), F32)
        e[t, B:B + 36] = b[pl.ds(r, 36, stride=8), :]
        e[t, LOAD:LOAD + 1] = top[r:r + 1, :]
        e[t, LOAD + 1:LOAD + 2] = depth[r:r + 1, :].astype(F32)
        e[t, LOAD + 2:LOAD + 4] = jnp.zeros((2, 128), F32)
        e[t, Q:Q + 36] = q[pl.ds(r, 36, stride=8), :]
        e[t, Q + 36:Q + 40] = jnp.zeros((4, 128), F32)
    for t in (0, 13):
        e[t, DEEP:PLANES] = jnp.zeros((PLANES - DEEP, 128), F32)

    @pl.when(gx == 0)
    def _():
        for t in (0, 1, 2):
            e[t] = jnp.zeros((PLANES, 128), F32)

    @pl.when(gx == nx - 1)
    def _():
        for t in (11, 12, 13):
            e[t] = jnp.zeros((PLANES, 128), F32)

    count = sum(has[side].astype(jnp.int32) for side in where)
    pl.semaphore_wait(barrier, count)

    def remote(src, dst, k, side):
        return pltpu.make_async_remote_copy(
            src_ref=src, dst_ref=dst, send_sem=send_sem.at[k], recv_sem=recv_sem.at[k],
            device_id=where[side], device_id_type=MESH,
        )

    down = [
        remote(e.at[3:6, 0:DEEP], e.at[11:14, 0:DEEP], 0, "down"),
        remote(e.at[3:5, DEEP:PLANES], e.at[11:13, DEEP:PLANES], 1, "down"),
    ]
    up = [
        remote(e.at[8:11, 0:DEEP], e.at[0:3, 0:DEEP], 2, "up"),
        remote(e.at[9:11, DEEP:PLANES], e.at[1:3, DEEP:PLANES], 3, "up"),
    ]

    @pl.when(has["down"])
    def _():
        for c in down:
            c.start()

    @pl.when(has["up"])
    def _():
        for c in up:
            c.start()

    lane = lax.broadcasted_iota(jnp.int32, (PLANES, 128), 1)
    row_of = ((lane + 1) & 127) >> 3
    column = ((lane + 1) & 7) - 1

    def pack(tiles):
        total = packed[...]
        for t in tiles:
            total = jnp.where(row_of == t, pltpu.roll(e[t], 8 * t + 3, 1), total)
        packed[...] = total

    packed[...] = jnp.zeros((PLANES, 128), F32)
    pack(range(3, 11))

    banded_weights(stiff[...], w)

    @pl.when(has["down"])
    def _():
        for c in up:
            c.wait_recv()

    @pl.when(has["up"])
    def _():
        for c in down:
            c.wait_recv()

    pack((0, 1, 2, 11, 12, 13))
    to_left = remote(packed, from_right, 4, "left")
    to_right = remote(packed, from_left, 5, "right")

    @pl.when(has["left"])
    def _():
        to_left.start()

    @pl.when(has["right"])
    def _():
        to_right.start()

    e[LEFT] = jnp.where(column >= 3, packed[...], 0.0)
    e[RIGHT] = jnp.where(column <= 2, packed[...], 0.0)

    @pl.when(has["left"])
    def _():
        to_right.wait_recv()
        e[LEFT] = jnp.where(column <= 2, from_left[...], e[LEFT])

    @pl.when(has["right"])
    def _():
        to_left.wait_recv()
        e[RIGHT] = jnp.where(column >= 3, from_right[...], e[RIGHT])

    @pl.when(has["down"])
    def _():
        for c in down:
            c.wait_send()

    @pl.when(has["up"])
    def _():
        for c in up:
            c.wait_send()

    @pl.when(has["left"])
    def _():
        to_left.wait_send()

    @pl.when(has["right"])
    def _():
        to_right.wait_send()


def halves(v):
    high = v.astype(BF16).astype(F32)
    return high, v - high


def spread_halves(here, rolled):
    (h, l), (hr, lr) = here, rolled
    return [jnp.concatenate(x, 0).astype(BF16) for x in ((h, l), (hr, lr), (h, hr))]


def plate_kernel(e, w, first_out, second_out, sens_out, fac, fup, srep, load, u0r, u1, u1r, u2, u2r, a2, a1, acc0, acc1, xu0, xu1, xz3, xz2, xz1, xs, first, second, sens, out_sem):
    lane = lax.broadcasted_iota(jnp.int32, (GROUP, 128), 1)
    layer = lax.broadcasted_iota(jnp.int32, (12, 128), 0).astype(F32)
    edge = (lane == 0) | (lane == 127)
    from_left = ((lane + 1) & 7) >= 4
    roll = lambda v, by: pltpu.roll(v, by, 1) if by else v
    tile_rows = lambda at: (lambda t: e[t, at:at + GROUP])
    of = lambda ref: (lambda t: ref[t])
    u_now, u_before, adj_next, adj_later = (tile_rows(at) for at in (U, B, A, Q))

    def put(x, t, v, rolled_ref=None):
        here = halves(v)
        if rolled_ref is None:
            rolled = tuple(roll(part, 127) for part in here)
        else:
            vr = roll(v, 127)
            rolled_ref[t] = vr
            rolled = halves(vr)
        for k, part in enumerate(spread_halves(here, rolled)):
            x[t, 80 * k:80 * k + 80] = part

    def put_seam(n, side, v):
        here = halves(v)
        cols = slice(128 * side, 128 * side + 128)
        at = 0
        for pair in ((0, 127), (120, 119)):
            parts = spread_halves(*(tuple(roll(part, by) for part in here) for by in pair))
            for part in parts:
                xs[n, at:at + 80, cols] = part
                at += 80

    def prepare(t):
        d = e[t, D:D + 12]
        f = jnp.where(d > 0.0, EMIN + (1.0 - EMIN) * (d * d * d), 0.0)
        s = e[t, S:S + 12]
        top = jnp.where(e[t, LOAD + 1:LOAD + 2] == layer, e[t, LOAD:LOAD + 1], 0.0)
        fac[t, 36:40] = jnp.zeros((4, 128), F32)
        fup[t, 0:1] = jnp.zeros((1, 128), F32)
        fup[t, 36:40] = jnp.zeros((4, 128), F32)
        srep[t, 36:40] = jnp.zeros((4, 128), F32)
        load[t, 0:24] = jnp.zeros((24, 128), F32)
        load[t, 24:36] = top
        load[t, 36:40] = jnp.zeros((4, 128), F32)
        for c in (0, 12, 24):
            fac[t, c:c + 12] = f
            fup[t, c + 1:c + 12] = f[0:11]
            if c:
                fup[t, c:c + 1] = jnp.zeros((1, 128), F32)
            srep[t, c:c + 12] = s

    def weigh(t, f):
        return [
            fac[t] * f[(2 * k) * GROUP:(2 * k + 1) * GROUP] + fup[t] * f[(2 * k + 1) * GROUP:(2 * k + 2) * GROUP]
            for k in range(4)
        ]

    def collect(t, f, corners, fresh):
        for dz, acc in ((0, acc0), (1, acc1)):
            total = None if fresh else acc[t]
            for k in range(4):
                term = f[(2 * k + dz) * GROUP:(2 * k + dz + 1) * GROUP] * corners[k]
                total = term if total is None else total + term
            acc[t] = total

    def seam_map(n, finish, state=None, fresh=False):
        f = jnp.dot(w[...], xs[n], preferred_element_type=F32)
        outs = []
        for side in (0, 1):
            t = LEFT + side
            part = f[:, 128 * side:128 * side + 128]
            if state is not None and side == 1:
                v = state(t)
                collect(t, part, [roll(v, by) for by in (0, 127, 120, 119)], fresh)
            g = weigh(t, part)
            outs.append(g[0] + roll(g[1], 1) + roll(g[2], 8) + roll(g[3], 9))
            if finish is not None:
                finish(side, outs[-1])
        return jnp.where(from_left, outs[0], outs[1])

    def main_map(x, start, stop, seam, finish, state=None, fresh=False):
        below = below_rolled = None
        pending = None

        def post(t0, f):
            nonlocal below, below_rolled
            for k in (0, 1):
                t = t0 + k
                if t >= stop:
                    continue
                part = f[:, 128 * k:128 * k + 128]
                if state is not None and 3 <= t <= 10:
                    now, rolled = state
                    collect(t, part, [now(t), rolled(t), now(t + 1), rolled(t + 1)], fresh)
                g = weigh(t, part)
                if below is not None:
                    out = g[0] + below + roll(g[1] + below_rolled, 1)
                    finish(t, jnp.where(edge, roll(seam, 125 - 8 * t), out))
                below, below_rolled = g[2], g[3]

        for t0 in range(start, stop, 2):
            wide = [jnp.concatenate([x[t], x[t + 1]], 0) for t in (t0, t0 + 1)]
            f = jnp.dot(w[...], jnp.concatenate(wide, 1), preferred_element_type=F32)
            if pending is not None:
                post(*pending)
            pending = (t0, f)
        post(*pending)

    def step_u(t, now, before, out):
        s = srep[t]
        return jnp.where(s > 0.0, 2.0 * now(t) - before(t) + s * (load[t] - out), 0.0)

    def step_a(t, now, before, out):
        return 2.0 * now(t) - before(t) + load[t] - out

    for t in (LEFT, RIGHT):
        prepare(t)
        put_seam(0, t - LEFT, u_now(t))
        put_seam(2, t - LEFT, srep[t] * adj_next(t))

    def seam_u1(side, out):
        v = step_u(LEFT + side, u_now, u_before, out)
        u1[LEFT + side] = v
        put_seam(1, side, v)

    def seam_u2(side, out):
        u2[LEFT + side] = step_u(LEFT + side, of(u1), u_now, out)

    def seam_a2(side, out):
        v = step_a(LEFT + side, adj_next, adj_later, out)
        a2[LEFT + side] = v
        put_seam(3, side, srep[LEFT + side] * v)

    def seam_a1(side, out):
        v = step_a(LEFT + side, of(a2), adj_next, out)
        put_seam(4, side, srep[LEFT + side] * v)

    for t in range(14):
        prepare(t)
        put(xu0, t, u_now(t), u0r)
    k1 = seam_map(0, seam_u1)
    k2 = seam_map(1, seam_u2)
    for t in range(14):
        put(xz3, t, srep[t] * adj_next(t))
    k3 = seam_map(2, seam_a2, of(u2), True)
    k4 = seam_map(3, seam_a1, of(u1))
    k5 = seam_map(4, None, u_now)

    def main_u1(t, out):
        v = step_u(t, u_now, u_before, out)
        u1[t] = v
        put(xu1, t, v, u1r)

    def main_u2(t, out):
        v = step_u(t, of(u1), u_now, out)
        u2[t] = v
        u2r[t] = roll(v, 127)

    def main_a2(t, out):
        v = step_a(t, adj_next, adj_later, out)
        a2[t] = v
        put(xz2, t, srep[t] * v)

    def main_a1(t, out):
        v = step_a(t, of(a2), adj_next, out)
        a1[t] = v
        put(xz1, t, srep[t] * v)
        if 3 <= t <= 10:
            second[pl.ds(t - 3, 36, stride=8), :] = v[0:36]

    def main_a0(t, out):
        first[pl.ds(t - 3, 36, stride=8), :] = step_a(t, of(a1), of(a2), out)[0:36]

    main_map(xu0, 1, 13, k1, main_u1)
    main_map(xu1, 2, 12, k2, main_u2)
    main_map(xz3, 0, 13, k3, main_a2, (of(u2), of(u2r)), True)
    main_map(xz2, 1, 12, k4, main_a1, (of(u1), of(u1r)))
    copy_second = pltpu.make_async_copy(second, second_out, out_sem.at[1])
    copy_second.start()
    main_map(xz1, 2, 11, k5, main_a0, (u_now, of(u0r)))
    copy_first = pltpu.make_async_copy(first, first_out, out_sem.at[0])
    copy_first.start()

    def total(t):
        return sum(acc0[t, c:c + 11] + acc1[t, c + 1:c + 12] for c in (0, 12, 24))

    seam = total(RIGHT)
    last = lax.broadcasted_iota(jnp.int32, (11, 128), 1) == 127
    for r in range(ROWS):
        t = r + 3
        d = e[t, D:D + 11]
        both = jnp.where(last, roll(seam, 125 - 8 * t), total(t))
        sens[pl.ds(r, 11, stride=8), :] = (-3.0 * (1.0 - EMIN)) * (d * d) * both
    copy_sens = pltpu.make_async_copy(sens, sens_out, out_sem.at[2])
    copy_sens.start()
    copy_second.wait()
    copy_first.wait()
    copy_sens.wait()


def local(u_now, u_prev, adjoint_next, adjoint_later, density, step_factor, fixed_nodes, load_top, load_depth, brick_stiffness):
    vmem = pl.BlockSpec(memory_space=pltpu.VMEM)
    flat = lambda x: x.reshape(-1, 128)
    sources = (
        flat(u_now), flat(u_prev), flat(adjoint_next), flat(adjoint_later), flat(density), flat(step_factor),
        flat(fixed_nodes), load_top, load_depth, brick_stiffness,
    )
    e, w = pl.pallas_call(
        exchange_kernel,
        out_shape=(
            jax.ShapeDtypeStruct((TILES, PLANES, 128), F32),
            jax.ShapeDtypeStruct((OUT, DEPTH), BF16),
        ),
        in_specs=[pl.BlockSpec(memory_space=pltpu.HBM)] * 10,
        out_specs=(vmem, vmem),
        scratch_shapes=[pltpu.VMEM(x.shape, x.dtype) for x in sources] + [
            pltpu.VMEM((PLANES, 128), F32),
            pltpu.VMEM((PLANES, 128), F32),
            pltpu.VMEM((PLANES, 128), F32),
            pltpu.SemaphoreType.DMA((10,)),
            pltpu.SemaphoreType.DMA((6,)),
            pltpu.SemaphoreType.DMA((6,)),
        ],
        compiler_params=pltpu.CompilerParams(collective_id=0, has_side_effects=True, vmem_limit_bytes=48 * 2**20),
        name="exchange",
    )(*(pltpu.with_memory_space_constraint(x, pltpu.HBM) for x in sources))
    tile = pltpu.VMEM((TILES, GROUP, 128), F32)
    wide = pltpu.VMEM((TILES, WIDE, 128), BF16)
    results = ((36 * ROWS, 128), (36 * ROWS, 128), (11 * ROWS, 128))
    first, second, sens = pl.pallas_call(
        plate_kernel,
        out_shape=tuple(jax.ShapeDtypeStruct(shape, F32) for shape in results),
        in_specs=[vmem] * 2,
        out_specs=(pl.BlockSpec(memory_space=pltpu.HBM),) * 3,
        scratch_shapes=[tile] * 13 + [wide] * 5
        + [pltpu.VMEM((5, DEPTH, 256), BF16)]
        + [pltpu.VMEM(shape, F32) for shape in results]
        + [pltpu.SemaphoreType.DMA((3,))],
        compiler_params=pltpu.CompilerParams(vmem_limit_bytes=48 * 2**20),
        name="plate",
    )(e, w)
    return (
        first.reshape(u_now.shape),
        second.reshape(u_now.shape),
        sens.reshape(density.shape),
    )


def solution(mesh):
    in_specs = (
        P(None, None, "gx", "gy"),
        P(None, None, "gx", "gy"),
        P(None, None, "gx", "gy"),
        P(None, None, "gx", "gy"),
        P(None, "gx", "gy"),
        P(None, "gx", "gy"),
        P(None, "gx", "gy"),
        P("gx", "gy"),
        P("gx", "gy"),
        P(),
    )
    out_specs = (P(None, None, "gx", "gy"), P(None, None, "gx", "gy"), P(None, "gx", "gy"))
    return jax.shard_map(local, mesh=mesh, in_specs=in_specs, out_specs=out_specs, check_vma=False)
```

```python
import jax
import jax.numpy as jnp
from jax import lax
from jax.experimental import pallas as pl
from jax.experimental.pallas import tpu as pltpu
from jax.sharding import PartitionSpec as P

EMIN = 0.001
MESH = pl.DeviceIdType.MESH
F32 = jnp.float32
BF16 = jnp.bfloat16

ROWS = 8
OWN = range(3, 11)
MAIN = 14
LEFT, RIGHT = 14, 15
TILES = 16
U, S, A, D, B, LOAD, Q, PLANES = 0, 36, 48, 84, 96, 132, 136, 192
FOLD = 48
GROUP = 40
OUT = 8 * GROUP
WIDE = 6 * GROUP
DEPTH = 2 * WIDE


def banded_weights(stiff, w):
    def split(place):
        comp = (place >= 12).astype(jnp.int32) + (place >= 24).astype(jnp.int32)
        return comp, place - 12 * comp

    iota = lambda shape, d: lax.broadcasted_iota(jnp.int32, shape, d)
    group, r = iota((8, GROUP, 24), 0), iota((8, GROUP, 24), 1)
    dz = group & 1
    comp, layer = split(r)
    element = layer - dz
    real = (r < 36) & (element >= 0) & (element <= 10)
    pick = jnp.where(real & (iota((8, GROUP, 24), 2) == comp * 8 + 4 * dz + (group >> 1)), 1.0, 0.0)
    pick = pick.reshape(OUT, 24).astype(BF16)

    def columns(shape):
        q = iota(shape, len(shape) - 1)
        block = sum((q >= GROUP * k).astype(jnp.int32) for k in range(1, 12))
        s = q - GROUP * block
        dx = (block >= 6).astype(jnp.int32)
        block = block - 6 * dx
        dy = ((block == 2) | (block == 3) | (block == 5)).astype(jnp.int32)
        return (2 * dx + dy, block >= 4, s) + split(s)

    place, fine, s, comp, _ = columns((24, DEPTH))
    offset = columns((8, GROUP, DEPTH))[4] - split(iota((8, GROUP, DEPTH), 1))[1] + (iota((8, GROUP, DEPTH), 0) & 1)
    offset = offset.reshape(OUT, DEPTH)
    low = stiff - stiff.astype(BF16).astype(F32)
    full = jnp.zeros((OUT, DEPTH), F32)
    for part, value in enumerate((stiff.astype(BF16), low.astype(BF16))):
        rows = jnp.dot(pick, value, preferred_element_type=F32).astype(BF16)
        for up in (0, 1):
            here = (s < 36) & (iota((24, DEPTH), 0) == comp * 8 + 4 * up + place) & (fine == bool(part))
            spread = jnp.where(here, 1.0, 0.0).astype(BF16)
            full = full + jnp.where(offset == up, jnp.dot(rows, spread, preferred_element_type=F32), 0.0)
    w[...] = full.astype(BF16)


def roll(v, by):
    return pltpu.roll(v, by % 128, 1) if by % 128 else v


def lanes(rows):
    return lax.broadcasted_iota(jnp.int32, (rows, 128), 1)


def halves(v):
    high = v.astype(BF16).astype(F32)
    return high, v - high


def spread_halves(here, rolled):
    (h, l), (hr, lr) = here, rolled
    return [jnp.concatenate(x, 0).astype(BF16) for x in ((h, l), (hr, lr), (h, hr))]


def put(x, t, v, rolled_ref=None):
    here = halves(v)
    if rolled_ref is None:
        rolled = tuple(roll(part, 127) for part in here)
    else:
        vr = roll(v, 127)
        rolled_ref[t] = vr
        rolled = halves(vr)
    for k, part in enumerate(spread_halves(here, rolled)):
        x[t, 80 * k:80 * k + 80] = part


def prepare(at, tile, fac, fup, srep, load):
    layer = lax.broadcasted_iota(jnp.int32, (12, 128), 0).astype(F32)
    d = tile[D:D + 12]
    f = jnp.where(d > 0.0, EMIN + (1.0 - EMIN) * (d * d * d), 0.0)
    s = tile[S:S + 12]
    zeros = lambda n: jnp.zeros((n, 128), F32)
    fac[at, 36:40] = zeros(4)
    fup[at, 36:40] = zeros(4)
    srep[at, 36:40] = zeros(4)
    load[at, 0:24] = zeros(24)
    load[at, 24:36] = jnp.where(tile[LOAD + 1:LOAD + 2] == layer, tile[LOAD:LOAD + 1], 0.0)
    load[at, 36:40] = zeros(4)
    for c in (0, 12, 24):
        fac[at, c:c + 12] = f
        fup[at, c:c + 1] = zeros(1)
        fup[at, c + 1:c + 12] = f[0:11]
        srep[at, c:c + 12] = s


def weigh(f, above, below):
    return [
        above * f[(2 * k) * GROUP:(2 * k + 1) * GROUP] + below * f[(2 * k + 1) * GROUP:(2 * k + 2) * GROUP]
        for k in range(4)
    ]


def pairs_of(w, jobs, post):
    pending = []
    for at in range(0, len(jobs), 2):
        two = jobs[at:at + 2]
        wide = [jnp.concatenate([x, y], 0) for _, x, y in two]
        wide = wide[0] if len(wide) == 1 else jnp.concatenate(wide, 1)
        f = jnp.dot(w[...], wide, preferred_element_type=F32)
        for job in pending:
            post(*job)
        pending = [(key, f[:, 128 * k:128 * k + 128]) for k, (key, _, _) in enumerate(two)]
    for job in pending:
        post(*job)


def exchange_kernel(*refs):
    sources, refs = refs[:10], refs[10:]
    e, w, mine, near, corner, fac, fup, srep, load, u0r, xu0, xz3, o1, o3, p1, p3, f3 = refs[:17]
    held, (corner_out, load_sem, send_sem, recv_sem) = refs[17:27], refs[27:]
    u, b, a, q, den, step, fix, top, depth, stiff = held
    gx, gy = lax.axis_index("gx"), lax.axis_index("gy")
    nx, ny = lax.axis_size("gx"), lax.axis_size("gy")
    down, up, left, right = gx > 0, gx < nx - 1, gy > 0, gy < ny - 1
    sides = {
        (-1, 0): down, (1, 0): up, (0, -1): left, (0, 1): right,
        (-1, -1): down & left, (1, -1): up & left, (-1, 1): down & right, (1, 1): up & right,
    }
    barrier = pltpu.get_barrier_semaphore()
    for (dx, dy), there in sides.items():
        @pl.when(there)
        def _(dx=dx, dy=dy):
            pl.semaphore_signal(barrier, inc=1, device_id=(gx + dx, gy + dy), device_id_type=MESH)

    loads = [pltpu.make_async_copy(src, dst, load_sem.at[k]) for k, (src, dst) in enumerate(zip(sources, held))]
    for c in loads:
        c.start()
    zeros = lambda n: jnp.zeros((n, 128), F32)
    e[0, 0:32] = zeros(32)
    e[0, 96:PLANES] = zeros(PLANES - 96)
    e[1, 96:128] = zeros(32)
    for t in (1, 2, 11, 12):
        e[t, 176:PLANES] = zeros(PLANES - 176)
    e[13, 88:PLANES] = zeros(PLANES - 88)

    @pl.when(jnp.logical_not(down))
    def _():
        for t in (0, 1, 2):
            e[t] = zeros(PLANES)

    @pl.when(jnp.logical_not(up))
    def _():
        for t in (11, 12, 13):
            e[t] = zeros(PLANES)

    for k, dy in enumerate((-1, 1)):
        @pl.when(jnp.logical_not(sides[0, dy]))
        def _(k=k):
            near[k] = zeros(FOLD)

        for j, dx in enumerate((-1, 1)):
            @pl.when(jnp.logical_not(sides[dx, dy]))
            def _(k=k, j=j):
                corner[2 * k + j] = zeros(FOLD // 2)

    for c in loads:
        c.wait()
    for r in range(ROWS):
        t = r + 3
        free = 1.0 - fix[pl.ds(r, 12, stride=8), :].astype(F32)
        e[t, U:U + 36] = u[pl.ds(r, 36, stride=8), :]
        e[t, S:S + 12] = free * step[pl.ds(r, 12, stride=8), :]
        e[t, A:A + 36] = a[pl.ds(r, 36, stride=8), :]
        e[t, D:D + 11] = den[pl.ds(r, 11, stride=8), :]
        e[t, D + 11:D + 12] = zeros(1)
        e[t, B:B + 36] = b[pl.ds(r, 36, stride=8), :]
        e[t, LOAD:LOAD + 1] = top[r:r + 1, :]
        e[t, LOAD + 1:LOAD + 2] = depth[r:r + 1, :].astype(F32)
        e[t, LOAD + 2:LOAD + 4] = zeros(2)
        e[t, Q:Q + 36] = q[pl.ds(r, 36, stride=8), :]
        e[t, Q + 36:PLANES] = zeros(PLANES - Q - 36)

    lane = lanes(FOLD)
    first_cols, last_cols = zeros(FOLD), zeros(FOLD)
    for g in range(4):
        for r in range(ROWS):
            slot = 16 * (g >> 1) + 2 * r + (g & 1)
            v = roll(e[r + 3, FOLD * g:FOLD * g + FOLD], 4 * slot + 3)
            first_cols = jnp.where(((lane - 3) & 127) >> 2 == slot, v, first_cols)
            last_cols = jnp.where(((lane + 1) & 127) >> 2 == slot, v, last_cols)
    mine[0] = first_cols
    mine[1] = last_cols
    half = FOLD // 2
    lane = lanes(half)
    for k, cols in enumerate((first_cols, last_cols)):
        low = ((lane - 3 + 4 * k) & 63) < 32
        corner_out[2 * k] = jnp.where(low, cols[0:half], roll(cols[half:FOLD], 32))
        corner_out[2 * k + 1] = jnp.where(low, roll(cols[half:FOLD], -32), cols[0:half])

    pl.semaphore_wait(barrier, sum(there.astype(jnp.int32) for there in sides.values()))
    plan = [
        ((-1, -1), corner_out.at[0], corner.at[3]),
        ((1, -1), corner_out.at[1], corner.at[2]),
        ((-1, 1), corner_out.at[2], corner.at[1]),
        ((1, 1), corner_out.at[3], corner.at[0]),
        ((0, -1), mine.at[0], near.at[1]),
        ((0, 1), mine.at[1], near.at[0]),
        ((-1, 0), e.at[3:5, 0:176], e.at[11:13, 0:176]),
        ((1, 0), e.at[9:11, 0:96], e.at[1:3, 0:96]),
        ((1, 0), e.at[9:11, 128:176], e.at[1:3, 128:176]),
        ((-1, 0), e.at[5, 0:88], e.at[13, 0:88]),
        ((1, 0), e.at[8, 32:96], e.at[0, 32:96]),
        ((1, 0), e.at[10, 96:128], e.at[2, 96:128]),
    ]
    copies = []
    for k, ((dx, dy), src, dst) in enumerate(plan):
        copies.append(((dx, dy), pltpu.make_async_remote_copy(
            src_ref=src, dst_ref=dst, send_sem=send_sem.at[k], recv_sem=recv_sem.at[k],
            device_id=(gx + dx, gy + dy), device_id_type=MESH,
        )))
    for to, c in copies:
        @pl.when(sides[to])
        def _(c=c):
            c.start()

    banded_weights(stiff[...], w)
    for t in OWN:
        k = t - 3
        prepare(k, e.at[t], fac, fup, srep, load)
        put(xu0, k, e[t, U:U + GROUP], u0r)
        put(xz3, k, srep[k] * e[t, A:A + GROUP])

    carry = {}

    def post(key, f):
        kind, k = key
        out, pieces = ((o1, p1), (o3, p3))[kind]
        if kind:
            f3[k] = f
        g = weigh(f, fac[k], fup[k])
        if k == 0:
            pieces[0], pieces[1] = g[0], g[1]
        else:
            out[k - 1] = g[0] + carry[kind][0] + roll(g[1] + carry[kind][1], 1)
        if k == 6:
            pieces[2], pieces[3] = g[2], g[3]
        carry[kind] = g[2:]

    pairs_of(w, [((kind, k), x[k], x[k + 1]) for kind, x in ((0, xu0), (1, xz3)) for k in range(7)], post)

    for (dx, dy), c in copies:
        @pl.when(sides[-dx, -dy])
        def _(c=c):
            c.wait_recv()
    for to, c in copies:
        @pl.when(sides[to])
        def _(c=c):
            c.wait_send()


class Split:
    def __init__(self, own, others):
        self.own, self.others = own, others

    def spot(self, t):
        if t in OWN:
            return self.own, t - 3
        return self.others, t if t < 3 else t - 8

    def __getitem__(self, t):
        ref, at = self.spot(t)
        return ref[at]


def plate_kernel(*refs):
    e, w, mine, near, corner = refs[:5]
    own = refs[5:12]
    o1, o3, p1, p3, f3 = refs[12:17]
    first_out, second_out, sens_out = refs[17:20]
    others = refs[20:27]
    u1, u1r, u2, u2r, a2, a1, acc0, acc1, xu1, xz2, xz1, xs, es, first, second, sens, out_sem = refs[27:]
    fac, fup, srep, load, u0r, xu0, xz3 = (Split(x, y) for x, y in zip(own, others))
    lane = lanes(GROUP)
    edge = (lane == 0) | (lane == 127)
    from_left = ((lane + 1) & 7) >= 4

    def tile_rows(at):
        return lambda t: es[t - LEFT, at:at + GROUP] if t >= LEFT else e[t, at:at + GROUP]

    of = lambda ref: (lambda t: ref[t])
    u_now, u_before, adj_next, adj_later = (tile_rows(at) for at in (U, B, A, Q))

    wide_lane = lanes(FOLD)
    row = ((wide_lane + 1) & 127) >> 3
    late = ((wide_lane + 1) & 7) >= 4
    inner, low, high = (row >= 3) & (row <= 10), row < 3, (row > 10) & (row < 14)
    half = FOLD // 2
    for g in range(4):
        by = 24 - 64 * (g >> 1) - 4 * (g & 1)
        planes = slice(FOLD * g, FOLD * g + FOLD)
        ghost = jnp.zeros((FOLD, 128), F32)
        for t in (0, 1, 2, 11, 12, 13):
            ghost = jnp.where(row == t, roll(e[t, planes], 8 * t + 3), ghost)
        for side in (0, 1):
            near_cols = roll(near[side], by)
            own_cols = roll(mine[side], by)
            below = jnp.concatenate([roll(corner[2 * side], by + 64), roll(corner[2 * side], by + 96)], 0)
            above = jnp.concatenate([roll(corner[2 * side + 1], by + 64), roll(corner[2 * side + 1], by + 32)], 0)
            far = jnp.where(inner, near_cols, jnp.where(low, below, jnp.where(high, above, 0.0)))
            here = jnp.where(inner, own_cols, ghost)
            es[side, planes] = jnp.where(late, here, far) if side == 0 else jnp.where(late, far, here)

    def put_seam(n, side, v):
        here = halves(v)
        cols = slice(128 * side, 128 * side + 128)
        at = 0
        for pair in ((0, 127), (120, 119)):
            parts = spread_halves(*(tuple(roll(part, by) for part in here) for by in pair))
            for part in parts:
                xs[n, at:at + 80, cols] = part
                at += 80

    def collect(t, f, corners, fresh):
        for dz, acc in ((0, acc0), (1, acc1)):
            total = None if fresh else acc[t]
            for k in range(4):
                term = f[(2 * k + dz) * GROUP:(2 * k + dz + 1) * GROUP] * corners[k]
                total = term if total is None else total + term
            acc[t] = total

    def seam_map(n, finish, state=None, fresh=False):
        f = jnp.dot(w[...], xs[n], preferred_element_type=F32)
        outs = []
        for side in (0, 1):
            t = LEFT + side
            part = f[:, 128 * side:128 * side + 128]
            if state is not None and side == 1:
                v = state(t)
                collect(t, part, [roll(v, by) for by in (0, 127, 120, 119)], fresh)
            g = weigh(part, fac[t], fup[t])
            outs.append(g[0] + roll(g[1], 1) + roll(g[2], 8) + roll(g[3], 9))
            if finish is not None:
                finish(side, outs[-1])
        return jnp.where(from_left, outs[0], outs[1])

    def fixed(t, out, seam):
        return jnp.where(edge, roll(seam, 125 - 8 * t), out)

    def main_map(x, elements, seam, finish, state=None, fresh=False, done=None):
        carry = None

        def node(t, above, below):
            out = above[0] + below[0] + roll(above[1] + below[1], 1)
            finish(t, fixed(t, out, seam))

        def post(t, f):
            nonlocal carry
            if state is not None and t in OWN:
                now, rolled = state
                collect(t, f, [now(t), rolled(t), now(t + 1), rolled(t + 1)], fresh)
            g = weigh(f, fac[t], fup[t])
            if done is not None and t == 10:
                node(t, g[0:2], (done[1][2], done[1][3]))
            elif carry is not None:
                node(t, g[0:2], carry)
            carry = g[2:]
            if done is not None and t == 2:
                node(3, (done[1][0], done[1][1]), carry)
                for k in range(6):
                    finish(k + 4, fixed(k + 4, done[0][k], seam))

        pairs_of(w, [(t, x[t], x[t + 1]) for t in elements], post)

    def step_u(t, now, before, out):
        s = srep[t]
        return jnp.where(s > 0.0, 2.0 * now(t) - before(t) + s * (load[t] - out), 0.0)

    def step_a(t, now, before, out):
        return 2.0 * now(t) - before(t) + load[t] - out

    for t in (LEFT, RIGHT):
        prepare(t - 8, es.at[t - LEFT], *others[0:4])
        put_seam(0, t - LEFT, u_now(t))
        put_seam(2, t - LEFT, srep[t] * adj_next(t))

    def seam_u1(side, out):
        v = step_u(LEFT + side, u_now, u_before, out)
        u1[LEFT + side] = v
        put_seam(1, side, v)

    def seam_u2(side, out):
        u2[LEFT + side] = step_u(LEFT + side, of(u1), u_now, out)

    def seam_a2(side, out):
        v = step_a(LEFT + side, adj_next, adj_later, out)
        a2[LEFT + side] = v
        put_seam(3, side, srep[LEFT + side] * v)

    def seam_a1(side, out):
        v = step_a(LEFT + side, of(a2), adj_next, out)
        put_seam(4, side, srep[LEFT + side] * v)

    for t in (0, 1, 2, 11, 12, 13):
        at = t if t < 3 else t - 8
        prepare(at, e.at[t], *others[0:4])
        put(xu0.others, at, u_now(t), u0r.others)
    k1 = seam_map(0, seam_u1)
    k2 = seam_map(1, seam_u2)
    for t in (0, 1, 2, 11, 12, 13):
        put(xz3.others, t if t < 3 else t - 8, srep[t] * adj_next(t))
    k3 = seam_map(2, seam_a2, of(u2), True)
    k4 = seam_map(3, seam_a1, of(u1))
    k5 = seam_map(4, None, u_now)

    def main_u1(t, out):
        v = step_u(t, u_now, u_before, out)
        u1[t] = v
        put(xu1, t, v, u1r)

    def main_u2(t, out):
        v = step_u(t, of(u1), u_now, out)
        u2[t] = v
        u2r[t] = roll(v, 127)

    def main_a2(t, out):
        v = step_a(t, adj_next, adj_later, out)
        a2[t] = v
        put(xz2, t, srep[t] * v)

    def main_a1(t, out):
        v = step_a(t, of(a2), adj_next, out)
        a1[t] = v
        put(xz1, t, srep[t] * v)
        if t in OWN:
            second[pl.ds(t - 3, 36, stride=8), :] = v[0:36]

    def main_a0(t, out):
        first[pl.ds(t - 3, 36, stride=8), :] = step_a(t, of(a1), of(a2), out)[0:36]

    main_map(xu0, (1, 2, 10, 11, 12), k1, main_u1, done=(o1, p1))
    main_map(xu1, range(2, 12), k2, main_u2)
    for t in range(3, 10):
        collect(t, f3[t - 3], [u2[t], u2r[t], u2[t + 1], u2r[t + 1]], True)
    main_map(xz3, (0, 1, 2, 10, 11, 12), k3, main_a2, (of(u2), of(u2r)), True, done=(o3, p3))
    main_map(xz2, range(1, 12), k4, main_a1, (of(u1), of(u1r)))
    copy_second = pltpu.make_async_copy(second, second_out, out_sem.at[1])
    copy_second.start()
    main_map(xz1, range(2, 11), k5, main_a0, (u_now, of(u0r)))
    copy_first = pltpu.make_async_copy(first, first_out, out_sem.at[0])
    copy_first.start()

    def total(t):
        return sum(acc0[t, c:c + 11] + acc1[t, c + 1:c + 12] for c in (0, 12, 24))

    seam = total(RIGHT)
    last = lanes(11) == 127
    for r in range(ROWS):
        t = r + 3
        d = e[t, D:D + 11]
        both = jnp.where(last, roll(seam, 125 - 8 * t), total(t))
        sens[pl.ds(r, 11, stride=8), :] = (-3.0 * (1.0 - EMIN)) * (d * d) * both
    copy_sens = pltpu.make_async_copy(sens, sens_out, out_sem.at[2])
    copy_sens.start()
    copy_second.wait()
    copy_first.wait()
    copy_sens.wait()


def local(u_now, u_prev, adjoint_next, adjoint_later, density, step_factor, fixed_nodes, load_top, load_depth, brick_stiffness):
    vmem = pl.BlockSpec(memory_space=pltpu.VMEM)
    hbm = pl.BlockSpec(memory_space=pltpu.HBM)
    flat = lambda x: x.reshape(-1, 128)
    sources = (
        flat(u_now), flat(u_prev), flat(adjoint_next), flat(adjoint_later), flat(density), flat(step_factor),
        flat(fixed_nodes), load_top, load_depth, brick_stiffness,
    )
    f32 = lambda *shape: jax.ShapeDtypeStruct(shape + (128,), F32)
    bf16 = lambda *shape: jax.ShapeDtypeStruct(shape, BF16)
    passed = (
        [f32(MAIN, PLANES), bf16(OUT, DEPTH), f32(2, FOLD), f32(2, FOLD), f32(4, FOLD // 2)]
        + [f32(ROWS, GROUP)] * 5 + [bf16(ROWS, WIDE, 128)] * 2
        + [f32(6, GROUP)] * 2 + [f32(4, GROUP)] * 2 + [f32(7, OUT)]
    )
    gathered = pl.pallas_call(
        exchange_kernel,
        out_shape=passed,
        in_specs=[hbm] * 10,
        out_specs=[vmem] * len(passed),
        scratch_shapes=[pltpu.VMEM(x.shape, x.dtype) for x in sources] + [
            pltpu.VMEM((4, FOLD // 2, 128), F32),
            pltpu.SemaphoreType.DMA((10,)),
            pltpu.SemaphoreType.DMA((12,)),
            pltpu.SemaphoreType.DMA((12,)),
        ],
        compiler_params=pltpu.CompilerParams(collective_id=0, has_side_effects=True, vmem_limit_bytes=32 * 2**20),
        name="exchange",
    )(*(pltpu.with_memory_space_constraint(x, pltpu.HBM) for x in sources))
    scratch = lambda n, shape, kind: [pltpu.VMEM((n, shape, 128), kind)]
    results = ((36 * ROWS, 128), (36 * ROWS, 128), (11 * ROWS, 128))
    first, second, sens = pl.pallas_call(
        plate_kernel,
        out_shape=tuple(jax.ShapeDtypeStruct(shape, F32) for shape in results),
        in_specs=[vmem] * len(passed),
        out_specs=(hbm,) * 3,
        scratch_shapes=scratch(8, GROUP, F32) * 5 + scratch(8, WIDE, BF16) * 2
        + scratch(TILES, GROUP, F32) * 8 + scratch(TILES, WIDE, BF16) * 3
        + [pltpu.VMEM((5, DEPTH, 256), BF16), pltpu.VMEM((2, PLANES, 128), F32)]
        + [pltpu.VMEM(shape, F32) for shape in results]
        + [pltpu.SemaphoreType.DMA((3,))],
        compiler_params=pltpu.CompilerParams(vmem_limit_bytes=40 * 2**20),
        name="plate",
    )(*gathered)
    return (
        first.reshape(u_now.shape),
        second.reshape(u_now.shape),
        sens.reshape(density.shape),
    )


def solution(mesh):
    in_specs = (
        P(None, None, "gx", "gy"),
        P(None, None, "gx", "gy"),
        P(None, None, "gx", "gy"),
        P(None, None, "gx", "gy"),
        P(None, "gx", "gy"),
        P(None, "gx", "gy"),
        P(None, "gx", "gy"),
        P("gx", "gy"),
        P("gx", "gy"),
        P(),
    )
    out_specs = (P(None, None, "gx", "gy"), P(None, None, "gx", "gy"), P(None, "gx", "gy"))
    return jax.shard_map(local, mesh=mesh, in_specs=in_specs, out_specs=out_specs, check_vma=False)
```

```python
import jax
import jax.numpy as jnp
from jax import lax
from jax.experimental import pallas as pl
from jax.experimental.pallas import tpu as pltpu
from jax.sharding import PartitionSpec as P

EMIN = 0.001
MESH = pl.DeviceIdType.MESH
F32 = jnp.float32
BF16 = jnp.bfloat16

ROWS = 8
OWN = range(3, 11)
MAIN = 14
LEFT, RIGHT = 14, 15
TILES = 16
U, S, B, D, A, LOAD, Q, PLANES = 0, 36, 48, 84, 96, 136, 144, 192
FOLD = 48
GROUP = 40
OUT = 8 * GROUP
WIDE = 6 * GROUP
DEPTH = 2 * WIDE


def banded_weights(stiff, w):
    def split(place):
        comp = (place >= 12).astype(jnp.int32) + (place >= 24).astype(jnp.int32)
        return comp, place - 12 * comp

    iota = lambda shape, d: lax.broadcasted_iota(jnp.int32, shape, d)
    group, r = iota((8, GROUP, 24), 0), iota((8, GROUP, 24), 1)
    dz = group & 1
    comp, layer = split(r)
    element = layer - dz
    real = (r < 36) & (element >= 0) & (element <= 10)
    pick = jnp.where(real & (iota((8, GROUP, 24), 2) == comp * 8 + 4 * dz + (group >> 1)), 1.0, 0.0)
    pick = pick.reshape(OUT, 24).astype(BF16)

    def columns(shape):
        q = iota(shape, len(shape) - 1)
        block = sum((q >= GROUP * k).astype(jnp.int32) for k in range(1, 12))
        s = q - GROUP * block
        dx = (block >= 6).astype(jnp.int32)
        block = block - 6 * dx
        dy = ((block == 2) | (block == 3) | (block == 5)).astype(jnp.int32)
        return (2 * dx + dy, block >= 4, s) + split(s)

    place, fine, s, comp, _ = columns((24, DEPTH))
    offset = columns((8, GROUP, DEPTH))[4] - split(iota((8, GROUP, DEPTH), 1))[1] + (iota((8, GROUP, DEPTH), 0) & 1)
    offset = offset.reshape(OUT, DEPTH)
    low = stiff - stiff.astype(BF16).astype(F32)
    full = jnp.zeros((OUT, DEPTH), F32)
    for part, value in enumerate((stiff.astype(BF16), low.astype(BF16))):
        rows = jnp.dot(pick, value, preferred_element_type=F32).astype(BF16)
        for up in (0, 1):
            here = (s < 36) & (iota((24, DEPTH), 0) == comp * 8 + 4 * up + place) & (fine == bool(part))
            spread = jnp.where(here, 1.0, 0.0).astype(BF16)
            full = full + jnp.where(offset == up, jnp.dot(rows, spread, preferred_element_type=F32), 0.0)
    w[...] = full.astype(BF16)


def roll(v, by):
    return pltpu.roll(v, by % 128, 1) if by % 128 else v


def lanes(rows):
    return lax.broadcasted_iota(jnp.int32, (rows, 128), 1)


def halves(v):
    high = v.astype(BF16).astype(F32)
    return high, v - high


def spread_halves(here, by):
    high, _ = here
    both = jnp.concatenate(here, 0).astype(BF16)
    rolled = roll(both, by)
    rolled_high = rolled.astype(F32)[0:GROUP]
    return both, rolled, jnp.concatenate([high, rolled_high], 0).astype(BF16)


def put(x, t, v):
    for k, part in enumerate(spread_halves(halves(v), 127)):
        x[t, 80 * k:80 * k + 80] = part


def put_seam(xs, n, side, v):
    high, low = halves(v)
    both = jnp.concatenate([high, low], 0).astype(BF16)
    at = 0
    for pair in ((0, 127), (120, 119)):
        two = [roll(both, by) for by in pair]
        third = jnp.concatenate([x.astype(F32)[0:GROUP] for x in two], 0).astype(BF16)
        for part in two + [third]:
            xs[n, at:at + 80, 128 * side:128 * side + 128] = part
            at += 80


def prepare(at, tile, fac, fup, srep, load):
    layer = lax.broadcasted_iota(jnp.int32, (12, 128), 0).astype(F32)
    d = tile[D:D + 12]
    f = jnp.where(d > 0.0, EMIN + (1.0 - EMIN) * (d * d * d), 0.0)
    s = tile[S:S + 12]
    zeros = lambda n: jnp.zeros((n, 128), F32)
    fac[at, 36:40] = zeros(4)
    fup[at, 36:40] = zeros(4)
    srep[at, 36:40] = zeros(4)
    load[at, 0:24] = zeros(24)
    load[at, 24:36] = jnp.where(tile[LOAD + 1:LOAD + 2] == layer, tile[LOAD:LOAD + 1], 0.0)
    load[at, 36:40] = zeros(4)
    for c in (0, 12, 24):
        fac[at, c:c + 12] = f
        fup[at, c:c + 1] = zeros(1)
        fup[at, c + 1:c + 12] = f[0:11]
        srep[at, c:c + 12] = s


def weigh(f, above, below):
    return [
        above * f[(2 * k) * GROUP:(2 * k + 1) * GROUP] + below * f[(2 * k + 1) * GROUP:(2 * k + 2) * GROUP]
        for k in range(4)
    ]


def pairs_of(w, jobs, post):
    pending = []
    for at in range(0, len(jobs), 2):
        two = jobs[at:at + 2]
        wide = [jnp.concatenate([x, y], 0) for _, x, y in two]
        wide = wide[0] if len(wide) == 1 else jnp.concatenate(wide, 1)
        f = jnp.dot(w[...], wide, preferred_element_type=F32)
        for job in pending:
            post(*job)
        pending = [(key, f[:, 128 * k:128 * k + 128]) for k, (key, _, _) in enumerate(two)]
    for job in pending:
        post(*job)


def seam_planes(es, e, near, corner, side, g, start, stop):
    lane = lanes(stop - start)
    row = ((lane + 1) & 127) >> 3
    late = ((lane + 1) & 7) >= 4
    inner, low, high = (row >= 3) & (row <= 10), row < 3, (row > 10) & (row < 14)
    by = 24 - 64 * (g >> 1) - 4 * (g & 1)
    planes = slice(FOLD * g + start, FOLD * g + stop)
    half = FOLD // 2

    def unfold(ref, first, second):
        parts = []
        if start < half:
            parts.append(roll(ref[start:min(stop, half)], by + first))
        if stop > half:
            parts.append(roll(ref[max(start, half) - half:stop - half], by + second))
        return parts[0] if len(parts) == 1 else jnp.concatenate(parts, 0)

    ghost = es[side, planes]
    for t in (0, 1, 2, 11, 12, 13):
        ghost = jnp.where(row == t, roll(e[t, planes], 8 * t + 3), ghost)
    below = unfold(corner.at[2 * side], 64, 96)
    above = unfold(corner.at[2 * side + 1], 64, 32)
    far = jnp.where(inner, roll(near[side, start:stop], by), jnp.where(low, below, jnp.where(high, above, 0.0)))
    return jnp.where(late, ghost, far) if side == 0 else jnp.where(late, far, ghost)


class Split:
    def __init__(self, ref, other, places):
        self.ref, self.other, self.places = ref, other, places

    def __getitem__(self, t):
        return self.other[self.places[t]] if t in self.places else self.ref[t]


class Maps:
    def __init__(self, w, xs, fac, fup, srep, load, acc):
        self.w, self.xs, self.fac, self.fup, self.srep, self.load, self.acc = w, xs, fac, fup, srep, load, acc
        lane = lanes(GROUP)
        self.edge = (lane == 0) | (lane == 127)
        self.from_left = ((lane + 1) & 7) >= 4

    def collect(self, t, f, corners, so_far):
        for dz in (0, 1):
            total = None if so_far is None else so_far[dz][t]
            for k in range(4):
                term = f[(2 * k + dz) * GROUP:(2 * k + dz + 1) * GROUP] * corners[k]
                total = term if total is None else total + term
            self.acc[dz][t] = total

    def seam(self, n, finish, state=None, so_far=None):
        f = jnp.dot(self.w[...], self.xs[n], preferred_element_type=F32)
        outs = []
        for side in (0, 1):
            t = LEFT + side
            part = f[:, 128 * side:128 * side + 128]
            if state is not None and side == 1:
                v = state(t)
                self.collect(t, part, [roll(v, by) for by in (0, 127, 120, 119)], so_far)
            g = weigh(part, self.fac[t], self.fup[t])
            outs.append(g[0] + roll(g[1], 1) + roll(g[2], 8) + roll(g[3], 9))
            if finish is not None:
                finish(side, outs[-1])
        return jnp.where(self.from_left, outs[0], outs[1])

    def fixed(self, t, out, seam):
        return jnp.where(self.edge, roll(seam, 125 - 8 * t), out)

    def main(self, x, elements, seam, finish, state=None, so_far=None, done=None):
        carry = None

        def node(t, above, below):
            out = above[0] + below[0] + roll(above[1] + below[1], 1)
            finish(t, self.fixed(t, out, seam))

        def post(t, f):
            nonlocal carry
            if state is not None and t in OWN:
                now, rolled = state
                self.collect(t, f, [now(t), rolled(t), now(t + 1), rolled(t + 1)], so_far)
            g = weigh(f, self.fac[t], self.fup[t])
            if done is not None and t == 10:
                node(t, g[0:2], (done[1][2], done[1][3]))
            elif carry is not None:
                node(t, g[0:2], carry)
            carry = g[2:]
            if done is not None and t == 2:
                node(3, (done[1][0], done[1][1]), carry)
                for k in range(6):
                    finish(k + 4, self.fixed(k + 4, done[0][k], seam))

        pairs_of(self.w, [(t, x[t], x[t + 1]) for t in elements], post)

    def step_u(self, t, now, before, out):
        s = self.srep[t]
        return jnp.where(s > 0.0, 2.0 * now(t) - before(t) + s * (self.load[t] - out), 0.0)

    def step_a(self, t, now, before, out):
        return 2.0 * now(t) - before(t) + self.load[t] - out


def of(ref):
    return lambda t: ref[t]


def exchange_kernel(*refs):
    sources, refs = refs[:10], refs[10:]
    e, w, mine, near, corner, es, fac, fup, srep, load, u0r, u1, u1r, u2, u2r, acc0, acc1, xz3, o3, p3 = refs[:20]
    held, (corner_out, xu0, xu1, o1, p1, f3, xs, load_sem, send_sem, recv_sem) = refs[20:30], refs[30:]
    u, b, a, q, den, step, fix, top, depth, stiff = held
    gx, gy = lax.axis_index("gx"), lax.axis_index("gy")
    nx, ny = lax.axis_size("gx"), lax.axis_size("gy")
    down, up, left, right = gx > 0, gx < nx - 1, gy > 0, gy < ny - 1
    sides = {
        (-1, 0): down, (1, 0): up, (0, -1): left, (0, 1): right,
        (-1, -1): down & left, (1, -1): up & left, (-1, 1): down & right, (1, 1): up & right,
    }
    barrier = pltpu.get_barrier_semaphore()
    for (dx, dy), there in sides.items():
        @pl.when(there)
        def _(dx=dx, dy=dy):
            pl.semaphore_signal(barrier, inc=1, device_id=(gx + dx, gy + dy), device_id_type=MESH)

    loads = [pltpu.make_async_copy(src, dst, load_sem.at[k]) for k, (src, dst) in enumerate(zip(sources, held))]
    for c in loads:
        c.start()
    zeros = lambda n: jnp.zeros((n, 128), F32)
    empty = {0: ((0, 32), (48, 80), (136, PLANES)), 1: ((48, 80), (184, PLANES)), 13: ((48, 96), (136, PLANES))}
    for t in (0, 1, 2, 11, 12, 13):
        for start, stop in empty.get(t, ((184, PLANES),)):
            e[t, start:stop] = zeros(stop - start)

    @pl.when(jnp.logical_not(down))
    def _():
        for t in (0, 1, 2):
            e[t] = zeros(PLANES)

    @pl.when(jnp.logical_not(up))
    def _():
        for t in (11, 12, 13):
            e[t] = zeros(PLANES)

    for k, dy in enumerate((-1, 1)):
        @pl.when(jnp.logical_not(sides[0, dy]))
        def _(k=k):
            near[k] = zeros(FOLD)

        for j, dx in enumerate((-1, 1)):
            @pl.when(jnp.logical_not(sides[dx, dy]))
            def _(k=k, j=j):
                corner[2 * k + j] = zeros(FOLD // 2)

    for c in loads:
        c.wait()
    for r in range(ROWS):
        t = r + 3
        free = 1.0 - fix[pl.ds(r, 12, stride=8), :].astype(F32)
        e[t, U:U + 36] = u[pl.ds(r, 36, stride=8), :]
        e[t, S:S + 12] = free * step[pl.ds(r, 12, stride=8), :]
        e[t, B:B + 36] = b[pl.ds(r, 36, stride=8), :]
        e[t, D:D + 11] = den[pl.ds(r, 11, stride=8), :]
        e[t, D + 11:D + 12] = zeros(1)
        e[t, A:A + 36] = a[pl.ds(r, 36, stride=8), :]
        e[t, A + 36:A + 40] = zeros(4)
        e[t, LOAD:LOAD + 1] = top[r:r + 1, :]
        e[t, LOAD + 1:LOAD + 2] = depth[r:r + 1, :].astype(F32)
        e[t, LOAD + 2:LOAD + 8] = zeros(6)
        e[t, Q:Q + 36] = q[pl.ds(r, 36, stride=8), :]
        e[t, Q + 36:PLANES] = zeros(PLANES - Q - 36)

    lane = lanes(FOLD)
    first_cols, last_cols = zeros(FOLD), zeros(FOLD)
    for g in range(4):
        for r in range(ROWS):
            slot = 16 * (g >> 1) + 2 * r + (g & 1)
            v = roll(e[r + 3, FOLD * g:FOLD * g + FOLD], 4 * slot + 3)
            first_cols = jnp.where(((lane - 3) & 127) >> 2 == slot, v, first_cols)
            last_cols = jnp.where(((lane + 1) & 127) >> 2 == slot, v, last_cols)
    mine[0] = first_cols
    mine[1] = last_cols
    half = FOLD // 2
    lane = lanes(half)
    for k, cols in enumerate((first_cols, last_cols)):
        low = ((lane - 3 + 4 * k) & 63) < 32
        corner_out[2 * k] = jnp.where(low, cols[0:half], roll(cols[half:FOLD], 32))
        corner_out[2 * k + 1] = jnp.where(low, roll(cols[half:FOLD], -32), cols[0:half])

    pl.semaphore_wait(barrier, sum(there.astype(jnp.int32) for there in sides.values()))

    def rows(to, start, stop, first, last):
        if to == 1:
            src, dst = e.at[11 - last:11 - first, start:stop], e.at[3 - last:3 - first, start:stop]
        else:
            src, dst = e.at[3 + first:3 + last, start:stop], e.at[11 + first:11 + last, start:stop]
        return ((to, 0), src, dst)

    early = [
        ((-1, -1), corner_out.at[0], corner.at[3]),
        ((1, -1), corner_out.at[1], corner.at[2]),
        ((-1, 1), corner_out.at[2], corner.at[1]),
        ((1, 1), corner_out.at[3], corner.at[0]),
        ((0, -1), mine.at[0], near.at[1]),
        ((0, 1), mine.at[1], near.at[0]),
        rows(-1, 0, 96, 0, 2),
        rows(1, 0, 48, 0, 2),
        rows(1, 80, 96, 0, 3),
        rows(1, 32, 48, 2, 3),
        rows(1, 48, 80, 0, 1),
        rows(-1, 0, 48, 2, 3),
        rows(-1, 136, 144, 0, 2),
        rows(1, 136, 144, 0, 2),
    ]
    later = [
        rows(-1, 96, 136, 0, 3),
        rows(1, 96, 136, 0, 3),
        rows(-1, 144, 184, 0, 2),
        rows(1, 144, 184, 0, 2),
    ]
    copies = []
    for k, (to, src, dst) in enumerate(early + later):
        copies.append((to, pltpu.make_async_remote_copy(
            src_ref=src, dst_ref=dst, send_sem=send_sem.at[k], recv_sem=recv_sem.at[k],
            device_id=(gx + to[0], gy + to[1]), device_id_type=MESH,
        )))
    for to, c in copies:
        @pl.when(sides[to])
        def _(c=c):
            c.start()

    def arrived(some):
        for (dx, dy), c in some:
            @pl.when(sides[-dx, -dy])
            def _(c=c):
                c.wait_recv()

    banded_weights(stiff[...], w)
    arrays = (fac, fup, srep, load)
    for t in OWN:
        prepare(t, e.at[t], *arrays)
        now = e[t, U:U + GROUP]
        u0r[t] = roll(now, 127)
        put(xu0, t, now)
        put(xz3, t - 3, srep[t] * e[t, A:A + GROUP])
    lane = lanes(FOLD)
    inner = (((lane + 1) & 127) >> 3 >= 3) & (((lane + 1) & 127) >> 3 <= 10)
    late = ((lane + 1) & 7) >= 4
    for g in range(4):
        by = 24 - 64 * (g >> 1) - 4 * (g & 1)
        for side in (0, 1):
            es[side, FOLD * g:FOLD * g + FOLD] = jnp.where(inner & (late == (side == 0)), roll(mine[side], by), 0.0)

    carry = {}

    def post(key, f):
        kind, t = key
        out, pieces = ((o1, p1), (o3, p3))[kind]
        if kind:
            f3[t - 3] = f
        g = weigh(f, fac[t], fup[t])
        if t == 3:
            pieces[0], pieces[1] = g[0], g[1]
        else:
            out[t - 4] = g[0] + carry[kind][0] + roll(g[1] + carry[kind][1], 1)
        if t == 9:
            pieces[2], pieces[3] = g[2], g[3]
        carry[kind] = g[2:]

    jobs = [((0, t), xu0[t], xu0[t + 1]) for t in range(3, 10)] + [((1, t), xz3[t - 3], xz3[t - 2]) for t in range(3, 10)]
    pairs_of(w, jobs, post)

    arrived(copies[:len(early)])
    maps = Maps(w, xs, fac, fup, srep, load, (acc0, acc1))

    def tile_rows(at):
        return lambda t: es[t - LEFT, at:at + GROUP] if t >= LEFT else e[t, at:at + GROUP]

    u_now, u_before = tile_rows(U), tile_rows(B)
    for side in (0, 1):
        for g, start, stop in ((0, 0, 48), (1, 0, 48), (2, 40, 48)):
            es[side, FOLD * g + start:FOLD * g + stop] = seam_planes(es, e, near, corner, side, g, start, stop)
        prepare(LEFT + side, es.at[side], *arrays)
        put_seam(xs, 0, side, u_now(LEFT + side))

    def seam_u1(side, out):
        v = maps.step_u(LEFT + side, u_now, u_before, out)
        u1[LEFT + side] = v
        put_seam(xs, 1, side, v)

    def seam_u2(side, out):
        u2[LEFT + side] = maps.step_u(LEFT + side, of(u1), u_now, out)

    def main_u1(t, out):
        v = maps.step_u(t, u_now, u_before, out)
        u1[t] = v
        if 3 <= t <= 11:
            u1r[t] = roll(v, 127)
        put(xu1, t, v)

    def main_u2(t, out):
        v = maps.step_u(t, of(u1), u_now, out)
        u2[t] = v
        u2r[t] = roll(v, 127)

    for t in (1, 2, 11, 12):
        prepare(t, e.at[t], *arrays)
    u0r[11] = roll(u_now(11), 127)
    for t in (1, 2, 11, 12, 13):
        put(xu0, t, u_now(t))
    k1 = maps.seam(0, seam_u1)
    k2 = maps.seam(1, seam_u2)
    maps.main(xu0, (1, 2, 10, 11, 12), k1, main_u1, done=(o1, p1))
    maps.main(xu1, range(2, 12), k2, main_u2)
    for t in range(3, 10):
        maps.collect(t, f3[t - 3], [u2[t], u2r[t], u2[t + 1], u2r[t + 1]], None)

    arrived(copies[len(early):])
    for to, c in copies:
        @pl.when(sides[to])
        def _(c=c):
            c.wait_send()


def plate_kernel(*refs):
    e, w, mine, near, corner, es, fac_in, fup_in, srep_in, load_in, u0r, u1, u1r, u2, u2r, acc0_in, acc1_in, xz3_in, o3, p3 = refs[:20]
    first_out, second_out, sens_out = refs[20:23]
    fac_more, fup_more, srep_more, load_more, xz3, acc0, acc1, a2, a1, xz2, xz1, xs, ea, first, second, sens, out_sem = refs[23:]
    ends = {0: 0, 13: 1}
    fac, fup, srep, load = (
        Split(x, y, ends) for x, y in ((fac_in, fac_more), (fup_in, fup_more), (srep_in, srep_more), (load_in, load_more))
    )
    xz = Split(xz3, xz3_in, {t: t - 3 for t in OWN})
    maps = Maps(w, xs, fac, fup, srep, load, (acc0, acc1))
    before = Split(acc0, acc0_in, {t: t for t in range(3, 10)}), Split(acc1, acc1_in, {t: t for t in range(3, 10)})

    def tile_rows(at, seams):
        return lambda t: seams[t - LEFT, at:at + GROUP] if t >= LEFT else e[t, at:at + GROUP]

    u_now, adj_next, adj_later = tile_rows(U, es), tile_rows(A, ea), tile_rows(Q, ea)
    for side in (0, 1):
        for g in (2, 3):
            ea[side, FOLD * g:FOLD * g + 40] = seam_planes(es, e, near, corner, side, g, 0, 40)
        put_seam(xs, 0, side, srep[LEFT + side] * adj_next(LEFT + side))

    def seam_a2(side, out):
        v = maps.step_a(LEFT + side, adj_next, adj_later, out)
        a2[LEFT + side] = v
        put_seam(xs, 1, side, srep[LEFT + side] * v)

    def seam_a1(side, out):
        v = maps.step_a(LEFT + side, of(a2), adj_next, out)
        put_seam(xs, 2, side, srep[LEFT + side] * v)

    def main_a2(t, out):
        v = maps.step_a(t, adj_next, adj_later, out)
        a2[t] = v
        put(xz2, t, srep[t] * v)

    def main_a1(t, out):
        v = maps.step_a(t, of(a2), adj_next, out)
        a1[t] = v
        put(xz1, t, srep[t] * v)
        if t in OWN:
            second[pl.ds(t - 3, 36, stride=8), :] = v[0:36]

    def main_a0(t, out):
        first[pl.ds(t - 3, 36, stride=8), :] = maps.step_a(t, of(a1), of(a2), out)[0:36]

    for t, at in ends.items():
        prepare(at, e.at[t], fac_more, fup_more, srep_more, load_more)
    for t in (0, 1, 2, 11, 12, 13):
        put(xz3, t, srep[t] * adj_next(t))
    k3 = maps.seam(0, seam_a2, of(u2))
    k4 = maps.seam(1, seam_a1, of(u1), (acc0, acc1))
    k5 = maps.seam(2, None, u_now, (acc0, acc1))
    maps.main(xz, (0, 1, 2, 10, 11, 12), k3, main_a2, (of(u2), of(u2r)), None, done=(o3, p3))
    maps.main(xz2, range(1, 12), k4, main_a1, (of(u1), of(u1r)), before)
    copy_second = pltpu.make_async_copy(second, second_out, out_sem.at[1])
    copy_second.start()
    maps.main(xz1, range(2, 11), k5, main_a0, (u_now, of(u0r)), (acc0, acc1))
    copy_first = pltpu.make_async_copy(first, first_out, out_sem.at[0])
    copy_first.start()

    def total(t):
        return sum(acc0[t, c:c + 11] + acc1[t, c + 1:c + 12] for c in (0, 12, 24))

    seam = total(RIGHT)
    last = lanes(11) == 127
    for r in range(ROWS):
        t = r + 3
        d = e[t, D:D + 11]
        both = jnp.where(last, roll(seam, 125 - 8 * t), total(t))
        sens[pl.ds(r, 11, stride=8), :] = (-3.0 * (1.0 - EMIN)) * (d * d) * both
    copy_sens = pltpu.make_async_copy(sens, sens_out, out_sem.at[2])
    copy_sens.start()
    copy_second.wait()
    copy_first.wait()
    copy_sens.wait()


def local(u_now, u_prev, adjoint_next, adjoint_later, density, step_factor, fixed_nodes, load_top, load_depth, brick_stiffness):
    vmem = pl.BlockSpec(memory_space=pltpu.VMEM)
    hbm = pl.BlockSpec(memory_space=pltpu.HBM)
    flat = lambda x: x.reshape(-1, 128)
    sources = (
        flat(u_now), flat(u_prev), flat(adjoint_next), flat(adjoint_later), flat(density), flat(step_factor),
        flat(fixed_nodes), load_top, load_depth, brick_stiffness,
    )
    f32 = lambda *shape: jax.ShapeDtypeStruct(shape + (128,), F32)
    bf16 = lambda *shape: jax.ShapeDtypeStruct(shape, BF16)
    passed = (
        [f32(MAIN, PLANES), bf16(OUT, DEPTH), f32(2, FOLD), f32(2, FOLD), f32(4, FOLD // 2), f32(2, PLANES)]
        + [f32(TILES, GROUP)] * 11 + [bf16(ROWS, WIDE, 128), f32(6, GROUP), f32(4, GROUP)]
    )
    tiles = lambda n, rows, kind: pltpu.VMEM((n, rows, 128), kind)
    gathered = pl.pallas_call(
        exchange_kernel,
        out_shape=passed,
        in_specs=[hbm] * 10,
        out_specs=[vmem] * len(passed),
        scratch_shapes=[pltpu.VMEM(x.shape, x.dtype) for x in sources] + [
            tiles(4, FOLD // 2, F32),
            tiles(MAIN, WIDE, BF16),
            tiles(MAIN, WIDE, BF16),
            tiles(6, GROUP, F32),
            tiles(4, GROUP, F32),
            tiles(7, OUT, F32),
            pltpu.VMEM((2, DEPTH, 256), BF16),
            pltpu.SemaphoreType.DMA((10,)),
            pltpu.SemaphoreType.DMA((18,)),
            pltpu.SemaphoreType.DMA((18,)),
        ],
        compiler_params=pltpu.CompilerParams(collective_id=0, has_side_effects=True, vmem_limit_bytes=32 * 2**20),
        name="exchange",
    )(*(pltpu.with_memory_space_constraint(x, pltpu.HBM) for x in sources))
    results = ((36 * ROWS, 128), (36 * ROWS, 128), (11 * ROWS, 128))
    first, second, sens = pl.pallas_call(
        plate_kernel,
        out_shape=tuple(jax.ShapeDtypeStruct(shape, F32) for shape in results),
        in_specs=[vmem] * len(passed),
        out_specs=(hbm,) * 3,
        scratch_shapes=[tiles(2, GROUP, F32)] * 4 + [tiles(MAIN, WIDE, BF16)] + [tiles(TILES, GROUP, F32)] * 4
        + [tiles(MAIN, WIDE, BF16)] * 2 + [pltpu.VMEM((3, DEPTH, 256), BF16), tiles(2, PLANES, F32)]
        + [pltpu.VMEM(shape, F32) for shape in results]
        + [pltpu.SemaphoreType.DMA((3,))],
        compiler_params=pltpu.CompilerParams(vmem_limit_bytes=32 * 2**20),
        name="plate",
    )(*gathered)
    return (
        first.reshape(u_now.shape),
        second.reshape(u_now.shape),
        sens.reshape(density.shape),
    )


def solution(mesh):
    in_specs = (
        P(None, None, "gx", "gy"),
        P(None, None, "gx", "gy"),
        P(None, None, "gx", "gy"),
        P(None, None, "gx", "gy"),
        P(None, "gx", "gy"),
        P(None, "gx", "gy"),
        P(None, "gx", "gy"),
        P("gx", "gy"),
        P("gx", "gy"),
        P(),
    )
    out_specs = (P(None, None, "gx", "gy"), P(None, None, "gx", "gy"), P(None, "gx", "gy"))
    return jax.shard_map(local, mesh=mesh, in_specs=in_specs, out_specs=out_specs, check_vma=False)
```

```python
import jax
import jax.numpy as jnp
from jax import lax
from jax.experimental import pallas as pl
from jax.experimental.pallas import tpu as pltpu
from jax.sharding import PartitionSpec as P

EMIN = 0.001
MESH = pl.DeviceIdType.MESH
F32 = jnp.float32
BF16 = jnp.bfloat16

ROWS = 8
OWN = range(3, 11)
DEEP_1, DEEP_2 = range(3, 10), range(4, 9)
ONCE, TWICE = range(4, 10), range(5, 9)
MAIN = 14
LEFT, RIGHT = 14, 15
TILES = 16
U, S, A, D, B, LOAD, Q, PLANES = 0, 36, 48, 84, 96, 132, 136, 192
FOLD = 48
GROUP = 40
OUT = 8 * GROUP
WIDE = 6 * GROUP
DEPTH = 2 * WIDE


def banded_weights(stiff, w):
    def split(place):
        comp = (place >= 12).astype(jnp.int32) + (place >= 24).astype(jnp.int32)
        return comp, place - 12 * comp

    iota = lambda shape, d: lax.broadcasted_iota(jnp.int32, shape, d)
    group, r = iota((8, GROUP, 24), 0), iota((8, GROUP, 24), 1)
    dz = group & 1
    comp, layer = split(r)
    element = layer - dz
    real = (r < 36) & (element >= 0) & (element <= 10)
    pick = jnp.where(real & (iota((8, GROUP, 24), 2) == comp * 8 + 4 * dz + (group >> 1)), 1.0, 0.0)
    pick = pick.reshape(OUT, 24).astype(BF16)

    def columns(shape):
        q = iota(shape, len(shape) - 1)
        block = sum((q >= GROUP * k).astype(jnp.int32) for k in range(1, 12))
        s = q - GROUP * block
        dx = (block >= 6).astype(jnp.int32)
        block = block - 6 * dx
        dy = ((block == 2) | (block == 3) | (block == 5)).astype(jnp.int32)
        return (2 * dx + dy, block >= 4, s) + split(s)

    place, fine, s, comp, _ = columns((24, DEPTH))
    offset = columns((8, GROUP, DEPTH))[4] - split(iota((8, GROUP, DEPTH), 1))[1] + (iota((8, GROUP, DEPTH), 0) & 1)
    offset = offset.reshape(OUT, DEPTH)
    low = stiff - stiff.astype(BF16).astype(F32)
    full = jnp.zeros((OUT, DEPTH), F32)
    for part, value in enumerate((stiff.astype(BF16), low.astype(BF16))):
        rows = jnp.dot(pick, value, preferred_element_type=F32).astype(BF16)
        for up in (0, 1):
            here = (s < 36) & (iota((24, DEPTH), 0) == comp * 8 + 4 * up + place) & (fine == bool(part))
            spread = jnp.where(here, 1.0, 0.0).astype(BF16)
            full = full + jnp.where(offset == up, jnp.dot(rows, spread, preferred_element_type=F32), 0.0)
    w[...] = full.astype(BF16)


def roll(v, by):
    return pltpu.roll(v, by % 128, 1) if by % 128 else v


def lanes(rows):
    return lax.broadcasted_iota(jnp.int32, (rows, 128), 1)


def halves(v):
    high = v.astype(BF16).astype(F32)
    return high, v - high


def spread_halves(here, by):
    high, _ = here
    both = jnp.concatenate(here, 0).astype(BF16)
    rolled = roll(both, by)
    rolled_high = rolled.astype(F32)[0:GROUP]
    return both, rolled, jnp.concatenate([high, rolled_high], 0).astype(BF16)


def put(x, t, v):
    for k, part in enumerate(spread_halves(halves(v), 127)):
        x[t, 80 * k:80 * k + 80] = part


def put_seam(xs, n, side, v):
    high, low = halves(v)
    both = jnp.concatenate([high, low], 0).astype(BF16)
    at = 0
    for pair in ((0, 127), (120, 119)):
        two = [roll(both, by) for by in pair]
        third = jnp.concatenate([x.astype(F32)[0:GROUP] for x in two], 0).astype(BF16)
        for part in two + [third]:
            xs[n, at:at + 80, 128 * side:128 * side + 128] = part
            at += 80


def prepare(at, tile, fac, fup, srep, load):
    layer = lax.broadcasted_iota(jnp.int32, (12, 128), 0).astype(F32)
    d = tile[D:D + 12]
    f = jnp.where(d > 0.0, EMIN + (1.0 - EMIN) * (d * d * d), 0.0)
    s = tile[S:S + 12]
    zeros = lambda n: jnp.zeros((n, 128), F32)
    fac[at, 36:40] = zeros(4)
    fup[at, 36:40] = zeros(4)
    srep[at, 36:40] = zeros(4)
    load[at, 0:24] = zeros(24)
    load[at, 24:36] = jnp.where(tile[LOAD + 1:LOAD + 2] == layer, tile[LOAD:LOAD + 1], 0.0)
    load[at, 36:40] = zeros(4)
    for c in (0, 12, 24):
        fac[at, c:c + 12] = f
        fup[at, c:c + 1] = zeros(1)
        fup[at, c + 1:c + 12] = f[0:11]
        srep[at, c:c + 12] = s


def weigh(f, above, below):
    return [
        above * f[(2 * k) * GROUP:(2 * k + 1) * GROUP] + below * f[(2 * k + 1) * GROUP:(2 * k + 2) * GROUP]
        for k in range(4)
    ]


def pairs_of(w, jobs, post):
    pending = []
    for at in range(0, len(jobs), 2):
        two = jobs[at:at + 2]
        wide = [jnp.concatenate([x, y], 0) for _, x, y in two]
        wide = wide[0] if len(wide) == 1 else jnp.concatenate(wide, 1)
        f = jnp.dot(w[...], wide, preferred_element_type=F32)
        for job in pending:
            post(*job)
        pending = [(key, f[:, 128 * k:128 * k + 128]) for k, (key, _, _) in enumerate(two)]
    for job in pending:
        post(*job)


def seam_planes(es, e, near, corner, side, g, start, stop):
    lane = lanes(stop - start)
    row = ((lane + 1) & 127) >> 3
    late = ((lane + 1) & 7) >= 4
    inner, low, high = (row >= 3) & (row <= 10), row < 3, (row > 10) & (row < 14)
    by = 24 - 64 * (g >> 1) - 4 * (g & 1)
    planes = slice(FOLD * g + start, FOLD * g + stop)
    half = FOLD // 2

    def unfold(ref, first, second):
        parts = []
        if start < half:
            parts.append(roll(ref[start:min(stop, half)], by + first))
        if stop > half:
            parts.append(roll(ref[max(start, half) - half:stop - half], by + second))
        return parts[0] if len(parts) == 1 else jnp.concatenate(parts, 0)

    ghost = es[side, planes]
    for t in (0, 1, 2, 11, 12, 13):
        ghost = jnp.where(row == t, roll(e[t, planes], 8 * t + 3), ghost)
    below = unfold(corner.at[2 * side], 64, 96)
    above = unfold(corner.at[2 * side + 1], 64, 32)
    far = jnp.where(inner, roll(near[side, start:stop], by), jnp.where(low, below, jnp.where(high, above, 0.0)))
    return jnp.where(late, ghost, far) if side == 0 else jnp.where(late, far, ghost)


class Tiles:
    def __init__(self, own, ref, more):
        self.own, self.ref, self.more = own, ref, more

    def __getitem__(self, t):
        return self.ref[t] if t in self.own else self.more[t]

    def __setitem__(self, t, v):
        self.more[t] = v


class Fresh:
    def __init__(self, own, ref):
        self.own, self.ref = own, ref

    def __getitem__(self, t):
        return self.ref[t] if t in self.own else None


class Field:
    def __init__(self, tile, at):
        self.tile, self.at = tile, at

    def __getitem__(self, t):
        return self.tile(t, self.at)


class Maps:
    def __init__(self, w, fac, fup, srep, load, acc):
        self.w, self.fac, self.fup, self.srep, self.load, self.acc = w, fac, fup, srep, load, acc

    def collect(self, t, f, corners, so_far):
        for dz in (0, 1):
            total = None if so_far is None else so_far[dz][t]
            for k in range(4):
                term = f[(2 * k + dz) * GROUP:(2 * k + dz + 1) * GROUP] * corners[k]
                total = term if total is None else total + term
            self.acc[dz][t] = total

    def seam_corners(self, v):
        return [roll(v, by) for by in (0, 127, 120, 119)]

    def seam(self, x, finish, state=None, so_far=None, forces=None):
        f = jnp.dot(self.w[...], x[...], preferred_element_type=F32)
        for side in (0, 1):
            t = LEFT + side
            part = f[:, 128 * side:128 * side + 128]
            if forces is not None:
                forces(t, part)
            if state is not None:
                v = state(t)
                self.collect(t, part, self.seam_corners(v), so_far)
            g = weigh(part, self.fac[t], self.fup[t])
            finish(t, g[0] + roll(g[1], 1) + roll(g[2], 8) + roll(g[3], 9))

    def main(self, x, elements, finish, state=None, so_far=None, pieces=None, keep=None, forces=None):
        carry = None
        first, last, ends = pieces if pieces is not None else (None, None, None)

        def node(t, above, below):
            finish(t, above[0] + below[0] + roll(above[1] + below[1], 1))

        def post(t, f):
            nonlocal carry
            if forces is not None:
                forces(t, f)
            if state is not None and t in OWN:
                now, rolled = state
                self.collect(t, f, [now[t], rolled[t], now[t + 1], rolled[t + 1]], so_far)
            g = weigh(f, self.fac[t], self.fup[t])
            if keep is not None and t == elements[0]:
                keep[0], keep[1] = g[0], g[1]
            if ends is not None and t == last + 1:
                node(t, g[0:2], (ends[2], ends[3]))
            elif carry is not None:
                node(t, g[0:2], carry)
            carry = g[2:]
            if ends is not None and t == first - 1:
                node(first, (ends[0], ends[1]), carry)
            if keep is not None and t == elements[-1]:
                keep[2], keep[3] = g[2], g[3]

        pairs_of(self.w, [(t, x[t], x[t + 1]) for t in elements], post)

    def step_u(self, t, now, before, out):
        s = self.srep[t]
        return jnp.where(s > 0.0, 2.0 * now - before + s * (self.load[t] - out), 0.0)

    def step_a(self, t, now, before, out):
        return 2.0 * now - before + self.load[t] - out


def exchange_kernel(*refs):
    sources, refs = refs[:10], refs[10:]
    e, w, near, corner, es, fac, fup, srep, load, u0r, u1, u1r, u2, a2, a1, acc0, acc1 = refs[:17]
    xu0, xz3, xu1, xz2, p1, p2, p3, p4, f3 = refs[17:26]
    held, (mine, corner_out, load_sem, send_sem, recv_sem) = refs[26:36], refs[36:]
    u, b, a, q, den, step, fix, top, depth, stiff = held
    gx, gy = lax.axis_index("gx"), lax.axis_index("gy")
    nx, ny = lax.axis_size("gx"), lax.axis_size("gy")
    down, up, left, right = gx > 0, gx < nx - 1, gy > 0, gy < ny - 1
    sides = {
        (-1, 0): down, (1, 0): up, (0, -1): left, (0, 1): right,
        (-1, -1): down & left, (1, -1): up & left, (-1, 1): down & right, (1, 1): up & right,
    }
    barrier = pltpu.get_barrier_semaphore()
    for (dx, dy), there in sides.items():
        @pl.when(there)
        def _(dx=dx, dy=dy):
            pl.semaphore_signal(barrier, inc=1, device_id=(gx + dx, gy + dy), device_id_type=MESH)

    loads = [pltpu.make_async_copy(src, dst, load_sem.at[k]) for k, (src, dst) in enumerate(zip(sources, held))]
    for c in loads:
        c.start()
    zeros = lambda n: jnp.zeros((n, 128), F32)
    e[0, 0:32] = zeros(32)
    e[0, 96:PLANES] = zeros(PLANES - 96)
    e[1, 96:128] = zeros(32)
    for t in (1, 2, 11, 12):
        e[t, 176:PLANES] = zeros(PLANES - 176)
    e[13, 88:PLANES] = zeros(PLANES - 88)

    @pl.when(jnp.logical_not(down))
    def _():
        for t in (0, 1, 2):
            e[t] = zeros(PLANES)

    @pl.when(jnp.logical_not(up))
    def _():
        for t in (11, 12, 13):
            e[t] = zeros(PLANES)

    for k, dy in enumerate((-1, 1)):
        @pl.when(jnp.logical_not(sides[0, dy]))
        def _(k=k):
            near[k] = zeros(FOLD)

        for j, dx in enumerate((-1, 1)):
            @pl.when(jnp.logical_not(sides[dx, dy]))
            def _(k=k, j=j):
                corner[2 * k + j] = zeros(FOLD // 2)

    for c in loads:
        c.wait()
    for r in range(ROWS):
        t = r + 3
        free = 1.0 - fix[pl.ds(r, 12, stride=8), :].astype(F32)
        e[t, U:U + 36] = u[pl.ds(r, 36, stride=8), :]
        e[t, S:S + 12] = free * step[pl.ds(r, 12, stride=8), :]
        e[t, A:A + 36] = a[pl.ds(r, 36, stride=8), :]
        e[t, D:D + 11] = den[pl.ds(r, 11, stride=8), :]
        e[t, D + 11:D + 12] = zeros(1)
        e[t, B:B + 36] = b[pl.ds(r, 36, stride=8), :]
        e[t, LOAD:LOAD + 1] = top[r:r + 1, :]
        e[t, LOAD + 1:LOAD + 2] = depth[r:r + 1, :].astype(F32)
        e[t, LOAD + 2:LOAD + 4] = zeros(2)
        e[t, Q:Q + 36] = q[pl.ds(r, 36, stride=8), :]
        e[t, Q + 36:PLANES] = zeros(PLANES - Q - 36)

    lane = lanes(FOLD)
    first_cols, last_cols = zeros(FOLD), zeros(FOLD)
    for g in range(4):
        for r in range(ROWS):
            slot = 16 * (g >> 1) + 2 * r + (g & 1)
            v = roll(e[r + 3, FOLD * g:FOLD * g + FOLD], 4 * slot + 3)
            first_cols = jnp.where(((lane - 3) & 127) >> 2 == slot, v, first_cols)
            last_cols = jnp.where(((lane + 1) & 127) >> 2 == slot, v, last_cols)
    mine[0] = first_cols
    mine[1] = last_cols
    half = FOLD // 2
    lane = lanes(half)
    for k, cols in enumerate((first_cols, last_cols)):
        low = ((lane - 3 + 4 * k) & 63) < 32
        corner_out[2 * k] = jnp.where(low, cols[0:half], roll(cols[half:FOLD], 32))
        corner_out[2 * k + 1] = jnp.where(low, roll(cols[half:FOLD], -32), cols[0:half])

    pl.semaphore_wait(barrier, sum(there.astype(jnp.int32) for there in sides.values()))
    plan = [
        ((-1, -1), corner_out.at[0], corner.at[3]),
        ((1, -1), corner_out.at[1], corner.at[2]),
        ((-1, 1), corner_out.at[2], corner.at[1]),
        ((1, 1), corner_out.at[3], corner.at[0]),
        ((0, -1), mine.at[0], near.at[1]),
        ((0, 1), mine.at[1], near.at[0]),
        ((-1, 0), e.at[3:5, 0:176], e.at[11:13, 0:176]),
        ((1, 0), e.at[9:11, 0:96], e.at[1:3, 0:96]),
        ((1, 0), e.at[9:11, 128:176], e.at[1:3, 128:176]),
        ((-1, 0), e.at[5, 0:88], e.at[13, 0:88]),
        ((1, 0), e.at[8, 32:96], e.at[0, 32:96]),
        ((1, 0), e.at[10, 96:128], e.at[2, 96:128]),
    ]
    copies = []
    for k, ((dx, dy), src, dst) in enumerate(plan):
        copies.append(((dx, dy), pltpu.make_async_remote_copy(
            src_ref=src, dst_ref=dst, send_sem=send_sem.at[k], recv_sem=recv_sem.at[k],
            device_id=(gx + dx, gy + dy), device_id_type=MESH,
        )))
    for to, c in copies:
        @pl.when(sides[to])
        def _(c=c):
            c.start()

    banded_weights(stiff[...], w)
    for t in OWN:
        prepare(t, e.at[t], fac, fup, srep, load)
        now = e[t, U:U + GROUP]
        u0r[t] = roll(now, 127)
        put(xu0, t, now)
        put(xz3, t, srep[t] * e[t, A:A + GROUP])
    maps = Maps(w, fac, fup, srep, load, (acc0, acc1))

    def main_u1(t, out):
        v = maps.step_u(t, e[t, U:U + GROUP], e[t, B:B + GROUP], out)
        u1[t] = v
        u1r[t] = roll(v, 127)
        put(xu1, t, v)

    def main_a2(t, out):
        v = maps.step_a(t, e[t, A:A + GROUP], e[t, Q:Q + GROUP], out)
        a2[t] = v
        put(xz2, t, srep[t] * v)

    def main_u2(t, out):
        u2[t] = maps.step_u(t, u1[t], e[t, U:U + GROUP], out)

    def main_a1(t, out):
        a1[t] = maps.step_a(t, a2[t], e[t, A:A + GROUP], out)

    def keep_forces(t, f):
        f3[t - 3] = f

    maps.main(xu0, DEEP_1, main_u1, keep=p1)
    maps.main(xz3, DEEP_1, main_a2, keep=p3, forces=keep_forces)
    maps.main(xu1, DEEP_2, main_u2, keep=p2)
    maps.main(xz2, DEEP_2, main_a1, (u1, u1r), None, keep=p4)
    lane = lanes(FOLD)
    inner = (((lane + 1) & 127) >> 3 >= 3) & (((lane + 1) & 127) >> 3 <= 10)
    late = ((lane + 1) & 7) >= 4
    for g in range(4):
        by = 24 - 64 * (g >> 1) - 4 * (g & 1)
        for side in (0, 1):
            es[side, FOLD * g:FOLD * g + FOLD] = jnp.where(inner & (late == (side == 0)), roll(mine[side], by), 0.0)

    for (dx, dy), c in copies:
        @pl.when(sides[-dx, -dy])
        def _(c=c):
            c.wait_recv()
    for to, c in copies:
        @pl.when(sides[to])
        def _(c=c):
            c.wait_send()


def plate_kernel(*refs):
    e, w, near, corner, es, fac_in, fup_in, srep_in, load_in, u0r_in, u1_in, u1r_in, u2_in, a2_in, a1_in, acc0_in, acc1_in = refs[:17]
    xu0_in, xz3_in, xu1_in, xz2_in, p1, p2, p3, p4, f3 = refs[17:26]
    first_out, second_out, sens_out = refs[26:29]
    more, (f10, fseam, ea, xs, first, second, sens, out_sem) = refs[29:47], refs[47:]
    fac, fup, srep, load, u0r = (Tiles(OWN, x, y) for x, y in zip((fac_in, fup_in, srep_in, load_in, u0r_in), more))
    u1, u1r, a2 = (Tiles(ONCE, x, y) for x, y in zip((u1_in, u1r_in, a2_in), more[5:]))
    u2, u2r, acc0, acc1, a1 = more[8:13]
    xu0, xz3 = (Tiles(OWN, x, y) for x, y in zip((xu0_in, xz3_in), more[13:]))
    xu1, xz2 = (Tiles(ONCE, x, y) for x, y in zip((xu1_in, xz2_in), more[15:]))
    xz1 = more[17]
    maps = Maps(w, fac, fup, srep, load, (acc0, acc1))
    so_far = Tiles(DEEP_2, acc0_in, acc0), Tiles(DEEP_2, acc1_in, acc1)
    fresh = Fresh(DEEP_2, acc0_in), Fresh(DEEP_2, acc1_in)
    lane = lanes(GROUP)
    from_left = ((lane + 1) & 7) >= 4
    edge = (lane == 0) | (lane == 127)
    edges = (lane <= 1) | (lane >= 126)
    ghosts = (0, 1, 2, 11, 12, 13)
    seams = (LEFT, RIGHT)

    def tile(t, at):
        return ea[t - LEFT, at:at + GROUP] if t >= LEFT else e[t, at:at + GROUP]

    def fixed(t, v, where, ref):
        return jnp.where(where, roll(jnp.where(from_left, ref[LEFT], ref[RIGHT]), 125 - 8 * t), v)

    def value_u1(t, out):
        v = maps.step_u(t, tile(t, U), tile(t, B), out)
        u1[t] = v
        return v

    def value_a2(t, out):
        v = maps.step_a(t, tile(t, A), tile(t, Q), out)
        a2[t] = v
        return v

    def main_u1(t, out):
        v = value_u1(t, out)
        if t in (3, 10, 11):
            u1r[t] = roll(v, 127)
        put(xu1.more, t, v)

    def main_a2(t, out):
        put(xz2.more, t, srep[t] * value_a2(t, out))

    def keep_forces(t, f):
        if t >= LEFT:
            fseam[t - LEFT] = f
        elif t == 10:
            f10[...] = f

    for t in ghosts:
        prepare(t, e.at[t], *more[0:4])
        put(xz3.more, t, srep[t] * tile(t, A))
    maps.main(xz3, (0, 1, 2, 10, 11, 12), main_a2, pieces=(3, 9, p3), forces=keep_forces)
    for side in (0, 1):
        for g in range(4):
            ea[side, FOLD * g:FOLD * g + FOLD] = seam_planes(es, e, near, corner, side, g, 0, FOLD)
        prepare(LEFT + side, ea.at[side], *more[0:4])
        put_seam(xs, 2, side, srep[LEFT + side] * tile(LEFT + side, A))
        put_seam(xs, 0, side, tile(LEFT + side, U))
    maps.seam(xs.at[2], lambda t, out: put_seam(xs, 3, t - LEFT, srep[t] * value_a2(t, out)), forces=keep_forces)
    maps.seam(xs.at[0], lambda t, out: put_seam(xs, 1, t - LEFT, value_u1(t, out)))
    u0r.more[11] = roll(tile(11, U), 127)
    for t in (1, 2, 11, 12, 13):
        put(xu0.more, t, tile(t, U))
    maps.main(xu0, (1, 2, 10, 11, 12), main_u1, pieces=(3, 9, p1))

    def seam_a1(t, out):
        v = maps.step_a(t, a2[t], tile(t, A), out)
        a1[t] = v
        put_seam(xs, 4, t - LEFT, srep[t] * v)

    def seam_u2(t, out):
        u2[t] = maps.step_u(t, u1[t], tile(t, U), out)

    def end_a1(t, v):
        v = fixed(t, v, edges, a1)
        a1[t] = v
        put(xz1, t, srep[t] * v)
        if t in OWN:
            second[pl.ds(t - 3, 36, stride=8), :] = v[0:36]

    def end_u2(t, v):
        v = fixed(t, v, edges, u2)
        u2[t] = v
        u2r[t] = roll(v, 127)

    maps.seam(xs.at[3], seam_a1, lambda t: u1[t], None)
    maps.main(
        xz2, (1, 2, 3, 9, 10, 11), lambda t, out: end_a1(t, maps.step_a(t, a2[t], tile(t, A), out)),
        (u1, u1r), fresh, pieces=(4, 8, p4),
    )
    for t in TWICE:
        end_a1(t, a1_in[t])
    maps.seam(xs.at[1], seam_u2)
    maps.main(xu1, (2, 3, 9, 10, 11), lambda t, out: end_u2(t, maps.step_u(t, u1[t], tile(t, U), out)), pieces=(4, 8, p2))
    for t in TWICE:
        end_u2(t, u2_in[t])

    def seam_a0(t, out):
        a0[t] = maps.step_a(t, a1[t], a2[t], out)

    def main_a0(t, out):
        v = fixed(t, maps.step_a(t, a1[t], a2[t], out), edge, a0)
        first[pl.ds(t - 3, 36, stride=8), :] = v[0:36]

    a0 = {}
    maps.seam(xs.at[4], seam_a0, lambda t: tile(t, U), (acc0, acc1))
    for t in seams:
        maps.collect(t, fseam[t - LEFT], maps.seam_corners(u2[t]), (acc0, acc1))
    maps.main(xz1, range(2, 11), main_a0, (Field(tile, U), u0r), so_far)
    for t in OWN:
        maps.collect(t, f3[t - 3] if t < 10 else f10[...], [u2[t], u2r[t], u2[t + 1], u2r[t + 1]], (acc0, acc1))
    copies = [pltpu.make_async_copy(src, dst, out_sem.at[k]) for k, (src, dst) in enumerate(
        ((first, first_out), (second, second_out), (sens, sens_out)))]
    copies[0].start()
    copies[1].start()

    def total(t):
        return sum(acc0[t, c:c + 11] + acc1[t, c + 1:c + 12] for c in (0, 12, 24))

    lane = lanes(11)
    seam = jnp.where(((lane + 1) & 7) >= 4, total(LEFT), total(RIGHT))
    ends = (lane == 0) | (lane >= 126)
    for r in range(ROWS):
        t = r + 3
        d = e[t, D:D + 11]
        sens[pl.ds(r, 11, stride=8), :] = (-3.0 * (1.0 - EMIN)) * (d * d) * jnp.where(ends, roll(seam, 125 - 8 * t), total(t))
    copies[2].start()
    for c in copies:
        c.wait()


def local(u_now, u_prev, adjoint_next, adjoint_later, density, step_factor, fixed_nodes, load_top, load_depth, brick_stiffness):
    vmem = pl.BlockSpec(memory_space=pltpu.VMEM)
    hbm = pl.BlockSpec(memory_space=pltpu.HBM)
    flat = lambda x: x.reshape(-1, 128)
    sources = (
        flat(u_now), flat(u_prev), flat(adjoint_next), flat(adjoint_later), flat(density), flat(step_factor),
        flat(fixed_nodes), load_top, load_depth, brick_stiffness,
    )
    f32 = lambda *shape: jax.ShapeDtypeStruct(shape + (128,), F32)
    bf16 = lambda *shape: jax.ShapeDtypeStruct(shape, BF16)
    passed = (
        [f32(MAIN, PLANES), bf16(OUT, DEPTH), f32(2, FOLD), f32(4, FOLD // 2), f32(2, PLANES)]
        + [f32(TILES, GROUP)] * 12 + [bf16(MAIN, WIDE, 128)] * 4 + [f32(4, GROUP)] * 4 + [f32(7, OUT)]
    )
    gathered = pl.pallas_call(
        exchange_kernel,
        out_shape=passed,
        in_specs=[hbm] * 10,
        out_specs=[vmem] * len(passed),
        scratch_shapes=[pltpu.VMEM(x.shape, x.dtype) for x in sources] + [
            pltpu.VMEM((2, FOLD, 128), F32),
            pltpu.VMEM((4, FOLD // 2, 128), F32),
            pltpu.SemaphoreType.DMA((10,)),
            pltpu.SemaphoreType.DMA((12,)),
            pltpu.SemaphoreType.DMA((12,)),
        ],
        compiler_params=pltpu.CompilerParams(collective_id=0, has_side_effects=True, vmem_limit_bytes=32 * 2**20),
        name="exchange",
    )(*(pltpu.with_memory_space_constraint(x, pltpu.HBM) for x in sources))
    tiles = lambda n, rows, kind: pltpu.VMEM((n, rows, 128), kind)
    results = ((36 * ROWS, 128), (36 * ROWS, 128), (11 * ROWS, 128))
    first, second, sens = pl.pallas_call(
        plate_kernel,
        out_shape=tuple(jax.ShapeDtypeStruct(shape, F32) for shape in results),
        in_specs=[vmem] * len(passed),
        out_specs=(hbm,) * 3,
        scratch_shapes=[tiles(TILES, GROUP, F32)] * 13 + [tiles(MAIN, WIDE, BF16)] * 5
        + [pltpu.VMEM((OUT, 128), F32), tiles(2, OUT, F32), tiles(2, PLANES, F32), pltpu.VMEM((5, DEPTH, 256), BF16)]
        + [pltpu.VMEM(shape, F32) for shape in results]
        + [pltpu.SemaphoreType.DMA((3,))],
        compiler_params=pltpu.CompilerParams(vmem_limit_bytes=40 * 2**20),
        name="plate",
    )(*gathered)
    return (
        first.reshape(u_now.shape),
        second.reshape(u_now.shape),
        sens.reshape(density.shape),
    )


def solution(mesh):
    in_specs = (
        P(None, None, "gx", "gy"),
        P(None, None, "gx", "gy"),
        P(None, None, "gx", "gy"),
        P(None, None, "gx", "gy"),
        P(None, "gx", "gy"),
        P(None, "gx", "gy"),
        P(None, "gx", "gy"),
        P("gx", "gy"),
        P("gx", "gy"),
        P(),
    )
    out_specs = (P(None, None, "gx", "gy"), P(None, None, "gx", "gy"), P(None, "gx", "gy"))
    return jax.shard_map(local, mesh=mesh, in_specs=in_specs, out_specs=out_specs, check_vma=False)
```

```python
import jax
import jax.numpy as jnp
from jax import lax
from jax.experimental import pallas as pl
from jax.experimental.pallas import tpu as pltpu
from jax.sharding import PartitionSpec as P

EMIN = 0.001
MESH = pl.DeviceIdType.MESH
F32 = jnp.float32
BF16 = jnp.bfloat16

ROWS = 8
OWN = range(3, 11)
DEEP_1, DEEP_2 = range(3, 10), range(4, 9)
ONCE, TWICE = range(4, 10), range(5, 9)
MAIN = 14
LEFT, RIGHT = 14, 15
TILES = 16
U, S, A, D, B, LOAD, Q, PLANES = 0, 36, 48, 84, 96, 132, 136, 192
FOLD = 48
GROUP = 40
OUT = 8 * GROUP
WIDE = 6 * GROUP
DEPTH = 2 * WIDE


def banded_weights(stiff, w):
    def split(place):
        comp = (place >= 12).astype(jnp.int32) + (place >= 24).astype(jnp.int32)
        return comp, place - 12 * comp

    iota = lambda shape, d: lax.broadcasted_iota(jnp.int32, shape, d)
    group, r = iota((8, GROUP, 24), 0), iota((8, GROUP, 24), 1)
    dz = group & 1
    comp, layer = split(r)
    element = layer - dz
    real = (r < 36) & (element >= 0) & (element <= 10)
    pick = jnp.where(real & (iota((8, GROUP, 24), 2) == comp * 8 + 4 * dz + (group >> 1)), 1.0, 0.0)
    pick = pick.reshape(OUT, 24).astype(BF16)

    def columns(shape):
        q = iota(shape, len(shape) - 1)
        block = sum((q >= GROUP * k).astype(jnp.int32) for k in range(1, 12))
        s = q - GROUP * block
        dx = (block >= 6).astype(jnp.int32)
        block = block - 6 * dx
        dy = ((block == 2) | (block == 3) | (block == 5)).astype(jnp.int32)
        return (2 * dx + dy, block >= 4, s) + split(s)

    place, fine, s, comp, _ = columns((24, DEPTH))
    offset = columns((8, GROUP, DEPTH))[4] - split(iota((8, GROUP, DEPTH), 1))[1] + (iota((8, GROUP, DEPTH), 0) & 1)
    offset = offset.reshape(OUT, DEPTH)
    low = stiff - stiff.astype(BF16).astype(F32)
    full = jnp.zeros((OUT, DEPTH), F32)
    for part, value in enumerate((stiff.astype(BF16), low.astype(BF16))):
        rows = jnp.dot(pick, value, preferred_element_type=F32).astype(BF16)
        for up in (0, 1):
            here = (s < 36) & (iota((24, DEPTH), 0) == comp * 8 + 4 * up + place) & (fine == bool(part))
            spread = jnp.where(here, 1.0, 0.0).astype(BF16)
            full = full + jnp.where(offset == up, jnp.dot(rows, spread, preferred_element_type=F32), 0.0)
    w[...] = full.astype(BF16)


def roll(v, by):
    return pltpu.roll(v, by % 128, 1) if by % 128 else v


def lanes(rows):
    return lax.broadcasted_iota(jnp.int32, (rows, 128), 1)


def halves(v):
    high = v.astype(BF16).astype(F32)
    return high, v - high


def spread_halves(here, by):
    high, _ = here
    both = jnp.concatenate(here, 0).astype(BF16)
    rolled = roll(both, by)
    rolled_high = rolled.astype(F32)[0:GROUP]
    return both, rolled, jnp.concatenate([high, rolled_high], 0).astype(BF16)


def put(x, t, v):
    for k, part in enumerate(spread_halves(halves(v), 127)):
        x[t, 80 * k:80 * k + 80] = part


def put_seam(xs, n, side, v):
    high, low = halves(v)
    both = jnp.concatenate([high, low], 0).astype(BF16)
    at = 0
    for pair in ((0, 127), (120, 119)):
        two = [roll(both, by) for by in pair]
        third = jnp.concatenate([x.astype(F32)[0:GROUP] for x in two], 0).astype(BF16)
        for part in two + [third]:
            xs[n, at:at + 80, 128 * side:128 * side + 128] = part
            at += 80


def prepare(at, tile, fac, fup, srep, load, push=True, elements=True):
    zeros = lambda n: jnp.zeros((n, 128), F32)
    s = tile[S:S + 12]
    srep[at, 36:40] = zeros(4)
    for c in (0, 12, 24):
        srep[at, c:c + 12] = s
    if elements:
        d = tile[D:D + 12]
        f = jnp.where(d > 0.0, EMIN + (1.0 - EMIN) * (d * d * d), 0.0)
        fac[at, 36:40] = zeros(4)
        fup[at, 36:40] = zeros(4)
        for c in (0, 12, 24):
            fac[at, c:c + 12] = f
            fup[at, c:c + 1] = zeros(1)
            fup[at, c + 1:c + 12] = f[0:11]
    if push:
        layer = lax.broadcasted_iota(jnp.int32, (12, 128), 0).astype(F32)
        load[at, 0:24] = zeros(24)
        load[at, 24:36] = jnp.where(tile[LOAD + 1:LOAD + 2] == layer, tile[LOAD:LOAD + 1], 0.0)
        load[at, 36:40] = zeros(4)


def weigh(f, above, below):
    return [
        above * f[(2 * k) * GROUP:(2 * k + 1) * GROUP] + below * f[(2 * k + 1) * GROUP:(2 * k + 2) * GROUP]
        for k in range(4)
    ]


def pairs_of(w, jobs):
    pending = []
    for at in range(0, len(jobs), 2):
        two = jobs[at:at + 2]
        wide = [operand() for _, operand, _ in two]
        f = jnp.dot(w[...], wide[0] if len(wide) == 1 else jnp.concatenate(wide, 1), preferred_element_type=F32)
        for t, part, post in pending:
            post(t, part)
        pending = [(t, f[:, 128 * k:128 * k + 128], post) for k, (t, _, post) in enumerate(two)]
    for t, part, post in pending:
        post(t, part)


def seam_planes(es, near, corner, edges, side, g):
    lane = lanes(FOLD)
    row = ((lane + 1) & 127) >> 3
    late = ((lane + 1) & 7) >= 4
    inner, outer = (row >= 3) & (row <= 10), (row < 3) | ((row > 10) & (row < 14))
    by = 24 - 64 * (g >> 1) - 4 * (g & 1)
    planes = slice(FOLD * g, FOLD * g + FOLD)

    def unfold(below, above, last):
        early = ((lanes(FOLD // 2) - 3 + 4 * last) & 63) < 32
        return jnp.concatenate(
            [roll(jnp.where(early, above, below), by + 64), roll(jnp.where(early, below, above), by + 32)], 0
        )

    here = jnp.where(outer, unfold(edges[0, side], edges[1, side], side), es[side, planes])
    beyond = unfold(corner[2 * side], corner[2 * side + 1], 1 - side)
    far = jnp.where(inner, roll(near[side], by), jnp.where(outer, beyond, 0.0))
    return jnp.where(late, here, far) if side == 0 else jnp.where(late, far, here)


class Tiles:
    def __init__(self, own, ref, more):
        self.own, self.ref, self.more = own, ref, more

    def __getitem__(self, t):
        return self.ref[t] if t in self.own else self.more[t]

    def __setitem__(self, t, v):
        self.more[t] = v


class Fresh:
    def __init__(self, own, ref):
        self.own, self.ref = own, ref

    def __getitem__(self, t):
        return self.ref[t] if t in self.own else None


class Field:
    def __init__(self, tile, at):
        self.tile, self.at = tile, at

    def __getitem__(self, t):
        return self.tile(t, self.at)


class Maps:
    def __init__(self, w, fac, fup, srep, load, acc):
        self.w, self.fac, self.fup, self.srep, self.load, self.acc = w, fac, fup, srep, load, acc

    def collect(self, t, f, corners, so_far):
        for dz in (0, 1):
            total = None if so_far is None else so_far[dz][t]
            for k in range(4):
                term = f[(2 * k + dz) * GROUP:(2 * k + dz + 1) * GROUP] * corners[k]
                total = term if total is None else total + term
            self.acc[dz][t] = total

    def seam_corners(self, v):
        return [roll(v, by) for by in (0, 127, 120, 119)]

    def seam(self, x, finish, state=None, so_far=None, forces=None):
        f = jnp.dot(self.w[...], x[...], preferred_element_type=F32)
        for side in (0, 1):
            t = LEFT + side
            part = f[:, 128 * side:128 * side + 128]
            if forces is not None:
                forces(t, part)
            if state is not None:
                v = state(t)
                self.collect(t, part, self.seam_corners(v), so_far)
            g = weigh(part, self.fac[t], self.fup[t])
            finish(t, g[0] + roll(g[1], 1) + roll(g[2], 8) + roll(g[3], 9))

    def main(self, x, elements, finish, state=None, so_far=None, pieces=None, keep=None, forces=None):
        carry = None
        first, last, ends = pieces if pieces is not None else (None, None, None)

        def node(t, above, below):
            finish(t, above[0] + below[0] + roll(above[1] + below[1], 1))

        def post(t, f):
            nonlocal carry
            if forces is not None:
                forces(t, f)
            if state is not None and t in OWN:
                now, rolled = state
                self.collect(t, f, [now[t], rolled[t], now[t + 1], rolled[t + 1]], so_far)
            g = weigh(f, self.fac[t], self.fup[t])
            if keep is not None and t == elements[0]:
                keep[0], keep[1] = g[0], g[1]
            if ends is not None and t == last + 1:
                node(t, g[0:2], (ends[2], ends[3]))
            elif carry is not None:
                node(t, g[0:2], carry)
            carry = g[2:]
            if ends is not None and t == first - 1:
                node(first, (ends[0], ends[1]), carry)
            if keep is not None and t == elements[-1]:
                keep[2], keep[3] = g[2], g[3]

        def operand(t):
            return lambda: jnp.concatenate([x[t], x[t + 1]], 0)

        return [(t, operand(t), post) for t in elements]

    def step_u(self, t, now, before, out):
        s = self.srep[t]
        return jnp.where(s > 0.0, 2.0 * now - before + s * (self.load[t] - out), 0.0)

    def step_a(self, t, now, before, out):
        return 2.0 * now - before + self.load[t] - out


def exchange_kernel(*refs):
    sources, refs = refs[:10], refs[10:]
    e, w, near, corner, edges, es, fac, fup, srep, load, u0r, u1, u1r, u2, a2, a1, acc0, acc1 = refs[:18]
    xu0, xz3, xu1, xz2, p1, p2, p3, p4, f3 = refs[18:27]
    held, (mine, corner_out, load_sem, send_sem, recv_sem) = refs[27:37], refs[37:]
    u, b, a, q, den, step, fix, top, depth, stiff = held
    gx, gy = lax.axis_index("gx"), lax.axis_index("gy")
    nx, ny = lax.axis_size("gx"), lax.axis_size("gy")
    down, up, left, right = gx > 0, gx < nx - 1, gy > 0, gy < ny - 1
    sides = {
        (-1, 0): down, (1, 0): up, (0, -1): left, (0, 1): right,
        (-1, -1): down & left, (1, -1): up & left, (-1, 1): down & right, (1, 1): up & right,
    }
    barrier = pltpu.get_barrier_semaphore()
    for (dx, dy), there in reversed(sides.items()):
        @pl.when(there)
        def _(dx=dx, dy=dy):
            pl.semaphore_signal(barrier, inc=1, device_id=(gx + dx, gy + dy), device_id_type=MESH)

    loads = [pltpu.make_async_copy(src, dst, load_sem.at[k]) for k, (src, dst) in enumerate(zip(sources, held))]
    for c in loads:
        c.start()
    zeros = lambda n: jnp.zeros((n, 128), F32)
    for t, start in ((1, 96), (2, 176), (11, 176), (12, 88)):
        e[t, start:PLANES] = zeros(PLANES - start)

    @pl.when(jnp.logical_not(down))
    def _():
        for t in (1, 2):
            e[t] = zeros(PLANES)
        edges[0] = jnp.zeros((2, FOLD // 2, 128), F32)
        a2[1] = zeros(GROUP)

    @pl.when(jnp.logical_not(up))
    def _():
        for t in (11, 12):
            e[t] = zeros(PLANES)
        edges[1] = jnp.zeros((2, FOLD // 2, 128), F32)
        u1[12] = zeros(GROUP)
        a2[12] = zeros(GROUP)

    for k, dy in enumerate((-1, 1)):
        @pl.when(jnp.logical_not(sides[0, dy]))
        def _(k=k):
            near[k] = zeros(FOLD)

        for j, dx in enumerate((-1, 1)):
            @pl.when(jnp.logical_not(sides[dx, dy]))
            def _(k=k, j=j):
                corner[2 * k + j] = zeros(FOLD // 2)

    for c in loads:
        c.wait()
    for r in range(ROWS):
        t = r + 3
        free = 1.0 - fix[pl.ds(r, 12, stride=8), :].astype(F32)
        e[t, U:U + 36] = u[pl.ds(r, 36, stride=8), :]
        e[t, S:S + 12] = free * step[pl.ds(r, 12, stride=8), :]
        e[t, A:A + 36] = a[pl.ds(r, 36, stride=8), :]
        e[t, D:D + 11] = den[pl.ds(r, 11, stride=8), :]
        e[t, D + 11:D + 12] = zeros(1)
        e[t, B:B + 36] = b[pl.ds(r, 36, stride=8), :]
        e[t, LOAD:LOAD + 1] = top[r:r + 1, :]
        e[t, LOAD + 1:LOAD + 2] = depth[r:r + 1, :].astype(F32)
        e[t, LOAD + 2:LOAD + 4] = zeros(2)
        e[t, Q:Q + 36] = q[pl.ds(r, 36, stride=8), :]
        e[t, Q + 36:PLANES] = zeros(PLANES - Q - 36)

    lane = lanes(FOLD)
    first_cols, last_cols = zeros(FOLD), zeros(FOLD)
    for g in range(4):
        for r in range(ROWS):
            slot = 16 * (g >> 1) + 2 * r + (g & 1)
            v = roll(e[r + 3, FOLD * g:FOLD * g + FOLD], 4 * slot + 3)
            first_cols = jnp.where(((lane - 3) & 127) >> 2 == slot, v, first_cols)
            last_cols = jnp.where(((lane + 1) & 127) >> 2 == slot, v, last_cols)
    mine[0] = first_cols
    mine[1] = last_cols
    half = FOLD // 2
    lane = lanes(half)
    for k, cols in enumerate((first_cols, last_cols)):
        low = ((lane - 3 + 4 * k) & 63) < 32
        corner_out[k] = jnp.where(low, cols[0:half], roll(cols[half:FOLD], 32))
        corner_out[2 + k] = jnp.where(low, roll(cols[half:FOLD], 32), cols[0:half])

    banded_weights(stiff[...], w)
    maps = Maps(w, fac, fup, srep, load, (acc0, acc1))

    def own_tiles(some):
        for t in some:
            prepare(t, e.at[t], fac, fup, srep, load)
            now = e[t, U:U + GROUP]
            u0r[t] = roll(now, 127)
            put(xu0, t, now)
            put(xz3, t, srep[t] * e[t, A:A + GROUP])

    def value_a2(t, out):
        return maps.step_a(t, e[t, A:A + GROUP], e[t, Q:Q + GROUP], out)

    def main_u1(t, out):
        v = maps.step_u(t, e[t, U:U + GROUP], e[t, B:B + GROUP], out)
        u1[t] = v
        u1r[t] = roll(v, 127)
        put(xu1, t, v)

    def main_a2(t, out):
        v = value_a2(t, out)
        if t < 9:
            a2[t] = v
        put(xz2, t, srep[t] * v)

    def row_6(t, out):
        a2[t] = value_a2(t, out)

    def keep_forces(t, f):
        f3[t - 3] = f

    own_tiles((3, 4, 5, 8, 9, 10))
    u_jobs = maps.main(xu0, DEEP_1, main_u1, keep=p1)
    z_jobs = maps.main(xz3, DEEP_1, main_a2, keep=p3, forces=keep_forces)
    pairs_of(w, z_jobs[0:2] + maps.main(xz3, (8, 9), row_6) + u_jobs[0:2])

    pl.semaphore_wait(barrier, sum(there.astype(jnp.int32) for there in sides.values()))
    plan = [
        ((-1, -1), corner_out.at[0], corner.at[3]),
        ((1, -1), corner_out.at[2], corner.at[2]),
        ((-1, 1), corner_out.at[1], corner.at[1]),
        ((1, 1), corner_out.at[3], corner.at[0]),
        ((0, -1), mine.at[0], near.at[1]),
        ((0, 1), mine.at[1], near.at[0]),
        ((-1, 0), corner_out.at[0:2], edges.at[1]),
        ((-1, 0), e.at[3, 0:176], e.at[11, 0:176]),
        ((-1, 0), e.at[4, 0:88], e.at[12, 0:88]),
        ((-1, 0), a2.at[4], a2.at[12]),
        ((-1, 0), u1.at[4], u1.at[12]),
        ((1, 0), corner_out.at[2:4], edges.at[0]),
        ((1, 0), e.at[10, 0:176], e.at[2, 0:176]),
        ((1, 0), e.at[9, 0:96], e.at[1, 0:96]),
        ((1, 0), a2.at[9], a2.at[1]),
    ]
    copies = {}
    for k, ((dx, dy), src, dst) in enumerate(plan):
        copies.setdefault((dx, dy), []).append(pltpu.make_async_remote_copy(
            src_ref=src, dst_ref=dst, send_sem=send_sem.at[k], recv_sem=recv_sem.at[k],
            device_id=(gx + dx, gy + dy), device_id_type=MESH,
        ))
    for to, group in copies.items():
        @pl.when(sides[to])
        def _(group=group):
            for c in group:
                c.start()

    own_tiles((6, 7))

    def main_u2(t, out):
        u2[t] = maps.step_u(t, u1[t], e[t, U:U + GROUP], out)

    def main_a1(t, out):
        a1[t] = maps.step_a(t, a2[t], e[t, A:A + GROUP], out)

    pairs_of(w, u_jobs[2:] + z_jobs[2:])
    pairs_of(w, maps.main(xu1, DEEP_2, main_u2, keep=p2) + maps.main(xz2, DEEP_2, main_a1, (u1, u1r), None, keep=p4))
    lane = lanes(FOLD)
    inner = (((lane + 1) & 127) >> 3 >= 3) & (((lane + 1) & 127) >> 3 <= 10)
    late = ((lane + 1) & 7) >= 4
    for g in range(4):
        by = 24 - 64 * (g >> 1) - 4 * (g & 1)
        for side in (0, 1):
            es[side, FOLD * g:FOLD * g + FOLD] = jnp.where(inner & (late == (side == 0)), roll(mine[side], by), 0.0)

    for to, group in copies.items():
        @pl.when(sides[to])
        def _(group=group):
            for c in group:
                c.wait_send()

    for (dx, dy), group in copies.items():
        @pl.when(sides[-dx, -dy])
        def _(group=group):
            for c in group:
                c.wait_recv()


def plate_kernel(*refs):
    e, w, near, corner, edges, es, fac_in, fup_in, srep_in, load_in, u0r_in, u1_in, u1r_in, u2_in, a2_in, a1_in, acc0_in, acc1_in = refs[:18]
    xu0_in, xz3_in, xu1_in, xz2_in, p1, p2, p3, p4, f3 = refs[18:27]
    first_out, second_out, sens_out = refs[27:30]
    more, (f10, fseam, ends, ea, xs, first, second, sens, out_sem) = refs[30:48], refs[48:]
    fac, fup, srep, load, u0r = (Tiles(OWN, x, y) for x, y in zip((fac_in, fup_in, srep_in, load_in, u0r_in), more))
    u1, u1r, a2 = (
        Tiles(own, x, y) for own, x, y in zip(((*ONCE, 12), ONCE, (1, *ONCE, 12)), (u1_in, u1r_in, a2_in), more[5:])
    )
    u2, u2r, acc0, acc1, a1 = more[8:13]
    xu0, xz3 = (Tiles(OWN, x, y) for x, y in zip((xu0_in, xz3_in), more[13:]))
    xu1, xz2 = (Tiles(ONCE, x, y) for x, y in zip((xu1_in, xz2_in), more[15:]))
    xz1 = more[17]
    maps = Maps(w, fac, fup, srep, load, (acc0, acc1))
    so_far = Tiles(DEEP_2, acc0_in, acc0), Tiles(DEEP_2, acc1_in, acc1)
    fresh = Fresh(DEEP_2, acc0_in), Fresh(DEEP_2, acc1_in)
    lane = lanes(GROUP)
    from_left = ((lane + 1) & 7) >= 4
    edge = (lane == 0) | (lane == 127)
    outermost = (lane <= 1) | (lane >= 126)
    ghosts = (1, 2, 11, 12)
    seams = (LEFT, RIGHT)

    def tile(t, at):
        return ea[t - LEFT, at:at + GROUP] if t >= LEFT else e[t, at:at + GROUP]

    def both(k, ref):
        ends[k] = jnp.where(from_left, ref[LEFT], ref[RIGHT])

    def fixed(t, v, where, k):
        return jnp.where(where, roll(ends[k], 125 - 8 * t), v)

    def value_u1(t, out):
        v = maps.step_u(t, tile(t, U), tile(t, B), out)
        u1[t] = v
        return v

    def value_a2(t, out):
        v = maps.step_a(t, tile(t, A), tile(t, Q), out)
        a2[t] = v
        return v

    def main_u1(t, out):
        v = value_u1(t, out)
        if t in (3, 10, 11):
            u1r[t] = roll(v, 127)
        put(xu1.more, t, v)

    def main_a2(t, out):
        put(xz2.more, t, srep[t] * value_a2(t, out))

    def keep_forces(t, f):
        if t >= LEFT:
            fseam[t - LEFT] = f
        elif t == 10:
            f10[...] = f

    def seam_a1(t, out):
        v = maps.step_a(t, a2[t], tile(t, A), out)
        a1[t] = v
        put_seam(xs, 4, t - LEFT, srep[t] * v)

    def seam_u2(t, out):
        u2[t] = maps.step_u(t, u1[t], tile(t, U), out)

    def end_a1(t, v):
        v = fixed(t, v, outermost, 0)
        a1[t] = v
        put(xz1, t, srep[t] * v)
        if t in OWN:
            second[pl.ds(t - 3, 36, stride=8), :] = v[0:36]

    def end_u2(t, v):
        v = fixed(t, v, outermost, 1)
        u2[t] = v
        u2r[t] = roll(v, 127)

    a0 = {}

    def seam_a0(t, out):
        a0[t] = maps.step_a(t, a1[t], a2[t], out)

    def main_a0(t, out):
        v = fixed(t, maps.step_a(t, a1[t], a2[t], out), edge, 2)
        first[pl.ds(t - 3, 36, stride=8), :] = v[0:36]

    def ghost_tiles():
        for t in ghosts:
            prepare(t, e.at[t], *more[0:4], push=1 < t < 12, elements=t < 12)

    def ghost_z3():
        for t in ghosts:
            put(xz3.more, t, srep[t] * tile(t, A))
        for t in (1, 12):
            put(xz2.more, t, srep[t] * a2[t])

    def ghost_u0():
        u0r.more[11] = roll(tile(11, U), 127)
        for t in ghosts:
            put(xu0.more, t, tile(t, U))
        put(xu1.more, 12, u1[12])

    def seam_tiles():
        for g in (1, 0, 2):
            for side in (0, 1):
                ea[side, FOLD * g:FOLD * g + FOLD] = seam_planes(es, near, corner, edges, side, g)
        for side in (0, 1):
            prepare(LEFT + side, ea.at[side], *more[0:4])
            put_seam(xs, 2, side, srep[LEFT + side] * tile(LEFT + side, A))
        for side in (0, 1):
            put_seam(xs, 0, side, tile(LEFT + side, U))
            ea[side, FOLD * 3:FOLD * 4] = seam_planes(es, near, corner, edges, side, 3)

    def z3_rows():
        pairs_of(w, maps.main(xz3, (1, 2, 10, 11), main_a2, pieces=(3, 9, p3), forces=keep_forces))

    def u0_rows():
        pairs_of(w, maps.main(xu0, (1, 2, 10, 11), main_u1, pieces=(3, 9, p1)))

    def z3_seam():
        maps.seam(xs.at[2], lambda t, out: put_seam(xs, 3, t - LEFT, srep[t] * value_a2(t, out)), forces=keep_forces)

    def u0_seam():
        maps.seam(xs.at[0], lambda t, out: put_seam(xs, 1, t - LEFT, value_u1(t, out)))

    def z2_seam():
        maps.seam(xs.at[3], seam_a1, lambda t: u1[t], None)
        both(0, a1)

    def u1_seam():
        maps.seam(xs.at[1], seam_u2)
        both(1, u2)

    def z2_rows():
        for t in TWICE:
            end_a1(t, a1_in[t])
        pairs_of(w, maps.main(
            xz2, (1, 2, 3, 9, 10, 11), lambda t, out: end_a1(t, maps.step_a(t, a2[t], tile(t, A), out)),
            (u1, u1r), fresh, pieces=(4, 8, p4),
        ))

    def u1_rows():
        for t in TWICE:
            end_u2(t, u2_in[t])
        pairs_of(w, maps.main(xu1, (2, 3, 9, 10, 11), lambda t, out: end_u2(t, maps.step_u(t, u1[t], tile(t, U), out)), pieces=(4, 8, p2)))

    def z1_seam():
        maps.seam(xs.at[4], seam_a0, lambda t: tile(t, U), (acc0, acc1))
        both(2, a0)

    def z1_rows():
        pairs_of(w, maps.main(xz1, range(2, 11), main_a0, (Field(tile, U), u0r), so_far))

    def seam_sums():
        for t in seams:
            maps.collect(t, fseam[t - LEFT], maps.seam_corners(u2[t]), (acc0, acc1))

    def row_sums():
        for t in OWN:
            maps.collect(t, f3[t - 3] if t < 10 else f10[...], [u2[t], u2r[t], u2[t + 1], u2r[t + 1]], (acc0, acc1))

    for block in (
        seam_tiles, ghost_tiles, ghost_z3, ghost_u0, z3_rows, z3_seam, u0_seam, u0_rows, z2_seam, z2_rows, u1_seam, z1_seam, u1_rows, seam_sums, z1_rows, row_sums,
    ):
        block()
    copies = [pltpu.make_async_copy(src, dst, out_sem.at[k]) for k, (src, dst) in enumerate(
        ((first, first_out), (second, second_out), (sens, sens_out)))]
    copies[0].start()
    copies[1].start()

    def total(t):
        return sum(acc0[t, c:c + 11] + acc1[t, c + 1:c + 12] for c in (0, 12, 24))

    lane = lanes(11)
    seam = jnp.where(((lane + 1) & 7) >= 4, total(LEFT), total(RIGHT))
    outer = (lane == 0) | (lane >= 126)
    for r in range(ROWS):
        t = r + 3
        d = e[t, D:D + 11]
        sens[pl.ds(r, 11, stride=8), :] = (-3.0 * (1.0 - EMIN)) * (d * d) * jnp.where(outer, roll(seam, 125 - 8 * t), total(t))
    copies[2].start()
    for c in copies:
        c.wait()


def local(u_now, u_prev, adjoint_next, adjoint_later, density, step_factor, fixed_nodes, load_top, load_depth, brick_stiffness):
    vmem = pl.BlockSpec(memory_space=pltpu.VMEM)
    hbm = pl.BlockSpec(memory_space=pltpu.HBM)
    flat = lambda x: x.reshape(-1, 128)
    sources = (
        flat(u_now), flat(u_prev), flat(adjoint_next), flat(adjoint_later), flat(density), flat(step_factor),
        flat(fixed_nodes), load_top, load_depth, brick_stiffness,
    )
    f32 = lambda *shape: jax.ShapeDtypeStruct(shape + (128,), F32)
    bf16 = lambda *shape: jax.ShapeDtypeStruct(shape, BF16)
    passed = (
        [f32(MAIN, PLANES), bf16(OUT, DEPTH), f32(2, FOLD), f32(4, FOLD // 2), f32(2, 2, FOLD // 2), f32(2, PLANES)]
        + [f32(TILES, GROUP)] * 12 + [bf16(MAIN, WIDE, 128)] * 4 + [f32(4, GROUP)] * 4 + [f32(7, OUT)]
    )
    gathered = pl.pallas_call(
        exchange_kernel,
        out_shape=passed,
        in_specs=[hbm] * 10,
        out_specs=[vmem] * len(passed),
        scratch_shapes=[pltpu.VMEM(x.shape, x.dtype) for x in sources] + [
            pltpu.VMEM((2, FOLD, 128), F32),
            pltpu.VMEM((4, FOLD // 2, 128), F32),
            pltpu.SemaphoreType.DMA((10,)),
            pltpu.SemaphoreType.DMA((15,)),
            pltpu.SemaphoreType.DMA((15,)),
        ],
        compiler_params=pltpu.CompilerParams(collective_id=0, has_side_effects=True, vmem_limit_bytes=32 * 2**20),
        name="exchange",
    )(*(pltpu.with_memory_space_constraint(x, pltpu.HBM) for x in sources))
    tiles = lambda n, rows, kind: pltpu.VMEM((n, rows, 128), kind)
    results = ((36 * ROWS, 128), (36 * ROWS, 128), (11 * ROWS, 128))
    first, second, sens = pl.pallas_call(
        plate_kernel,
        out_shape=tuple(jax.ShapeDtypeStruct(shape, F32) for shape in results),
        in_specs=[vmem] * len(passed),
        out_specs=(hbm,) * 3,
        scratch_shapes=[tiles(TILES, GROUP, F32)] * 13 + [tiles(MAIN, WIDE, BF16)] * 5
        + [pltpu.VMEM((OUT, 128), F32), tiles(2, OUT, F32), tiles(3, GROUP, F32), tiles(2, PLANES, F32), pltpu.VMEM((5, DEPTH, 256), BF16)]
        + [pltpu.VMEM(shape, F32) for shape in results]
        + [pltpu.SemaphoreType.DMA((3,))],
        compiler_params=pltpu.CompilerParams(vmem_limit_bytes=40 * 2**20),
        name="plate",
    )(*gathered)
    return (
        first.reshape(u_now.shape),
        second.reshape(u_now.shape),
        sens.reshape(density.shape),
    )


def solution(mesh):
    in_specs = (
        P(None, None, "gx", "gy"),
        P(None, None, "gx", "gy"),
        P(None, None, "gx", "gy"),
        P(None, None, "gx", "gy"),
        P(None, "gx", "gy"),
        P(None, "gx", "gy"),
        P(None, "gx", "gy"),
        P("gx", "gy"),
        P("gx", "gy"),
        P(),
    )
    out_specs = (P(None, None, "gx", "gy"), P(None, None, "gx", "gy"), P(None, "gx", "gy"))
    return jax.shard_map(local, mesh=mesh, in_specs=in_specs, out_specs=out_specs, check_vma=False)
```

```python
import jax
import jax.numpy as jnp
from jax import lax
from jax.experimental import pallas as pl
from jax.experimental.pallas import tpu as pltpu
from jax.sharding import PartitionSpec as P

EMIN = 0.001
MESH = pl.DeviceIdType.MESH
F32 = jnp.float32
BF16 = jnp.bfloat16

ROWS = 8
OWN = range(3, 11)
DEEP_1, DEEP_2 = range(3, 10), range(4, 9)
ONCE, TWICE = range(4, 10), range(5, 9)
MAIN = 14
LEFT, RIGHT = 14, 15
TILES = 16
U, S, A, D, B, LOAD, Q, PLANES = 0, 36, 48, 84, 96, 132, 136, 192
FOLD = 48
GROUP = 40
OUT = 8 * GROUP
WIDE = 6 * GROUP
DEPTH = 2 * WIDE


def banded_weights(stiff, w):
    def split(place):
        comp = (place >= 12).astype(jnp.int32) + (place >= 24).astype(jnp.int32)
        return comp, place - 12 * comp

    iota = lambda shape, d: lax.broadcasted_iota(jnp.int32, shape, d)
    group, r = iota((8, GROUP, 24), 0), iota((8, GROUP, 24), 1)
    dz = group & 1
    comp, layer = split(r)
    element = layer - dz
    real = (r < 36) & (element >= 0) & (element <= 10)
    pick = jnp.where(real & (iota((8, GROUP, 24), 2) == comp * 8 + 4 * dz + (group >> 1)), 1.0, 0.0)
    pick = pick.reshape(OUT, 24).astype(BF16)

    def columns(shape):
        q = iota(shape, len(shape) - 1)
        block = sum((q >= GROUP * k).astype(jnp.int32) for k in range(1, 12))
        s = q - GROUP * block
        dx = (block >= 6).astype(jnp.int32)
        block = block - 6 * dx
        dy = ((block == 2) | (block == 3) | (block == 5)).astype(jnp.int32)
        return (2 * dx + dy, block >= 4, s) + split(s)

    place, fine, s, comp, _ = columns((24, DEPTH))
    offset = columns((8, GROUP, DEPTH))[4] - split(iota((8, GROUP, DEPTH), 1))[1] + (iota((8, GROUP, DEPTH), 0) & 1)
    offset = offset.reshape(OUT, DEPTH)
    low = stiff - stiff.astype(BF16).astype(F32)
    full = jnp.zeros((OUT, DEPTH), F32)
    for part, value in enumerate((stiff.astype(BF16), low.astype(BF16))):
        rows = jnp.dot(pick, value, preferred_element_type=F32).astype(BF16)
        for up in (0, 1):
            here = (s < 36) & (iota((24, DEPTH), 0) == comp * 8 + 4 * up + place) & (fine == bool(part))
            spread = jnp.where(here, 1.0, 0.0).astype(BF16)
            full = full + jnp.where(offset == up, jnp.dot(rows, spread, preferred_element_type=F32), 0.0)
    w[...] = full.astype(BF16)


def roll(v, by):
    return pltpu.roll(v, by % 128, 1) if by % 128 else v


def lanes(rows):
    return lax.broadcasted_iota(jnp.int32, (rows, 128), 1)


def halves(v):
    high = v.astype(BF16).astype(F32)
    return high, v - high


def spread_halves(here, by):
    high, _ = here
    both = jnp.concatenate(here, 0).astype(BF16)
    rolled = roll(both, by)
    rolled_high = rolled.astype(F32)[0:GROUP]
    return both, rolled, jnp.concatenate([high, rolled_high], 0).astype(BF16)


def put(x, t, v):
    for k, part in enumerate(spread_halves(halves(v), 127)):
        x[t, 80 * k:80 * k + 80] = part


def put_seam(xs, n, side, v):
    high, low = halves(v)
    both = jnp.concatenate([high, low], 0).astype(BF16)
    at = 0
    for pair in ((0, 127), (120, 119)):
        two = [roll(both, by) for by in pair]
        third = jnp.concatenate([x.astype(F32)[0:GROUP] for x in two], 0).astype(BF16)
        for part in two + [third]:
            xs[n, at:at + 80, 128 * side:128 * side + 128] = part
            at += 80


def prepare(at, tile, fac, fup, srep, load, push=True, elements=True):
    zeros = lambda n: jnp.zeros((n, 128), F32)
    s = tile[S:S + 12]
    srep[at, 36:40] = zeros(4)
    for c in (0, 12, 24):
        srep[at, c:c + 12] = s
    if elements:
        d = tile[D:D + 12]
        f = jnp.where(d > 0.0, EMIN + (1.0 - EMIN) * (d * d * d), 0.0)
        fac[at, 36:40] = zeros(4)
        fup[at, 36:40] = zeros(4)
        for c in (0, 12, 24):
            fac[at, c:c + 12] = f
            fup[at, c:c + 1] = zeros(1)
            fup[at, c + 1:c + 12] = f[0:11]
    if push:
        layer = lax.broadcasted_iota(jnp.int32, (12, 128), 0).astype(F32)
        load[at, 0:24] = zeros(24)
        load[at, 24:36] = jnp.where(tile[LOAD + 1:LOAD + 2] == layer, tile[LOAD:LOAD + 1], 0.0)
        load[at, 36:40] = zeros(4)


def weigh(f, above, below):
    return [
        above * f[(2 * k) * GROUP:(2 * k + 1) * GROUP] + below * f[(2 * k + 1) * GROUP:(2 * k + 2) * GROUP]
        for k in range(4)
    ]


def pairs_of(w, jobs):
    pending = []
    for at in range(0, len(jobs), 2):
        two = jobs[at:at + 2]
        wide = [operand() for _, operand, _ in two]
        f = jnp.dot(w[...], wide[0] if len(wide) == 1 else jnp.concatenate(wide, 1), preferred_element_type=F32)
        for t, part, post in pending:
            post(t, part)
        pending = [(t, f[:, 128 * k:128 * k + 128], post) for k, (t, _, post) in enumerate(two)]
    for t, part, post in pending:
        post(t, part)


def seam_planes(es, near, corner, edges, side, g):
    lane = lanes(FOLD)
    row = ((lane + 1) & 127) >> 3
    late = ((lane + 1) & 7) >= 4
    inner, outer = (row >= 3) & (row <= 10), (row < 3) | ((row > 10) & (row < 14))
    by = 24 - 64 * (g >> 1) - 4 * (g & 1)
    planes = slice(FOLD * g, FOLD * g + FOLD)

    def unfold(below, above, last):
        early = ((lanes(FOLD // 2) - 3 + 4 * last) & 63) < 32
        return jnp.concatenate(
            [roll(jnp.where(early, above, below), by + 64), roll(jnp.where(early, below, above), by + 32)], 0
        )

    here = jnp.where(outer, unfold(edges[0, side], edges[1, side], side), es[side, planes])
    beyond = unfold(corner[2 * side], corner[2 * side + 1], 1 - side)
    far = jnp.where(inner, roll(near[side], by), jnp.where(outer, beyond, 0.0))
    return jnp.where(late, here, far) if side == 0 else jnp.where(late, far, here)


class Tiles:
    def __init__(self, own, ref, more):
        self.own, self.ref, self.more = own, ref, more

    def __getitem__(self, t):
        return self.ref[t] if t in self.own else self.more[t]

    def __setitem__(self, t, v):
        self.more[t] = v


class Fresh:
    def __init__(self, own, ref):
        self.own, self.ref = own, ref

    def __getitem__(self, t):
        return self.ref[t] if t in self.own else None


class Field:
    def __init__(self, tile, at):
        self.tile, self.at = tile, at

    def __getitem__(self, t):
        return self.tile(t, self.at)


class Maps:
    def __init__(self, w, fac, fup, srep, load, acc):
        self.w, self.fac, self.fup, self.srep, self.load, self.acc = w, fac, fup, srep, load, acc

    def collect(self, t, f, corners, so_far):
        for dz in (0, 1):
            total = None if so_far is None else so_far[dz][t]
            for k in range(4):
                term = f[(2 * k + dz) * GROUP:(2 * k + dz + 1) * GROUP] * corners[k]
                total = term if total is None else total + term
            self.acc[dz][t] = total

    def seam_corners(self, v):
        return [roll(v, by) for by in (0, 127, 120, 119)]

    def seam(self, x, finish, state=None, so_far=None, forces=None):
        f = jnp.dot(self.w[...], x[...], preferred_element_type=F32)
        for side in (0, 1):
            t = LEFT + side
            part = f[:, 128 * side:128 * side + 128]
            if forces is not None:
                forces(t, part)
            if state is not None:
                v = state(t)
                self.collect(t, part, self.seam_corners(v), so_far)
            g = weigh(part, self.fac[t], self.fup[t])
            finish(t, g[0] + roll(g[1], 1) + roll(g[2], 8) + roll(g[3], 9))

    def main(self, x, elements, finish, state=None, so_far=None, pieces=None, keep=None, forces=None, beyond=None):
        carry = None
        first, last, ends = pieces if pieces is not None else (None, None, None)

        def node(t, above, below):
            finish(t, above[0] + below[0] + roll(above[1] + below[1], 1))

        def post(t, f):
            nonlocal carry
            if forces is not None:
                forces(t, f)
            if state is not None and t in OWN:
                now, rolled = state
                self.collect(t, f, [now[t], rolled[t], now[t + 1], rolled[t + 1]], so_far)
            g = weigh(f, self.fac[t], self.fup[t])
            if keep is not None and t == elements[0]:
                keep[0], keep[1] = g[0], g[1]
            if ends is not None and t == last + 1:
                node(t, g[0:2], (ends[2], ends[3]))
            elif carry is not None:
                node(t, g[0:2], carry)
            carry = g[2:]
            if ends is not None and t == first - 1:
                node(first, (ends[0], ends[1]), carry)
            if beyond is not None and t == first - 1:
                finish(t, g[0] + roll(g[1], 1) + beyond[0])
            if beyond is not None and t == last + 1:
                finish(t + 1, g[2] + roll(g[3], 1) + beyond[1])
            if keep is not None and t == elements[-1]:
                keep[2], keep[3] = g[2], g[3]

        def operand(t):
            return lambda: jnp.concatenate([x[t], x[t + 1]], 0)

        return [(t, operand(t), post) for t in elements]

    def step_u(self, t, now, before, out):
        s = self.srep[t]
        return jnp.where(s > 0.0, 2.0 * now - before + s * (self.load[t] - out), 0.0)

    def step_a(self, t, now, before, out):
        return 2.0 * now - before + self.load[t] - out


def exchange_kernel(*refs):
    sources, refs = refs[:10], refs[10:]
    e, w, near, corner, edges, zin, pin, es, fac, fup, srep, load, u0r, u1, u1r, u2, a2, a1, acc0, acc1 = refs[:20]
    xu0, xz3, xu1, xz2, p1, p2, p3, p4, f3 = refs[20:29]
    held, (mine, corner_out, zout, pout, ends_u, ends_z, load_sem, send_sem, recv_sem) = refs[29:39], refs[39:]
    u, b, a, q, den, step, fix, top, depth, stiff = held
    gx, gy = lax.axis_index("gx"), lax.axis_index("gy")
    nx, ny = lax.axis_size("gx"), lax.axis_size("gy")
    down, up, left, right = gx > 0, gx < nx - 1, gy > 0, gy < ny - 1
    sides = {
        (-1, 0): down, (1, 0): up, (0, -1): left, (0, 1): right,
        (-1, -1): down & left, (1, -1): up & left, (-1, 1): down & right, (1, 1): up & right,
    }
    barrier = pltpu.get_barrier_semaphore()
    for (dx, dy), there in reversed(sides.items()):
        @pl.when(there)
        def _(dx=dx, dy=dy):
            pl.semaphore_signal(barrier, inc=1, device_id=(gx + dx, gy + dy), device_id_type=MESH)

    loads = [pltpu.make_async_copy(src, dst, load_sem.at[k]) for k, (src, dst) in enumerate(zip(sources, held))]
    loads[-1].start()
    for c in loads[:-1]:
        c.start()
    zeros = lambda n: jnp.zeros((n, 128), F32)
    for t, start, stop in ((1, 0, 80), (1, 96, PLANES), (2, 176, PLANES), (11, 176, PLANES)):
        e[t, start:stop] = zeros(stop - start)

    @pl.when(jnp.logical_not(down))
    def _():
        for t in (1, 2):
            e[t] = zeros(PLANES)
        edges[0] = jnp.zeros((2, FOLD // 2, 128), F32)
        zin[0] = zeros(GROUP)
        pin[2], pin[3] = zeros(GROUP), zeros(GROUP)

    @pl.when(jnp.logical_not(up))
    def _():
        e[11] = zeros(PLANES)
        edges[1] = jnp.zeros((2, FOLD // 2, 128), F32)
        u1[12] = zeros(GROUP)
        zin[1] = zeros(GROUP)
        pin[0], pin[1] = zeros(GROUP), zeros(GROUP)

    for k, dy in enumerate((-1, 1)):
        @pl.when(jnp.logical_not(sides[0, dy]))
        def _(k=k):
            near[k] = zeros(FOLD)

        for j, dx in enumerate((-1, 1)):
            @pl.when(jnp.logical_not(sides[dx, dy]))
            def _(k=k, j=j):
                corner[2 * k + j] = zeros(FOLD // 2)

    loads[-1].wait()
    banded_weights(stiff[...], w)
    for c in loads[:-1]:
        c.wait()
    for r in range(ROWS):
        t = r + 3
        free = 1.0 - fix[pl.ds(r, 12, stride=8), :].astype(F32)
        e[t, U:U + 36] = u[pl.ds(r, 36, stride=8), :]
        e[t, S:S + 12] = free * step[pl.ds(r, 12, stride=8), :]
        e[t, A:A + 36] = a[pl.ds(r, 36, stride=8), :]
        e[t, D:D + 11] = den[pl.ds(r, 11, stride=8), :]
        e[t, D + 11:D + 12] = zeros(1)
        e[t, B:B + 36] = b[pl.ds(r, 36, stride=8), :]
        e[t, LOAD:LOAD + 1] = top[r:r + 1, :]
        e[t, LOAD + 1:LOAD + 2] = depth[r:r + 1, :].astype(F32)
        e[t, LOAD + 2:LOAD + 4] = zeros(2)
        e[t, Q:Q + 36] = q[pl.ds(r, 36, stride=8), :]
        e[t, Q + 36:PLANES] = zeros(PLANES - Q - 36)

    lane = lanes(FOLD)
    first_cols, last_cols = zeros(FOLD), zeros(FOLD)
    for g in range(4):
        for r in range(ROWS):
            slot = 16 * (g >> 1) + 2 * r + (g & 1)
            v = roll(e[r + 3, FOLD * g:FOLD * g + FOLD], 4 * slot + 3)
            first_cols = jnp.where(((lane - 3) & 127) >> 2 == slot, v, first_cols)
            last_cols = jnp.where(((lane + 1) & 127) >> 2 == slot, v, last_cols)
    mine[0] = first_cols
    mine[1] = last_cols
    half = FOLD // 2
    lane = lanes(half)
    for k, cols in enumerate((first_cols, last_cols)):
        low = ((lane - 3 + 4 * k) & 63) < 32
        corner_out[k] = jnp.where(low, cols[0:half], roll(cols[half:FOLD], 32))
        corner_out[2 + k] = jnp.where(low, roll(cols[half:FOLD], 32), cols[0:half])

    maps = Maps(w, fac, fup, srep, load, (acc0, acc1))

    def own_tiles(some):
        for t in some:
            prepare(t, e.at[t], fac, fup, srep, load)
            now = e[t, U:U + GROUP]
            u0r[t] = roll(now, 127)
            put(xu0, t, now)
            put(xz3, t, srep[t] * e[t, A:A + GROUP])

    def value_a2(t, out):
        return maps.step_a(t, e[t, A:A + GROUP], e[t, Q:Q + GROUP], out)

    def main_u1(t, out):
        v = maps.step_u(t, e[t, U:U + GROUP], e[t, B:B + GROUP], out)
        u1[t] = v
        u1r[t] = roll(v, 127)
        put(xu1, t, v)

    def main_a2(t, out):
        v = value_a2(t, out)
        a2[t] = v
        v = srep[t] * v
        if t == 4:
            zout[0] = v
        put(xz2, t, v)

    def row_6(t, out):
        zout[1] = srep[t] * value_a2(t, out)

    def keep_forces(t, f):
        f3[t - 3] = f

    own_tiles((3, 4, 5, 8, 9, 10))
    u_jobs = maps.main(xu0, DEEP_1, main_u1, keep=p1)
    z_jobs = maps.main(xz3, DEEP_1, main_a2, keep=p3, forces=keep_forces)
    pairs_of(w, z_jobs[0:2] + maps.main(xz3, (8, 9), row_6, keep=ends_z) + u_jobs[0:2] + maps.main(xu0, (9,), None, keep=ends_u))
    for k, (p, q) in enumerate(((p1, 0), (p3, 0), (ends_u, 2), (ends_z, 2))):
        pout[k] = p[q] + roll(p[q + 1], 1)

    pl.semaphore_wait(barrier, sum(there.astype(jnp.int32) for there in sides.values()))
    plan = [
        ((-1, -1), corner_out.at[0], corner.at[3]),
        ((1, -1), corner_out.at[2], corner.at[2]),
        ((-1, 1), corner_out.at[1], corner.at[1]),
        ((1, 1), corner_out.at[3], corner.at[0]),
        ((0, -1), mine.at[0], near.at[1]),
        ((0, 1), mine.at[1], near.at[0]),
        ((-1, 0), corner_out.at[0:2], edges.at[1]),
        ((-1, 0), e.at[3, 0:176], e.at[11, 0:176]),
        ((-1, 0), u1.at[4], u1.at[12]),
        ((-1, 0), zout.at[0], zin.at[1]),
        ((-1, 0), pout.at[0:2], pin.at[0:2]),
        ((1, 0), corner_out.at[2:4], edges.at[0]),
        ((1, 0), e.at[10, 0:176], e.at[2, 0:176]),
        ((1, 0), e.at[9, 80:96], e.at[1, 80:96]),
        ((1, 0), zout.at[1], zin.at[0]),
        ((1, 0), pout.at[2:4], pin.at[2:4]),
    ]
    copies = {}
    for k, ((dx, dy), src, dst) in enumerate(plan):
        copies.setdefault((dx, dy), []).append(pltpu.make_async_remote_copy(
            src_ref=src, dst_ref=dst, send_sem=send_sem.at[k], recv_sem=recv_sem.at[k],
            device_id=(gx + dx, gy + dy), device_id_type=MESH,
        ))
    for to, group in copies.items():
        @pl.when(sides[to])
        def _(group=group):
            for c in group:
                c.start()

    own_tiles((6, 7))

    def main_u2(t, out):
        u2[t] = maps.step_u(t, u1[t], e[t, U:U + GROUP], out)

    def main_a1(t, out):
        a1[t] = maps.step_a(t, a2[t], e[t, A:A + GROUP], out)

    pairs_of(w, u_jobs[2:] + z_jobs[2:])
    pairs_of(w, maps.main(xu1, DEEP_2, main_u2, keep=p2) + maps.main(xz2, DEEP_2, main_a1, (u1, u1r), None, keep=p4))
    lane = lanes(FOLD)
    inner = (((lane + 1) & 127) >> 3 >= 3) & (((lane + 1) & 127) >> 3 <= 10)
    late = ((lane + 1) & 7) >= 4
    for g in range(4):
        by = 24 - 64 * (g >> 1) - 4 * (g & 1)
        for side in (0, 1):
            es[side, FOLD * g:FOLD * g + FOLD] = jnp.where(inner & (late == (side == 0)), roll(mine[side], by), 0.0)

    for to, group in copies.items():
        @pl.when(sides[to])
        def _(group=group):
            for c in group:
                c.wait_send()

    for (dx, dy), group in copies.items():
        @pl.when(sides[-dx, -dy])
        def _(group=group):
            for c in group:
                c.wait_recv()


def plate_kernel(*refs):
    e, w, near, corner, edges, zin, pin, es, fac_in, fup_in, srep_in, load_in, u0r_in, u1_in, u1r_in, u2_in, a2_in, a1_in, acc0_in, acc1_in = refs[:20]
    xu0_in, xz3_in, xu1_in, xz2_in, p1, p2, p3, p4, f3 = refs[20:29]
    first_out, second_out, sens_out = refs[29:32]
    more, (f10, fseam, ends, ea, xs, first, second, sens, out_sem) = refs[32:50], refs[50:]
    fac, fup, srep, load, u0r = (Tiles(OWN, x, y) for x, y in zip((fac_in, fup_in, srep_in, load_in, u0r_in), more))
    u1, u1r, a2 = (
        Tiles(own, x, y) for own, x, y in zip(((*ONCE, 12), ONCE, ONCE), (u1_in, u1r_in, a2_in), more[5:])
    )
    u2, u2r, acc0, acc1, a1 = more[8:13]
    xu0, xz3 = (Tiles(OWN, x, y) for x, y in zip((xu0_in, xz3_in), more[13:]))
    xu1, xz2 = (Tiles(ONCE, x, y) for x, y in zip((xu1_in, xz2_in), more[15:]))
    xz1 = more[17]
    maps = Maps(w, fac, fup, srep, load, (acc0, acc1))
    so_far = Tiles(DEEP_2, acc0_in, acc0), Tiles(DEEP_2, acc1_in, acc1)
    fresh = Fresh(DEEP_2, acc0_in), Fresh(DEEP_2, acc1_in)
    lane = lanes(GROUP)
    from_left = ((lane + 1) & 7) >= 4
    edge = (lane == 0) | (lane == 127)
    outermost = (lane <= 1) | (lane >= 126)
    ghosts = (2, 11)
    seams = (LEFT, RIGHT)

    def tile(t, at):
        return ea[t - LEFT, at:at + GROUP] if t >= LEFT else e[t, at:at + GROUP]

    def both(k, ref):
        ends[k] = jnp.where(from_left, ref[LEFT], ref[RIGHT])

    def fixed(t, v, where, k):
        return jnp.where(where, roll(ends[k], 125 - 8 * t), v)

    def value_u1(t, out):
        v = maps.step_u(t, tile(t, U), tile(t, B), out)
        u1[t] = v
        return v

    def value_a2(t, out):
        v = maps.step_a(t, tile(t, A), tile(t, Q), out)
        a2[t] = v
        return v

    def main_u1(t, out):
        v = value_u1(t, out)
        if t in (3, 10, 11):
            u1r[t] = roll(v, 127)
        put(xu1.more, t, v)

    def main_a2(t, out):
        put(xz2.more, t, srep[t] * value_a2(t, out))

    def keep_forces(t, f):
        if t >= LEFT:
            fseam[t - LEFT] = f
        elif t == 10:
            f10[...] = f

    def seam_a1(t, out):
        v = maps.step_a(t, a2[t], tile(t, A), out)
        a1[t] = v
        put_seam(xs, 4, t - LEFT, srep[t] * v)

    def seam_u2(t, out):
        u2[t] = maps.step_u(t, u1[t], tile(t, U), out)

    def end_a1(t, v):
        v = fixed(t, v, outermost, 0)
        a1[t] = v
        put(xz1, t, srep[t] * v)
        if t in OWN:
            second[pl.ds(t - 3, 36, stride=8), :] = v[0:36]

    def end_u2(t, v):
        v = fixed(t, v, outermost, 1)
        u2[t] = v
        u2r[t] = roll(v, 127)

    a0 = {}

    def seam_a0(t, out):
        a0[t] = maps.step_a(t, a1[t], a2[t], out)

    def main_a0(t, out):
        v = fixed(t, maps.step_a(t, a1[t], a2[t], out), edge, 2)
        first[pl.ds(t - 3, 36, stride=8), :] = v[0:36]

    def ghost_tiles():
        for t in ghosts:
            prepare(t, e.at[t], *more[0:4])
        prepare(1, e.at[1], *more[0:4], push=False)

    def ghost_z3():
        for t in ghosts:
            put(xz3.more, t, srep[t] * tile(t, A))
        put(xz2.more, 1, zin[0])
        put(xz2.more, 12, zin[1])

    def ghost_u0():
        u0r.more[11] = roll(tile(11, U), 127)
        for t in ghosts:
            put(xu0.more, t, tile(t, U))
        put(xu1.more, 12, u1[12])

    def seam_tiles():
        for g in (1, 0, 2):
            for side in (0, 1):
                ea[side, FOLD * g:FOLD * g + FOLD] = seam_planes(es, near, corner, edges, side, g)
        for side in (0, 1):
            prepare(LEFT + side, ea.at[side], *more[0:4])
            put_seam(xs, 2, side, srep[LEFT + side] * tile(LEFT + side, A))
        for side in (0, 1):
            put_seam(xs, 0, side, tile(LEFT + side, U))
            ea[side, FOLD * 3:FOLD * 4] = seam_planes(es, near, corner, edges, side, 3)

    def z3_rows():
        pairs_of(w, maps.main(xz3, (2, 10), main_a2, pieces=(3, 9, p3), forces=keep_forces, beyond=(pin[3], pin[1])))

    def u0_rows():
        pairs_of(w, maps.main(xu0, (2, 10), main_u1, pieces=(3, 9, p1), beyond=(pin[2], pin[0])))

    def z3_seam():
        maps.seam(xs.at[2], lambda t, out: put_seam(xs, 3, t - LEFT, srep[t] * value_a2(t, out)), forces=keep_forces)

    def u0_seam():
        maps.seam(xs.at[0], lambda t, out: put_seam(xs, 1, t - LEFT, value_u1(t, out)))

    def z2_seam():
        maps.seam(xs.at[3], seam_a1, lambda t: u1[t], None)
        both(0, a1)

    def u1_seam():
        maps.seam(xs.at[1], seam_u2)
        both(1, u2)

    def z2_rows():
        for t in TWICE:
            end_a1(t, a1_in[t])
        pairs_of(w, maps.main(
            xz2, (1, 2, 3, 9, 10, 11), lambda t, out: end_a1(t, maps.step_a(t, a2[t], tile(t, A), out)),
            (u1, u1r), fresh, pieces=(4, 8, p4),
        ))

    def u1_rows():
        for t in TWICE:
            end_u2(t, u2_in[t])
        pairs_of(w, maps.main(xu1, (2, 3, 9, 10, 11), lambda t, out: end_u2(t, maps.step_u(t, u1[t], tile(t, U), out)), pieces=(4, 8, p2)))

    def z1_seam():
        maps.seam(xs.at[4], seam_a0, lambda t: tile(t, U), (acc0, acc1))
        both(2, a0)

    def z1_rows():
        pairs_of(w, maps.main(xz1, range(2, 11), main_a0, (Field(tile, U), u0r), so_far))

    def seam_sums():
        for t in seams:
            maps.collect(t, fseam[t - LEFT], maps.seam_corners(u2[t]), (acc0, acc1))

    def row_sums():
        for t in OWN:
            maps.collect(t, f3[t - 3] if t < 10 else f10[...], [u2[t], u2r[t], u2[t + 1], u2r[t + 1]], (acc0, acc1))

    for block in (
        seam_tiles, ghost_tiles, ghost_z3, z3_seam, ghost_u0, z3_rows, u0_seam, u0_rows,
        z2_seam, z2_rows, u1_seam, u1_rows, z1_seam, seam_sums, z1_rows, row_sums,
    ):
        block()
    copies = [pltpu.make_async_copy(src, dst, out_sem.at[k]) for k, (src, dst) in enumerate(
        ((first, first_out), (second, second_out), (sens, sens_out)))]
    copies[0].start()
    copies[1].start()

    def total(t):
        return sum(acc0[t, c:c + 11] + acc1[t, c + 1:c + 12] for c in (0, 12, 24))

    lane = lanes(11)
    seam = jnp.where(((lane + 1) & 7) >= 4, total(LEFT), total(RIGHT))
    outer = (lane == 0) | (lane >= 126)
    for r in range(ROWS):
        t = r + 3
        d = e[t, D:D + 11]
        sens[pl.ds(r, 11, stride=8), :] = (-3.0 * (1.0 - EMIN)) * (d * d) * jnp.where(outer, roll(seam, 125 - 8 * t), total(t))
    copies[2].start()
    for c in copies:
        c.wait()


def local(u_now, u_prev, adjoint_next, adjoint_later, density, step_factor, fixed_nodes, load_top, load_depth, brick_stiffness):
    vmem = pl.BlockSpec(memory_space=pltpu.VMEM)
    hbm = pl.BlockSpec(memory_space=pltpu.HBM)
    flat = lambda x: x.reshape(-1, 128)
    sources = (
        flat(u_now), flat(u_prev), flat(adjoint_next), flat(adjoint_later), flat(density), flat(step_factor),
        flat(fixed_nodes), load_top, load_depth, brick_stiffness,
    )
    f32 = lambda *shape: jax.ShapeDtypeStruct(shape + (128,), F32)
    bf16 = lambda *shape: jax.ShapeDtypeStruct(shape, BF16)
    passed = (
        [f32(MAIN, PLANES), bf16(OUT, DEPTH), f32(2, FOLD), f32(4, FOLD // 2), f32(2, 2, FOLD // 2), f32(2, GROUP), f32(4, GROUP), f32(2, PLANES)]
        + [f32(TILES, GROUP)] * 12 + [bf16(MAIN, WIDE, 128)] * 4 + [f32(4, GROUP)] * 4 + [f32(7, OUT)]
    )
    tiles = lambda n, rows, kind: pltpu.VMEM((n, rows, 128), kind)
    gathered = pl.pallas_call(
        exchange_kernel,
        out_shape=passed,
        in_specs=[hbm] * 10,
        out_specs=[vmem] * len(passed),
        scratch_shapes=[pltpu.VMEM(x.shape, x.dtype) for x in sources] + [
            pltpu.VMEM((2, FOLD, 128), F32),
            pltpu.VMEM((4, FOLD // 2, 128), F32),
            tiles(2, GROUP, F32),
            tiles(4, GROUP, F32),
            tiles(4, GROUP, F32),
            tiles(4, GROUP, F32),
            pltpu.SemaphoreType.DMA((10,)),
            pltpu.SemaphoreType.DMA((16,)),
            pltpu.SemaphoreType.DMA((16,)),
        ],
        compiler_params=pltpu.CompilerParams(collective_id=0, has_side_effects=True, vmem_limit_bytes=32 * 2**20),
        name="exchange",
    )(*(pltpu.with_memory_space_constraint(x, pltpu.HBM) for x in sources))
    results = ((36 * ROWS, 128), (36 * ROWS, 128), (11 * ROWS, 128))
    first, second, sens = pl.pallas_call(
        plate_kernel,
        out_shape=tuple(jax.ShapeDtypeStruct(shape, F32) for shape in results),
        in_specs=[vmem] * len(passed),
        out_specs=(hbm,) * 3,
        scratch_shapes=[tiles(TILES, GROUP, F32)] * 13 + [tiles(MAIN, WIDE, BF16)] * 5
        + [pltpu.VMEM((OUT, 128), F32), tiles(2, OUT, F32), tiles(3, GROUP, F32), tiles(2, PLANES, F32), pltpu.VMEM((5, DEPTH, 256), BF16)]
        + [pltpu.VMEM(shape, F32) for shape in results]
        + [pltpu.SemaphoreType.DMA((3,))],
        compiler_params=pltpu.CompilerParams(vmem_limit_bytes=40 * 2**20),
        name="plate",
    )(*gathered)
    return (
        first.reshape(u_now.shape),
        second.reshape(u_now.shape),
        sens.reshape(density.shape),
    )


def solution(mesh):
    in_specs = (
        P(None, None, "gx", "gy"),
        P(None, None, "gx", "gy"),
        P(None, None, "gx", "gy"),
        P(None, None, "gx", "gy"),
        P(None, "gx", "gy"),
        P(None, "gx", "gy"),
        P(None, "gx", "gy"),
        P("gx", "gy"),
        P("gx", "gy"),
        P(),
    )
    out_specs = (P(None, None, "gx", "gy"), P(None, None, "gx", "gy"), P(None, "gx", "gy"))
    return jax.shard_map(local, mesh=mesh, in_specs=in_specs, out_specs=out_specs, check_vma=False)
```

```python
import jax
import jax.numpy as jnp
from jax import lax
from jax.experimental import pallas as pl
from jax.experimental.pallas import tpu as pltpu
from jax.sharding import PartitionSpec as P

EMIN = 0.001
MESH = pl.DeviceIdType.MESH
F32 = jnp.float32
BF16 = jnp.bfloat16

ROWS = 8
OWN = range(3, 11)
DEEP_1, DEEP_2 = range(3, 10), range(4, 9)
ONCE, TWICE = range(4, 10), range(5, 9)
MAIN = 14
LEFT, RIGHT = 14, 15
TILES = 16
U, S, A, D, B, LOAD, Q, PLANES = 0, 36, 48, 84, 96, 132, 136, 192
FOLD = 48
GROUP = 40
OUT = 8 * GROUP
WIDE = 6 * GROUP
DEPTH = 2 * WIDE


def banded_weights(stiff, w):
    def split(place):
        comp = (place >= 12).astype(jnp.int32) + (place >= 24).astype(jnp.int32)
        return comp, place - 12 * comp

    iota = lambda shape, d: lax.broadcasted_iota(jnp.int32, shape, d)
    group, r = iota((8, GROUP, 24), 0), iota((8, GROUP, 24), 1)
    dz = group & 1
    comp, layer = split(r)
    element = layer - dz
    real = (r < 36) & (element >= 0) & (element <= 10)
    pick = jnp.where(real & (iota((8, GROUP, 24), 2) == comp * 8 + 4 * dz + (group >> 1)), 1.0, 0.0)
    pick = pick.reshape(OUT, 24).astype(BF16)

    def columns(shape):
        q = iota(shape, len(shape) - 1)
        block = sum((q >= GROUP * k).astype(jnp.int32) for k in range(1, 12))
        s = q - GROUP * block
        dx = (block >= 6).astype(jnp.int32)
        block = block - 6 * dx
        dy = ((block == 2) | (block == 3) | (block == 5)).astype(jnp.int32)
        return (2 * dx + dy, block >= 4, s) + split(s)

    place, fine, s, comp, _ = columns((24, DEPTH))
    offset = columns((8, GROUP, DEPTH))[4] - split(iota((8, GROUP, DEPTH), 1))[1] + (iota((8, GROUP, DEPTH), 0) & 1)
    offset = offset.reshape(OUT, DEPTH)
    low = stiff - stiff.astype(BF16).astype(F32)
    full = jnp.zeros((OUT, DEPTH), F32)
    for part, value in enumerate((stiff.astype(BF16), low.astype(BF16))):
        rows = jnp.dot(pick, value, preferred_element_type=F32).astype(BF16)
        for up in (0, 1):
            here = (s < 36) & (iota((24, DEPTH), 0) == comp * 8 + 4 * up + place) & (fine == bool(part))
            spread = jnp.where(here, 1.0, 0.0).astype(BF16)
            full = full + jnp.where(offset == up, jnp.dot(rows, spread, preferred_element_type=F32), 0.0)
    w[...] = full.astype(BF16)


def roll(v, by):
    return pltpu.roll(v, by % 128, 1) if by % 128 else v


def lanes(rows):
    return lax.broadcasted_iota(jnp.int32, (rows, 128), 1)


def halves(v):
    high = v.astype(BF16).astype(F32)
    return high, v - high


def spread_halves(here, by):
    high, _ = here
    both = jnp.concatenate(here, 0).astype(BF16)
    rolled = roll(both, by)
    rolled_high = rolled.astype(F32)[0:GROUP]
    return both, rolled, jnp.concatenate([high, rolled_high], 0).astype(BF16)


def put(x, t, v):
    for k, part in enumerate(spread_halves(halves(v), 127)):
        x[t, 80 * k:80 * k + 80] = part


def put_seam(xs, n, side, v):
    high, low = halves(v)
    both = jnp.concatenate([high, low], 0).astype(BF16)
    at = 0
    for pair in ((0, 127), (120, 119)):
        two = [roll(both, by) for by in pair]
        third = jnp.concatenate([x.astype(F32)[0:GROUP] for x in two], 0).astype(BF16)
        for part in two + [third]:
            xs[n, at:at + 80, 128 * side:128 * side + 128] = part
            at += 80


def prepare(at, tile, fac, fup, srep, load, push=True, elements=True):
    zeros = lambda n: jnp.zeros((n, 128), F32)
    s = tile[S:S + 12]
    srep[at, 36:40] = zeros(4)
    for c in (0, 12, 24):
        srep[at, c:c + 12] = s
    if elements:
        d = tile[D:D + 12]
        f = jnp.where(d > 0.0, EMIN + (1.0 - EMIN) * (d * d * d), 0.0)
        fac[at, 36:40] = zeros(4)
        fup[at, 36:40] = zeros(4)
        for c in (0, 12, 24):
            fac[at, c:c + 12] = f
            fup[at, c:c + 1] = zeros(1)
            fup[at, c + 1:c + 12] = f[0:11]
    if push:
        layer = lax.broadcasted_iota(jnp.int32, (12, 128), 0).astype(F32)
        load[at, 0:24] = zeros(24)
        load[at, 24:36] = jnp.where(tile[LOAD + 1:LOAD + 2] == layer, tile[LOAD:LOAD + 1], 0.0)
        load[at, 36:40] = zeros(4)


def weigh(f, above, below):
    return [
        above * f[(2 * k) * GROUP:(2 * k + 1) * GROUP] + below * f[(2 * k + 1) * GROUP:(2 * k + 2) * GROUP]
        for k in range(4)
    ]


def pairs_of(w, jobs):
    pending = []
    for at in range(0, len(jobs), 2):
        two = jobs[at:at + 2]
        wide = [operand() for _, operand, _ in two]
        f = jnp.dot(w[...], wide[0] if len(wide) == 1 else jnp.concatenate(wide, 1), preferred_element_type=F32)
        for t, part, post in pending:
            post(t, part)
        pending = [(t, f[:, 128 * k:128 * k + 128], post) for k, (t, _, post) in enumerate(two)]
    for t, part, post in pending:
        post(t, part)


def seam_planes(es, near, corner, edges, side, g):
    lane = lanes(FOLD)
    row = ((lane + 1) & 127) >> 3
    late = ((lane + 1) & 7) >= 4
    inner, outer = (row >= 3) & (row <= 10), (row < 3) | ((row > 10) & (row < 14))
    by = 24 - 64 * (g >> 1) - 4 * (g & 1)
    planes = slice(FOLD * g, FOLD * g + FOLD)

    def unfold(below, above, last):
        early = ((lanes(FOLD // 2) - 3 + 4 * last) & 63) < 32
        return jnp.concatenate(
            [roll(jnp.where(early, above, below), by + 64), roll(jnp.where(early, below, above), by + 32)], 0
        )

    here = jnp.where(outer, unfold(edges[0, side], edges[1, side], side), es[side, planes])
    beyond = unfold(corner[2 * side], corner[2 * side + 1], 1 - side)
    far = jnp.where(inner, roll(near[side], by), jnp.where(outer, beyond, 0.0))
    return jnp.where(late, here, far) if side == 0 else jnp.where(late, far, here)


class Tiles:
    def __init__(self, own, ref, more):
        self.own, self.ref, self.more = own, ref, more

    def __getitem__(self, t):
        return self.ref[t] if t in self.own else self.more[t]

    def __setitem__(self, t, v):
        self.more[t] = v


class Fresh:
    def __init__(self, own, ref):
        self.own, self.ref = own, ref

    def __getitem__(self, t):
        return self.ref[t] if t in self.own else None


class Field:
    def __init__(self, tile, at):
        self.tile, self.at = tile, at

    def __getitem__(self, t):
        return self.tile(t, self.at)


class Maps:
    def __init__(self, w, fac, fup, srep, load, acc):
        self.w, self.fac, self.fup, self.srep, self.load, self.acc = w, fac, fup, srep, load, acc

    def collect(self, t, f, corners, so_far):
        for dz in (0, 1):
            total = None if so_far is None else so_far[dz][t]
            for k in range(4):
                term = f[(2 * k + dz) * GROUP:(2 * k + dz + 1) * GROUP] * corners[k]
                total = term if total is None else total + term
            self.acc[dz][t] = total

    def seam_corners(self, v):
        return [roll(v, by) for by in (0, 127, 120, 119)]

    def seam(self, x, finish, state=None, so_far=None, forces=None):
        f = jnp.dot(self.w[...], x[...], preferred_element_type=F32)
        for side in (0, 1):
            t = LEFT + side
            part = f[:, 128 * side:128 * side + 128]
            if forces is not None:
                forces(t, part)
            if state is not None:
                v = state(t)
                self.collect(t, part, self.seam_corners(v), so_far)
            g = weigh(part, self.fac[t], self.fup[t])
            finish(t, g[0] + roll(g[1], 1) + roll(g[2], 8) + roll(g[3], 9))

    def main(self, x, elements, finish, state=None, so_far=None, pieces=None, keep=None, forces=None, beyond=None):
        carry = None
        first, last, ends = pieces if pieces is not None else (None, None, None)

        def node(t, above, below):
            finish(t, above[0] + below[0] + roll(above[1] + below[1], 1))

        def post(t, f):
            nonlocal carry
            if forces is not None:
                forces(t, f)
            if state is not None and t in OWN:
                now, rolled = state
                self.collect(t, f, [now[t], rolled[t], now[t + 1], rolled[t + 1]], so_far)
            g = weigh(f, self.fac[t], self.fup[t])
            if keep is not None and t == elements[0]:
                keep[0], keep[1] = g[0], g[1]
            if ends is not None and t == last + 1:
                node(t, g[0:2], (ends[2], ends[3]))
            elif carry is not None:
                node(t, g[0:2], carry)
            carry = g[2:]
            if ends is not None and t == first - 1:
                node(first, (ends[0], ends[1]), carry)
            if beyond is not None and t == first - 1:
                finish(t, g[0] + roll(g[1], 1) + beyond[0])
            if beyond is not None and t == last + 1:
                finish(t + 1, g[2] + roll(g[3], 1) + beyond[1])
            if keep is not None and t == elements[-1]:
                keep[2], keep[3] = g[2], g[3]

        def operand(t):
            return lambda: jnp.concatenate([x[t], x[t + 1]], 0)

        return [(t, operand(t), post) for t in elements]

    def step_u(self, t, now, before, out):
        s = self.srep[t]
        return jnp.where(s > 0.0, 2.0 * now - before + s * (self.load[t] - out), 0.0)

    def step_a(self, t, now, before, out):
        return 2.0 * now - before + self.load[t] - out


def exchange_kernel(*refs):
    sources, refs = refs[:10], refs[10:]
    e, w, near, corner, edges, zin, pin, es, fac, fup, srep, load, u0r, u1, u1r, u2, a2, a1, acc0, acc1 = refs[:20]
    xu0, xz3, xu1, xz2, p1, p2, p3, p4, f3 = refs[20:29]
    held, (mine, corner_out, zout, pout, ends_u, ends_z, load_sem, send_sem, recv_sem) = refs[29:39], refs[39:]
    u, b, a, q, den, step, fix, top, depth, stiff = held
    gx, gy = lax.axis_index("gx"), lax.axis_index("gy")
    nx, ny = lax.axis_size("gx"), lax.axis_size("gy")
    down, up, left, right = gx > 0, gx < nx - 1, gy > 0, gy < ny - 1
    sides = {
        (-1, 0): down, (1, 0): up, (0, -1): left, (0, 1): right,
        (-1, -1): down & left, (1, -1): up & left, (-1, 1): down & right, (1, 1): up & right,
    }
    barrier = pltpu.get_barrier_semaphore()
    for (dx, dy), there in reversed(sides.items()):
        @pl.when(there)
        def _(dx=dx, dy=dy):
            pl.semaphore_signal(barrier, inc=1, device_id=(gx + dx, gy + dy), device_id_type=MESH)

    loads = [
        pltpu.make_async_copy(src, dst.at[0:src.shape[0]], load_sem.at[k]) for k, (src, dst) in enumerate(zip(sources, held))
    ]
    loads[-1].start()
    for c in loads[:-1]:
        c.start()
    zeros = lambda n: jnp.zeros((n, 128), F32)
    for t, start, stop in ((1, 0, 80), (1, 96, PLANES), (2, 176, PLANES), (11, 176, PLANES)):
        e[t, start:stop] = zeros(stop - start)

    @pl.when(jnp.logical_not(down))
    def _():
        for t in (1, 2):
            e[t] = zeros(PLANES)
        edges[0] = jnp.zeros((2, FOLD // 2, 128), F32)
        zin[0] = zeros(GROUP)
        pin[2], pin[3] = zeros(GROUP), zeros(GROUP)

    @pl.when(jnp.logical_not(up))
    def _():
        e[11] = zeros(PLANES)
        edges[1] = jnp.zeros((2, FOLD // 2, 128), F32)
        u1[12] = zeros(GROUP)
        zin[1] = zeros(GROUP)
        pin[0], pin[1] = zeros(GROUP), zeros(GROUP)

    for k, dy in enumerate((-1, 1)):
        @pl.when(jnp.logical_not(sides[0, dy]))
        def _(k=k):
            near[k] = zeros(FOLD)

        for j, dx in enumerate((-1, 1)):
            @pl.when(jnp.logical_not(sides[dx, dy]))
            def _(k=k, j=j):
                corner[2 * k + j] = zeros(FOLD // 2)

    loads[-1].wait()
    banded_weights(stiff[...], w)
    for c in loads[:-1]:
        c.wait()
    for r in range(ROWS):
        t = r + 3
        free = 1.0 - fix[pl.ds(r, 12, stride=8), :].astype(F32)
        e[t, U:U + 36] = u[pl.ds(r, 36, stride=8), :]
        e[t, S:S + 12] = free * step[pl.ds(r, 12, stride=8), :]
        e[t, A:A + 36] = a[pl.ds(r, 36, stride=8), :]
        e[t, D:D + 11] = den[pl.ds(r, 11, stride=8), :]
        e[t, D + 11:D + 12] = zeros(1)
        e[t, B:B + 36] = b[pl.ds(r, 36, stride=8), :]
        e[t, LOAD:LOAD + 1] = top[r:r + 1, :]
        e[t, LOAD + 1:LOAD + 2] = depth[r:r + 1, :].astype(F32)
        e[t, LOAD + 2:LOAD + 4] = zeros(2)
        e[t, Q:Q + 36] = q[pl.ds(r, 36, stride=8), :]
        e[t, Q + 36:PLANES] = zeros(PLANES - Q - 36)

    lane = lanes(FOLD)
    first_cols, last_cols = zeros(FOLD), zeros(FOLD)
    for g in range(4):
        for r in range(ROWS):
            slot = 16 * (g >> 1) + 2 * r + (g & 1)
            v = roll(e[r + 3, FOLD * g:FOLD * g + FOLD], 4 * slot + 3)
            first_cols = jnp.where(((lane - 3) & 127) >> 2 == slot, v, first_cols)
            last_cols = jnp.where(((lane + 1) & 127) >> 2 == slot, v, last_cols)
    mine[0] = first_cols
    mine[1] = last_cols
    half = FOLD // 2
    lane = lanes(half)
    for k, cols in enumerate((first_cols, last_cols)):
        low = ((lane - 3 + 4 * k) & 63) < 32
        corner_out[k] = jnp.where(low, cols[0:half], roll(cols[half:FOLD], 32))
        corner_out[2 + k] = jnp.where(low, roll(cols[half:FOLD], 32), cols[0:half])

    maps = Maps(w, fac, fup, srep, load, (acc0, acc1))

    def own_tiles(some):
        for t in some:
            prepare(t, e.at[t], fac, fup, srep, load)
            now = e[t, U:U + GROUP]
            u0r[t] = roll(now, 127)
            put(xu0, t, now)
            put(xz3, t, srep[t] * e[t, A:A + GROUP])

    def value_a2(t, out):
        return maps.step_a(t, e[t, A:A + GROUP], e[t, Q:Q + GROUP], out)

    def main_u1(t, out):
        v = maps.step_u(t, e[t, U:U + GROUP], e[t, B:B + GROUP], out)
        u1[t] = v
        u1r[t] = roll(v, 127)
        put(xu1, t, v)

    def main_a2(t, out):
        v = value_a2(t, out)
        a2[t] = v
        v = srep[t] * v
        if t == 4:
            zout[0] = v
        put(xz2, t, v)

    def row_6(t, out):
        zout[1] = srep[t] * value_a2(t, out)

    def keep_forces(t, f):
        f3[t - 3] = f

    own_tiles((3, 4, 5, 8, 9, 10))
    u_jobs = maps.main(xu0, DEEP_1, main_u1, keep=p1)
    z_jobs = maps.main(xz3, DEEP_1, main_a2, keep=p3, forces=keep_forces)
    pairs_of(w, z_jobs[0:2] + maps.main(xz3, (8, 9), row_6, keep=ends_z) + u_jobs[0:2] + maps.main(xu0, (9,), None, keep=ends_u))
    for k, (p, q) in enumerate(((p1, 0), (p3, 0), (ends_u, 2), (ends_z, 2))):
        pout[k] = p[q] + roll(p[q + 1], 1)

    pl.semaphore_wait(barrier, sum(there.astype(jnp.int32) for there in sides.values()))
    plan = [
        ((-1, -1), corner_out.at[0], corner.at[3]),
        ((1, -1), corner_out.at[2], corner.at[2]),
        ((-1, 1), corner_out.at[1], corner.at[1]),
        ((1, 1), corner_out.at[3], corner.at[0]),
        ((0, -1), mine.at[0], near.at[1]),
        ((0, 1), mine.at[1], near.at[0]),
        ((-1, 0), corner_out.at[0:2], edges.at[1]),
        ((-1, 0), e.at[3, 0:176], e.at[11, 0:176]),
        ((-1, 0), u1.at[4], u1.at[12]),
        ((-1, 0), zout.at[0], zin.at[1]),
        ((-1, 0), pout.at[0:2], pin.at[0:2]),
        ((1, 0), corner_out.at[2:4], edges.at[0]),
        ((1, 0), e.at[10, 0:176], e.at[2, 0:176]),
        ((1, 0), e.at[9, 80:96], e.at[1, 80:96]),
        ((1, 0), zout.at[1], zin.at[0]),
        ((1, 0), pout.at[2:4], pin.at[2:4]),
    ]
    copies = {}
    for k, ((dx, dy), src, dst) in enumerate(plan):
        copies.setdefault((dx, dy), []).append(pltpu.make_async_remote_copy(
            src_ref=src, dst_ref=dst, send_sem=send_sem.at[k], recv_sem=recv_sem.at[k],
            device_id=(gx + dx, gy + dy), device_id_type=MESH,
        ))
    for to, group in copies.items():
        @pl.when(sides[to])
        def _(group=group):
            for c in group:
                c.start()

    own_tiles((6, 7))

    def main_u2(t, out):
        u2[t] = maps.step_u(t, u1[t], e[t, U:U + GROUP], out)

    def main_a1(t, out):
        a1[t] = maps.step_a(t, a2[t], e[t, A:A + GROUP], out)

    pairs_of(w, u_jobs[2:] + z_jobs[2:])
    pairs_of(w, maps.main(xu1, DEEP_2, main_u2, keep=p2) + maps.main(xz2, DEEP_2, main_a1, (u1, u1r), None, keep=p4))
    lane = lanes(FOLD)
    inner = (((lane + 1) & 127) >> 3 >= 3) & (((lane + 1) & 127) >> 3 <= 10)
    late = ((lane + 1) & 7) >= 4
    for g in range(4):
        by = 24 - 64 * (g >> 1) - 4 * (g & 1)
        for side in (0, 1):
            es[side, FOLD * g:FOLD * g + FOLD] = jnp.where(inner & (late == (side == 0)), roll(mine[side], by), 0.0)

    for to, group in copies.items():
        @pl.when(sides[to])
        def _(group=group):
            for c in group:
                c.wait_send()

    for (dx, dy), group in copies.items():
        @pl.when(sides[-dx, -dy])
        def _(group=group):
            for c in group:
                c.wait_recv()


def plate_kernel(*refs):
    e, w, near, corner, edges, zin, pin, es, fac_in, fup_in, srep_in, load_in, u0r_in, u1_in, u1r_in, u2_in, a2_in, a1_in, acc0_in, acc1_in = refs[:20]
    xu0_in, xz3_in, xu1_in, xz2_in, p1, p2, p3, p4, f3 = refs[20:29]
    first_out, second_out, sens_out = refs[29:32]
    more, (f10, fseam, ends, ea, xs, first, second, sens, out_sem) = refs[32:50], refs[50:]
    fac, fup, srep, load, u0r = (Tiles(OWN, x, y) for x, y in zip((fac_in, fup_in, srep_in, load_in, u0r_in), more))
    u1, u1r, a2 = (
        Tiles(own, x, y) for own, x, y in zip(((*ONCE, 12), ONCE, ONCE), (u1_in, u1r_in, a2_in), more[5:])
    )
    u2, u2r, acc0, acc1, a1 = more[8:13]
    xu0, xz3 = (Tiles(OWN, x, y) for x, y in zip((xu0_in, xz3_in), more[13:]))
    xu1, xz2 = (Tiles(ONCE, x, y) for x, y in zip((xu1_in, xz2_in), more[15:]))
    xz1 = more[17]
    maps = Maps(w, fac, fup, srep, load, (acc0, acc1))
    so_far = Tiles(DEEP_2, acc0_in, acc0), Tiles(DEEP_2, acc1_in, acc1)
    fresh = Fresh(DEEP_2, acc0_in), Fresh(DEEP_2, acc1_in)
    lane = lanes(GROUP)
    from_left = ((lane + 1) & 7) >= 4
    edge = (lane == 0) | (lane == 127)
    outermost = (lane <= 1) | (lane >= 126)
    ghosts = (2, 11)
    seams = (LEFT, RIGHT)

    def tile(t, at):
        return ea[t - LEFT, at:at + GROUP] if t >= LEFT else e[t, at:at + GROUP]

    def both(k, ref):
        ends[k] = jnp.where(from_left, ref[LEFT], ref[RIGHT])

    def fixed(t, v, where, k):
        return jnp.where(where, roll(ends[k], 125 - 8 * t), v)

    def value_u1(t, out):
        v = maps.step_u(t, tile(t, U), tile(t, B), out)
        u1[t] = v
        return v

    def value_a2(t, out):
        v = maps.step_a(t, tile(t, A), tile(t, Q), out)
        a2[t] = v
        return v

    def main_u1(t, out):
        v = value_u1(t, out)
        if t in (3, 10, 11):
            u1r[t] = roll(v, 127)
        put(xu1.more, t, v)

    def main_a2(t, out):
        put(xz2.more, t, srep[t] * value_a2(t, out))

    def keep_forces(t, f):
        if t >= LEFT:
            fseam[t - LEFT] = f
        elif t == 10:
            f10[...] = f

    def seam_a1(t, out):
        v = maps.step_a(t, a2[t], tile(t, A), out)
        a1[t] = v
        put_seam(xs, 4, t - LEFT, srep[t] * v)

    def seam_u2(t, out):
        u2[t] = maps.step_u(t, u1[t], tile(t, U), out)

    def end_a1(t, v):
        v = fixed(t, v, outermost, 0)
        a1[t] = v
        put(xz1, t, srep[t] * v)
        if t in OWN:
            second[pl.ds(t - 3, 36, stride=8), :] = v[0:36]

    def end_u2(t, v):
        v = fixed(t, v, outermost, 1)
        u2[t] = v
        u2r[t] = roll(v, 127)

    a0 = {}

    def seam_a0(t, out):
        a0[t] = maps.step_a(t, a1[t], a2[t], out)

    def main_a0(t, out):
        v = fixed(t, maps.step_a(t, a1[t], a2[t], out), edge, 2)
        first[pl.ds(t - 3, 36, stride=8), :] = v[0:36]

    def ghost_tiles():
        for t in ghosts:
            prepare(t, e.at[t], *more[0:4])
        prepare(1, e.at[1], *more[0:4], push=False)

    def ghost_z3():
        for t in ghosts:
            put(xz3.more, t, srep[t] * tile(t, A))
        put(xz2.more, 1, zin[0])
        put(xz2.more, 12, zin[1])

    def ghost_u0():
        u0r.more[11] = roll(tile(11, U), 127)
        for t in ghosts:
            put(xu0.more, t, tile(t, U))
        put(xu1.more, 12, u1[12])

    def seam_tiles():
        for g in (1, 0, 2):
            for side in (0, 1):
                ea[side, FOLD * g:FOLD * g + FOLD] = seam_planes(es, near, corner, edges, side, g)
        for side in (0, 1):
            prepare(LEFT + side, ea.at[side], *more[0:4])
            put_seam(xs, 2, side, srep[LEFT + side] * tile(LEFT + side, A))
        for side in (0, 1):
            put_seam(xs, 0, side, tile(LEFT + side, U))
            ea[side, FOLD * 3:FOLD * 4] = seam_planes(es, near, corner, edges, side, 3)

    def z3_rows():
        pairs_of(w, maps.main(xz3, (2, 10), main_a2, pieces=(3, 9, p3), forces=keep_forces, beyond=(pin[3], pin[1])))

    def u0_rows():
        pairs_of(w, maps.main(xu0, (2, 10), main_u1, pieces=(3, 9, p1), beyond=(pin[2], pin[0])))

    def z3_seam():
        maps.seam(xs.at[2], lambda t, out: put_seam(xs, 3, t - LEFT, srep[t] * value_a2(t, out)), forces=keep_forces)

    def u0_seam():
        maps.seam(xs.at[0], lambda t, out: put_seam(xs, 1, t - LEFT, value_u1(t, out)))

    def z2_seam():
        maps.seam(xs.at[3], seam_a1, lambda t: u1[t], None)
        both(0, a1)

    def u1_seam():
        maps.seam(xs.at[1], seam_u2)
        both(1, u2)

    def z2_rows():
        for t in TWICE:
            end_a1(t, a1_in[t])
        pairs_of(w, maps.main(
            xz2, (1, 2, 3, 9, 10, 11), lambda t, out: end_a1(t, maps.step_a(t, a2[t], tile(t, A), out)),
            (u1, u1r), fresh, pieces=(4, 8, p4),
        ))

    def u1_rows():
        for t in TWICE:
            end_u2(t, u2_in[t])
        pairs_of(w, maps.main(xu1, (2, 3, 9, 10, 11), lambda t, out: end_u2(t, maps.step_u(t, u1[t], tile(t, U), out)), pieces=(4, 8, p2)))

    def z1_seam():
        maps.seam(xs.at[4], seam_a0, lambda t: tile(t, U), (acc0, acc1))
        both(2, a0)

    def z1_rows():
        pairs_of(w, maps.main(xz1, range(2, 11), main_a0, (Field(tile, U), u0r), so_far))

    def seam_sums():
        for t in seams:
            maps.collect(t, fseam[t - LEFT], maps.seam_corners(u2[t]), (acc0, acc1))

    def row_sums():
        for t in OWN:
            maps.collect(t, f3[t - 3] if t < 10 else f10[...], [u2[t], u2r[t], u2[t + 1], u2r[t + 1]], (acc0, acc1))

    for block in (
        seam_tiles, ghost_tiles, ghost_z3, z3_seam, ghost_u0, z3_rows, u0_seam, u0_rows,
        z2_seam, z2_rows, u1_seam, u1_rows, z1_seam, seam_sums, z1_rows, row_sums,
    ):
        block()
    copies = [pltpu.make_async_copy(src.at[0:dst.shape[0]], dst, out_sem.at[k]) for k, (src, dst) in enumerate(
        ((first, first_out), (second, second_out), (sens, sens_out)))]
    copies[0].start()
    copies[1].start()

    def total(t):
        return sum(acc0[t, c:c + 11] + acc1[t, c + 1:c + 12] for c in (0, 12, 24))

    lane = lanes(11)
    seam = jnp.where(((lane + 1) & 7) >= 4, total(LEFT), total(RIGHT))
    outer = (lane == 0) | (lane >= 126)
    for r in range(ROWS):
        t = r + 3
        d = e[t, D:D + 11]
        sens[pl.ds(r, 11, stride=8), :] = (-3.0 * (1.0 - EMIN)) * (d * d) * jnp.where(outer, roll(seam, 125 - 8 * t), total(t))
    copies[2].start()
    for c in copies:
        c.wait()


def roomy(shape):
    rows, cols = shape
    return (rows, cols) if cols != 128 else (-(-rows // 64) * 64 if rows > 8 else 16, cols)


def local(u_now, u_prev, adjoint_next, adjoint_later, density, step_factor, fixed_nodes, load_top, load_depth, brick_stiffness):
    vmem = pl.BlockSpec(memory_space=pltpu.VMEM)
    hbm = pl.BlockSpec(memory_space=pltpu.HBM)
    flat = lambda x: x.reshape(-1, 128)
    sources = (
        flat(u_now), flat(u_prev), flat(adjoint_next), flat(adjoint_later), flat(density), flat(step_factor),
        flat(fixed_nodes), load_top, load_depth, brick_stiffness,
    )
    f32 = lambda *shape: jax.ShapeDtypeStruct(shape + (128,), F32)
    bf16 = lambda *shape: jax.ShapeDtypeStruct(shape, BF16)
    passed = (
        [f32(MAIN, PLANES), bf16(OUT, DEPTH), f32(2, FOLD), f32(4, FOLD // 2), f32(2, 2, FOLD // 2), f32(2, GROUP), f32(4, GROUP), f32(2, PLANES)]
        + [f32(TILES + 1, GROUP)] * 12 + [bf16(MAIN, WIDE, 128)] * 4 + [f32(4, GROUP)] * 4 + [f32(7, OUT)]
    )
    tiles = lambda n, rows, kind: pltpu.VMEM((n, rows, 128), kind)
    gathered = pl.pallas_call(
        exchange_kernel,
        out_shape=passed,
        in_specs=[hbm] * 10,
        out_specs=[vmem] * len(passed),
        scratch_shapes=[pltpu.VMEM(roomy(x.shape), x.dtype) for x in sources] + [
            pltpu.VMEM((2, FOLD, 128), F32),
            pltpu.VMEM((4, FOLD // 2, 128), F32),
            tiles(2, GROUP, F32),
            tiles(4, GROUP, F32),
            tiles(4, GROUP, F32),
            tiles(4, GROUP, F32),
            pltpu.SemaphoreType.DMA((10,)),
            pltpu.SemaphoreType.DMA((16,)),
            pltpu.SemaphoreType.DMA((16,)),
        ],
        compiler_params=pltpu.CompilerParams(collective_id=0, has_side_effects=True, vmem_limit_bytes=32 * 2**20),
        name="exchange",
    )(*(pltpu.with_memory_space_constraint(x, pltpu.HBM) for x in sources))
    results = ((36 * ROWS, 128), (36 * ROWS, 128), (11 * ROWS, 128))
    first, second, sens = pl.pallas_call(
        plate_kernel,
        out_shape=tuple(jax.ShapeDtypeStruct(shape, F32) for shape in results),
        in_specs=[vmem] * len(passed),
        out_specs=(hbm,) * 3,
        scratch_shapes=[tiles(TILES + 1, GROUP, F32)] * 13 + [tiles(MAIN, WIDE, BF16)] * 5
        + [pltpu.VMEM((OUT, 128), F32), tiles(2, OUT, F32), tiles(3, GROUP, F32), tiles(2, PLANES, F32), pltpu.VMEM((5, DEPTH, 256), BF16)]
        + [pltpu.VMEM(roomy(shape), F32) for shape in results]
        + [pltpu.SemaphoreType.DMA((3,))],
        compiler_params=pltpu.CompilerParams(vmem_limit_bytes=40 * 2**20),
        name="plate",
    )(*gathered)
    return (
        first.reshape(u_now.shape),
        second.reshape(u_now.shape),
        sens.reshape(density.shape),
    )


def solution(mesh):
    in_specs = (
        P(None, None, "gx", "gy"),
        P(None, None, "gx", "gy"),
        P(None, None, "gx", "gy"),
        P(None, None, "gx", "gy"),
        P(None, "gx", "gy"),
        P(None, "gx", "gy"),
        P(None, "gx", "gy"),
        P("gx", "gy"),
        P("gx", "gy"),
        P(),
    )
    out_specs = (P(None, None, "gx", "gy"), P(None, None, "gx", "gy"), P(None, "gx", "gy"))
    return jax.shard_map(local, mesh=mesh, in_specs=in_specs, out_specs=out_specs, check_vma=False)
```
